32 devices in a mesh: section: 2 (over x), dp: 8 (over z, y), tensor: 2 (over core).
Axes of the slice: x: 2, y: 2, z: 4, core: 2. Of those that a mesh axis runs over, the one named last changes fastest.
Arguments:
- tokens: bfloat16 [8192, 768], P(('dp', 'tensor')), may hold values from -6 to 6
- segment_ids: int32 [32, 256], P('dp'), may hold values from 0 to 3, never falling along the last dimension, each value on 1 to 128 neighbouring positions
- out_cotangent: bfloat16 [8192, 768], P(('dp', 'tensor')), may hold values from -6 to 6
- w_qkv: bfloat16 [2, 768, 3, 768], P('section', None, None, 'tensor'), may hold values from -0.21875 to 0.21875
- qv_bias: bfloat16 [2, 2, 768], P('section', None, 'tensor'), may hold values from -3 to 3
- w_out: bfloat16 [2, 768, 768], P('section', 'tensor'), may hold values from -0.875 to 0.875
- w_up: bfloat16 [2, 768, 3072], P('section', None, 'tensor'), may hold values from -0.21875 to 0.21875
- up_bias: bfloat16 [2, 3072], P('section', 'tensor'), may hold values from -3 to 3
- w_down: bfloat16 [2, 3072, 768], P('section', 'tensor'), may hold values from -0.15625 to 0.15625
- add_bias: float32 [2, 2, 768], P('section'), may hold values from -3 to 3
- norm_gain: float32 [2, 2, 768], P('section'), may hold values from 0.5 to 1.5
- norm_bias: float32 [2, 2, 768], P('section'), may hold values from -3 to 3
Outputs:
- layer_outputs: bfloat16 [2, 8192, 768], P('section', ('dp', 'tensor'))
- input_grads: float32 [2, 8192, 768], P('section', ('dp', 'tensor'))
- grad_w_qkv: float32 [2, 768, 3, 768], P('section', None, None, 'tensor')
- grad_qv_bias: float32 [2, 2, 768], P('section', None, 'tensor')
- grad_w_out: float32 [2, 768, 768], P('section', 'tensor')
- grad_w_up: float32 [2, 768, 3072], P('section', None, 'tensor')
- grad_up_bias: float32 [2, 3072], P('section', 'tensor')
- grad_w_down: float32 [2, 3072, 768], P('section', 'tensor')
- grad_add_bias: float32 [2, 2, 768], P('section', None, 'tensor')
- grad_norm_gain: float32 [2, 2, 768], P('section', None, 'tensor')
- grad_norm_bias: float32 [2, 2, 768], P('section', None, 'tensor')
The draws below stay inside these ranges and needn't reach their ends.
Inputs may be any that keep to these rules, and one draw needn't show every extreme that they name: `segment_ids`: along each packed sequence the numbers never fall; each number covers 1 to 128 rows; rows attend only to rows with the same number in the same sequence.
All inputs are finite; a program needn't handle non-finite values.
Results may differ from the reference program's by a relative error of at most 0.02.
Values may be sent and summed in bfloat16 or wider, within the bound.
A program may use at most 192 MiB of HBM per device.

```python
import math
import jax
import jax.numpy as jnp
import numpy as np
from jax import lax

D = 768
HEADS = 12
HEAD_DIM = 64
FF = 3072
SEQ_LEN = 256
LAYERS = 2
SEQS = 32
TOKENS = 8192


def shard_levels(key, extent, shards, low, high):
    level, own = 1.0, jax.random.fold_in(key, 6)
    for position, shards_of in shards:
        steps = jnp.exp(jax.random.uniform(jax.random.fold_in(own, position), (shards_of,), jnp.float32, low / len(shards), high / len(shards)))
        level = level * jnp.repeat(steps, extent[position] // shards_of).reshape([-1 if axis == position else 1 for axis in range(len(extent))])
    return level


def profile(amount, total, reach, lean):
    loads = [(1 << 20) // math.isqrt(grade ** lean) + 1 for grade in range(2, amount + 1)]
    rest, holding = total - reach - (amount - 1), [1] * (amount - 1)
    while rest > 0:
        movable = [i for i in range(amount - 1) if holding[i] < reach]
        pool, remaining = sum([loads[i] for i in movable]), rest
        for i in movable:
            more = min(reach - holding[i], max(1, remaining * loads[i] // pool), rest)
            holding[i] = holding[i] + more
            rest = rest - more
    return np.array([reach] + holding)


def uneven(key, amount, total, limit, lean):
    if amount == 2:
        one = jax.random.randint(key, (), max(1, total - limit), min(limit, total - 1) + 1)
        return jnp.stack([one, total - one])
    tallies = jnp.asarray(profile(amount, total, limit, lean), jnp.int32)
    couples = (amount - 1) // 2
    source_of, taker = tallies[1:1 + 2 * couples:2], tallies[2:2 + 2 * couples:2]
    room = jnp.minimum(source_of - 1, limit - taker)
    shifted = jax.random.randint(jax.random.fold_in(key, 1), (couples,), 0, 1 << 20) % (room + 1)
    tallies = tallies.at[1:1 + 2 * couples:2].set(source_of - shifted).at[2:2 + 2 * couples:2].set(taker + shifted)
    return tallies[jax.random.permutation(jax.random.fold_in(key, 2), amount)]


def gaussian(stream_key, shape, deviation, reach, shards=(), kind=jnp.bfloat16):
    result = jax.random.normal(stream_key, shape, jnp.float32) * deviation
    if len(shards) > 0:
        result = shard_levels(stream_key, shape, shards, -0.22, 0.18) * result
    return jnp.clip(result, min=-reach, max=reach).astype(kind)


def setup_inputs(seed: int = 0) -> dict:
    key_of = jax.random.split(jax.random.key(seed), 13)
    return {
        "tokens": gaussian(key_of[0], (TOKENS, D), 1.0, 6.0, ((0, 16),)),
        "segment_ids": jax.vmap(lambda own: jnp.searchsorted(jnp.cumsum(uneven(own, 4, SEQ_LEN, SEQ_LEN // 2, 0)), jnp.arange(SEQ_LEN), side="right"))(jax.random.split(key_of[1], SEQS)).reshape((SEQS, SEQ_LEN)).astype(jnp.int32),
        "out_cotangent": gaussian(key_of[2], (TOKENS, D), 1.0, 6.0, ((0, 16),)),
        "w_qkv": gaussian(key_of[3], (LAYERS, D, 3, D), D ** -0.5, 0.21875, ((0, 2), (3, 2))),
        "qv_bias": gaussian(key_of[4], (LAYERS, 2, D), 0.5, 3.0, ((0, 2), (2, 2))),
        "w_out": gaussian(key_of[5], (LAYERS, D, D), (D // 16) ** -0.5, 0.875, ((0, 2), (1, 2))),
        "w_up": gaussian(key_of[6], (LAYERS, D, FF), D ** -0.5, 0.21875, ((0, 2), (2, 2))),
        "up_bias": gaussian(key_of[7], (LAYERS, FF), 0.5, 3.0, ((0, 2), (1, 2))),
        "w_down": gaussian(key_of[8], (LAYERS, FF, D), (FF // 2) ** -0.5, 0.15625, ((0, 2), (1, 2))),
        "add_bias": gaussian(key_of[9], (LAYERS, 2, D), 0.5, 3.0, ((0, 2),), jnp.float32),
        "norm_gain": jnp.clip(1.0 + 0.1 * jax.random.normal(key_of[10], (LAYERS, 2, D), jnp.float32), 0.5, 1.5),
        "norm_bias": gaussian(key_of[11], (LAYERS, 2, D), 0.5, 3.0, ((0, 2),), jnp.float32),
    }


@jax.custom_vjp
def low(v):
    return lax.optimization_barrier(v.astype(jnp.bfloat16)).astype(jnp.float32)

@jax.custom_vjp
def low_back(v):
    return v

def low_keep(v):
    return (low(v), None)

def low_pass(kept, grad):
    return (grad,)

def back_keep(v):
    return (v, None)

def back_low(kept, grad):
    return (low(grad),)
low.defvjp(low_keep, low_pass)
low_back.defvjp(back_keep, back_low)
norm_eps = 1e-12
masked_score = -1e+30

def matmul(left_side, right_side):
    return jnp.dot(left_side, right_side, precision=lax.Precision.HIGHEST, preferred_element_type=jnp.float32)

def layer_norm(residual, gain_row, shift_row):
    centered = residual - lax.optimization_barrier(jnp.mean(residual, axis=-1, keepdims=True))
    scaled = lax.rsqrt(lax.optimization_barrier(jnp.mean(centered * centered, axis=-1, keepdims=True)) + norm_eps)
    return centered * scaled * gain_row + shift_row

def attend_group(blocks):
    query_rows, key_rows, value_rows, seg_block = blocks
    scores = jnp.einsum('sqhe,skhe->shqk', query_rows, key_rows, precision=lax.Precision.HIGHEST) * HEAD_DIM ** (-0.5)
    scores = low_back(scores)
    same_pair = (seg_block[:, :, None] == seg_block[:, None, :])[:, None]
    scores = jnp.where(same_pair, scores, masked_score)
    weights = low(jax.nn.softmax(scores, axis=-1))
    return jnp.einsum('shqk,skhe->sqhe', weights, value_rows, precision=lax.Precision.HIGHEST)

def attention(query_rows, key_rows, value_rows, segment_ids):
    group_size = math.gcd(SEQS, max(1, 4096 // SEQ_LEN))
    block_count = SEQS // group_size

    def by_group(array):
        return array.reshape((block_count, group_size) + array.shape[1:])
    mixed_heads = lax.map(jax.checkpoint(attend_group), (by_group(query_rows), by_group(key_rows), by_group(value_rows), by_group(segment_ids)))
    return mixed_heads.reshape(query_rows.shape)

def layer(token_rows, segment_ids, w_qkv, qv_bias, w_out, w_up, up_bias, w_down, add_bias, norm_gain, norm_bias):
    projected = matmul(token_rows, w_qkv.reshape(D, 3 * D)).reshape(-1, 3, D)
    head_shape = (SEQS, SEQ_LEN, HEADS, HEAD_DIM)
    query_rows = low(low_back(projected[:, 0] + qv_bias[0])).reshape(head_shape)
    key_rows = low(low_back(projected[:, 1])).reshape(head_shape)
    value_rows = low(low_back(projected[:, 2] + qv_bias[1])).reshape(head_shape)
    mixed_heads = attention(query_rows, key_rows, value_rows, segment_ids).reshape(-1, D)
    mixed_heads = low(low_back(mixed_heads))
    residual = token_rows + low_back(matmul(mixed_heads, w_out)) + add_bias[0]
    hidden = layer_norm(residual, norm_gain[0], norm_bias[0])
    pre_active = low_back(matmul(low(hidden), w_up)) + up_bias
    active = low(jax.nn.gelu(pre_active, approximate=False))
    residual_two = hidden + low_back(matmul(active, w_down)) + add_bias[1]
    return layer_norm(residual_two, norm_gain[1], norm_bias[1])

def reference(tokens, segment_ids, out_cotangent, w_qkv, qv_bias, w_out, w_up, up_bias, w_down, add_bias, norm_gain, norm_bias):
    weights = tuple((member.astype(jnp.float32) for member in (w_qkv, qv_bias, w_out, w_up, up_bias, w_down, add_bias, norm_gain, norm_bias)))
    start_rows = tokens.astype(jnp.float32)
    probe_rows = jnp.zeros_like(start_rows)

    def forward(start_rows, probe_rows, *weights):
        first_out = layer(start_rows, segment_ids, *[member[0] for member in weights])
        sent_rows = low_back(low(first_out)) + probe_rows
        last_out = layer(sent_rows, segment_ids, *[member[1] for member in weights])
        return (last_out, first_out)
    last_out, pull_back, first_out = jax.vjp(forward, start_rows, probe_rows, *weights, has_aux=True)
    gradients = pull_back(out_cotangent.astype(jnp.float32))
    layer_outputs = jnp.stack([first_out, last_out]).astype(jnp.bfloat16)
    input_grads = jnp.stack([gradients[0], gradients[1]])
    return (layer_outputs, input_grads, gradients[2], gradients[3], gradients[4], gradients[5], gradients[6], gradients[7], gradients[8], gradients[9], gradients[10])
```

```python
from functools import partial

import jax
import jax.numpy as jnp
from jax import lax
from jax.experimental import pallas as pl
from jax.experimental.pallas import tpu as pltpu
from jax.sharding import PartitionSpec as P

HEAD_DIM = 64
norm_eps = 1e-12
masked_score = -1e30
MESH = pl.DeviceIdType.MESH
F32 = jnp.float32
BF16 = jnp.bfloat16


def mm(a, b):
    return lax.dot_general(a, b, (((1,), (0,)), ((), ())), preferred_element_type=F32)


def mm_nt(a, b):
    return lax.dot_general(a, b, (((1,), (1,)), ((), ())), preferred_element_type=F32)


def mm_tn(a, b):
    return lax.dot_general(a, b, (((0,), (0,)), ((), ())), preferred_element_type=F32)


def ds(start, size, align=None):
    return pl.ds(pl.multiple_of(start, align or size), size)


def row_mean(v):
    return jnp.sum(v, axis=-1, keepdims=True) * (1.0 / v.shape[-1])


def main_kernel(
    D, FF, S,
    tok, cot, segk, segq, wq_in, wo_in, wu_in, wd_in, bq_in, bu_in, vec,
    lo, ig, gq, go, gu, gd, gsq, gsu, gsv,
    wq, wo, wu, wd, bq, bu,
    X, QKV, O, N1, N2, Hr, U, GP, R, dB, dA, dOs, dQKV,
    r1s, r2s, Hf, Zf, bias, dY, YB, IGB, IGF, T1, T2, T3,
    rq, ro, ru, rd, sq, su, sv, sqr, sur, svr,
    lsem, wsend, wrecv, rsend, rrecv, gsend, grecv, osem,
):
    s = lax.axis_index("section")
    d = lax.axis_index("dp")
    c = lax.axis_index("tensor")
    other = 1 - c
    core_peer = (s, d, other)
    x_peer = (1 - s, d, c)
    half_d, half_f, half_q = D // 2, FF // 2, 3 * D // 2
    pairs = D // 128
    lo_pairs = pairs // 2

    barrier = pltpu.get_barrier_semaphore()
    pl.semaphore_signal(barrier, inc=1, device_id=core_peer, device_id_type=MESH)
    pl.semaphore_signal(barrier, inc=1, device_id=x_peer, device_id_type=MESH)

    def places(k):
        return [
            (wq_in, wq.at[:, ds(k * half_q, half_q, 128)]),
            (bq_in, bq.at[:, ds(k * half_q, half_q, 128)]),
            (wo_in, wo.at[ds(k * half_d, half_d), :]),
            (bu_in, bu.at[:, ds(k * half_f, half_f, 128)]),
            (wu_in, wu.at[:, ds(k * half_f, half_f, 128)]),
            (wd_in, wd.at[ds(k * half_f, half_f), :]),
        ]

    own_places = places(c)
    local = [pltpu.make_async_copy(src, dst, lsem.at[i]) for i, (src, dst) in enumerate(own_places)]
    remote = [
        pltpu.make_async_remote_copy(src, dst, wsend.at[i], wrecv.at[i], device_id=core_peer, device_id_type=MESH)
        for i, (src, dst) in enumerate(own_places)
    ]
    tok_copy = pltpu.make_async_copy(tok, X, lsem.at[6])
    cot_copy = pltpu.make_async_copy(cot, dY, lsem.at[7])

    @pl.when(s == 0)
    def _():
        tok_copy.start()

    @pl.when(s == 1)
    def _():
        cot_copy.start()

    local[0].start()
    local[1].start()
    pl.semaphore_wait(barrier, 2)
    for i in range(6):
        remote[i].start()
        if i >= 2:
            local[i].start()

    def need(*which):
        for i in which:
            local[i].wait()
            remote[i].wait_recv()

    for q in range(2):
        bias[q] = jnp.where(segk[q] == segq[q], 0.0, masked_score)
    sq[...] = jnp.zeros_like(sq)
    su[...] = jnp.zeros_like(su)
    sv[...] = jnp.zeros_like(sv)
    lane = lax.broadcasted_iota(jnp.int32, (1, 128), 1)
    first_scaled = jnp.where(lane < HEAD_DIM, 0.125, 0.0).astype(BF16)
    second_scaled = jnp.where(lane < HEAD_DIM, 0.0, 0.125).astype(BF16)
    first_half = jnp.where(lane < HEAD_DIM, 1.0, 0.0).astype(BF16)
    second_half = jnp.where(lane < HEAD_DIM, 0.0, 1.0).astype(BF16)

    def relay(m):
        rows = ds(m * S, S)
        return pltpu.make_async_remote_copy(YB.at[rows], X.at[rows], rsend.at[m], rrecv.at[m], device_id=x_peer, device_id_type=MESH)

    def relay_back(m):
        rows = ds(m * S, S)
        return pltpu.make_async_remote_copy(IGB.at[rows], dY.at[rows], rsend.at[m], rrecv.at[m], device_id=x_peer, device_id_type=MESH)

    def pair_columns(p):
        base = (p // lo_pairs) * half_q + (p % lo_pairs) * 128
        return ds(base, 128), ds(base + half_d, 128), ds(base + 2 * half_d, 128)

    def normed(z, which):
        centered = z - row_mean(z)
        scaled = lax.rsqrt(row_mean(centered * centered) + norm_eps)
        n = centered * scaled
        return n, scaled, n * vec[2 + which : 3 + which, :] + vec[4 + which : 5 + which, :]

    def forward(t, m):
        rows = ds(m * S, S)

        @pl.when(t == 0)
        def _():
            @pl.when(s == 0)
            def _():
                tok_copy.wait()
            need(0, 1)

        @pl.when(s == 1)
        def _():
            relay(m).wait_recv()

        def qkv_tile(i, _):
            cols = ds(i * 256, 256)
            QKV[rows, cols] = (mm(X[rows, :], wq[:, cols]) + bq[0:1, cols]).astype(BF16)
            return 0

        lax.fori_loop(0, 3 * D // 256, qkv_tile, 0)

        def attend(p, _):
            qc, kc, vc = pair_columns(p)
            q2, k2, v2 = QKV[rows, qc], QKV[rows, kc], QKV[rows, vc]
            vt = v2.T
            outs = []
            for h, mask in enumerate((first_scaled, second_scaled)):
                st = mm_nt(k2 * mask, q2) + bias[m]
                e = jnp.exp(st - jnp.max(st, axis=0, keepdims=True))
                r = (e * (1.0 / jnp.sum(e, axis=0, keepdims=True))).astype(BF16)
                R[ds((m * pairs + p) * 2 * S + h * S, S), :] = r
                outs.append(mm(vt[h * HEAD_DIM : (h + 1) * HEAD_DIM], r))
            O[rows, ds(p * 128, 128)] = jnp.concatenate(outs, axis=0).T.astype(BF16)
            return 0

        lax.fori_loop(0, pairs, attend, 0)

        @pl.when(t == 0)
        def _():
            need(2)

        def out_tile(i, _):
            cols = ds(i * 256, 256)
            Zf[:, cols] = mm(O[rows, :], wo[:, cols]) + X[rows, cols].astype(F32) + vec[0:1, cols]
            return 0

        lax.fori_loop(0, D // 256, out_tile, 0)
        n, r, h = normed(Zf[...], 0)
        N1[rows, :] = n.astype(BF16)
        r1s[rows, :] = jnp.broadcast_to(r, (S, 128))
        Hf[...] = h
        Hr[rows, :] = h.astype(BF16)

        @pl.when(t == 0)
        def _():
            need(3, 4)

        def up_tile(i, _):
            cols = ds(i * 256, 256)
            g = mm(Hr[rows, :], wu[:, cols]) + bu[0:1, cols]
            cdf = 0.5 + 0.5 * lax.erf(g * 0.7071067811865476)
            U[rows, cols] = (g * cdf).astype(BF16)
            GP[rows, cols] = (cdf + g * (0.3989422804014327 * jnp.exp(g * g * -0.5))).astype(BF16)
            return 0

        lax.fori_loop(0, FF // 256, up_tile, 0)

        @pl.when(t == 0)
        def _():
            need(5)

        def down_tile(i, _):
            cols = ds(i * 256, 256)
            Zf[:, cols] = mm(U[rows, :], wd[:, cols]) + Hf[:, cols] + vec[1:2, cols]
            return 0

        lax.fori_loop(0, D // 256, down_tile, 0)
        n, r, y = normed(Zf[...], 1)
        N2[rows, :] = n.astype(BF16)
        r2s[rows, :] = jnp.broadcast_to(r, (S, 128))
        YB[rows, :] = y.astype(BF16)
        pltpu.make_async_copy(YB.at[rows], lo.at[rows], osem.at[m]).start()

        @pl.when(s == 0)
        def _():
            relay(m).start()

    def column_sum(v):
        return jnp.sum(v, axis=0, keepdims=True)

    def norm_back(dy, n, r, which):
        e = dy * vec[2 + which : 3 + which, :]
        dz = r * (e - row_mean(e) - n * row_mean(e * n))
        sv[0 + which : 1 + which, :] += column_sum(dz)
        sv[2 + which : 3 + which, :] += column_sum(dy * n)
        sv[4 + which : 5 + which, :] += column_sum(dy)
        return dz

    def backward(t, m):
        rows = ds(m * S, S)

        @pl.when(s == 0)
        def _():
            relay_back(m).wait_recv()

        @pl.when((s == 1) & (m == 0))
        def _():
            cot_copy.wait()

        dz2 = norm_back(dY[rows, :].astype(F32), N2[rows, :].astype(F32), r2s[rows, 0:1], 1)
        Zf[...] = dz2
        dB[rows, :] = dz2.astype(BF16)

        def down_back(i, _):
            cols = ds(i * 256, 256)
            dg = mm_nt(dB[rows, :], wd[cols, :]) * GP[rows, cols].astype(F32)
            su[0:1, cols] += column_sum(dg)
            GP[rows, cols] = dg.astype(BF16)
            return 0

        lax.fori_loop(0, FF // 256, down_back, 0)

        def up_back(i, _):
            cols = ds(i * 256, 256)
            Hf[:, cols] = mm_nt(GP[rows, :], wu[cols, :]) + Zf[:, cols]
            return 0

        lax.fori_loop(0, D // 256, up_back, 0)
        dz1 = norm_back(Hf[...], N1[rows, :].astype(F32), r1s[rows, 0:1], 0)
        Zf[...] = dz1
        dA[rows, :] = dz1.astype(BF16)

        def out_back(i, _):
            cols = ds(i * 256, 256)
            dOs[:, cols] = mm_nt(dA[rows, :], wo[cols, :]).astype(BF16)
            return 0

        lax.fori_loop(0, D // 256, out_back, 0)

        def attend_back(p, _):
            qc, kc, vc = pair_columns(p)
            q2, k2, v2 = QKV[rows, qc], QKV[rows, kc], QKV[rows, vc]
            do2 = dOs[:, ds(p * 128, 128)]
            kt = k2.T
            dk, dv, dqt = 0.0, 0.0, []
            for h, (scaled, half) in enumerate(((first_scaled, first_half), (second_scaled, second_half))):
                r = R[ds((m * pairs + p) * 2 * S + h * S, S), :]
                drt = mm_nt(v2 * half, do2)
                rf = r.astype(F32)
                w = rf * drt
                dst = (w - rf * jnp.sum(w, axis=0, keepdims=True)).astype(BF16)
                dk += mm(dst, q2 * scaled)
                dv += mm(r, do2 * half)
                dqt.append(mm(kt[h * HEAD_DIM : (h + 1) * HEAD_DIM], dst))
            dq = (jnp.concatenate(dqt, axis=0) * 0.125).T.astype(BF16)
            dvb = dv.astype(BF16)
            dQKV[rows, qc] = dq
            dQKV[rows, kc] = dk.astype(BF16)
            dQKV[rows, vc] = dvb
            sq[0:1, qc] += column_sum(dq.astype(F32))
            sq[0:1, vc] += column_sum(dvb.astype(F32))
            return 0

        lax.fori_loop(0, pairs, attend_back, 0)

        def in_back(i, _):
            cols = ds(i * 256, 256)
            dx = mm_nt(dQKV[rows, :], wq[cols, :]) + Zf[:, cols]
            IGF[rows, cols] = dx
            IGB[rows, cols] = dx.astype(BF16)
            return 0

        lax.fori_loop(0, D // 256, in_back, 0)
        pltpu.make_async_copy(IGF.at[rows], ig.at[rows], osem.at[2 + m]).start()

        @pl.when(s == 1)
        def _():
            relay_back(m).start()

    def step(t, _):
        back = jnp.where(s == 0, t // 2, t % 2)
        m = jnp.where(s == 0, t % 2, t // 2)

        @pl.when(back == 0)
        def _():
            forward(t, m)

        @pl.when(back == 1)
        def _():
            backward(t, m)

        return 0

    lax.fori_loop(0, 4, step, 0)
    for i in range(6):
        remote[i].wait_send()

    def grads_down(k, mine):
        def tile(i, _):
            rows = ds(k * half_f + i * 256, 256)
            g = mm(U[:, rows].T, dB[...])
            if mine:
                g = g + rd[ds(i * 256, 256), :].astype(F32)
            wd[rows, :] = g.astype(BF16)
            return 0
        lax.fori_loop(0, half_f // 256, tile, 0)

    def grads_up(k, mine):
        def tile(i, _):
            cols = ds(k * half_f + i * 256, 256)
            g = mm(T1[...], GP[:, cols])
            if mine:
                g = g + ru[:, ds(i * 256, 256)].astype(F32)
            wu[:, cols] = g.astype(BF16)
            return 0
        lax.fori_loop(0, half_f // 256, tile, 0)

    def grads_out(k, mine):
        rows = ds(k * half_d, half_d)
        g = mm(T2[rows, :], dA[...])
        if mine:
            g = g + ro[...].astype(F32)
        wo[rows, :] = g.astype(BF16)

    def grads_qkv(k, mine):
        def tile(i, _):
            cols = ds(k * half_q + i * 384, 384, 128)
            g = mm(T3[...], dQKV[:, cols])
            if mine:
                g = g + rq[:, ds(i * 384, 384)].astype(F32)
            wq[:, cols] = g.astype(BF16)
            return 0
        lax.fori_loop(0, half_q // 384, tile, 0)

    slices = [
        (wd.at[ds(other * half_f, half_f), :], rd),
        (wu.at[:, ds(other * half_f, half_f, 128)], ru),
        (wo.at[ds(other * half_d, half_d), :], ro),
        (wq.at[:, ds(other * half_q, half_q, 128)], rq),
        (sq, sqr), (su, sur), (sv, svr),
    ]
    exchange = [
        pltpu.make_async_remote_copy(src, dst, gsend.at[i], grecv.at[i], device_id=core_peer, device_id_type=MESH)
        for i, (src, dst) in enumerate(slices)
    ]
    for i in (4, 5, 6):
        exchange[i].start()
    T1[...] = Hr[...].T
    T2[...] = O[...].T
    T3[...] = X[...].T
    for i, work in enumerate((grads_down, grads_up, grads_out, grads_qkv)):
        work(other, False)
        exchange[i].start()
    results = [
        (wd.at[ds(c * half_f, half_f), :], gd),
        (wu.at[:, ds(c * half_f, half_f, 128)], gu),
        (wo.at[ds(c * half_d, half_d), :], go),
        (wq.at[:, ds(c * half_q, half_q, 128)], gq),
        (sq, gsq), (su, gsu), (sv, gsv),
    ]
    results = [pltpu.make_async_copy(src, dst, osem.at[4 + i]) for i, (src, dst) in enumerate(results)]
    for i, work in enumerate((grads_down, grads_up, grads_out, grads_qkv)):
        exchange[i].wait_recv()
        work(c, True)
        results[i].start()
    for i, (mine, theirs) in ((4, (sq, sqr)), (5, (su, sur)), (6, (sv, svr))):
        exchange[i].wait()
        mine[...] += theirs[...]
        results[i].start()
    for i in range(4):
        exchange[i].wait_send()
    for i in range(7):
        results[i].wait()
    for m in range(2):
        rows = ds(m * S, S)
        pltpu.make_async_copy(YB.at[rows], lo.at[rows], osem.at[m]).wait()
        pltpu.make_async_copy(IGF.at[rows], ig.at[rows], osem.at[2 + m]).wait()

    @pl.when(s == 0)
    def _():
        for m in range(2):
            relay(m).wait_send()

    @pl.when(s == 1)
    def _():
        for m in range(2):
            relay_back(m).wait_send()


def main_call(tok, cot, segk, segq, wq, wo, wu, wd, bq, bu, vec, S):
    rows, D = tok.shape
    FF = 2 * wu.shape[1]
    hd, hf, hq = D // 2, FF // 2, 3 * D // 2
    any_spec = pl.BlockSpec(memory_space=pl.ANY)
    vm_spec = pl.BlockSpec(memory_space=pltpu.VMEM)
    sds = jax.ShapeDtypeStruct
    V = pltpu.VMEM
    out_shape = (
        sds((rows, D), BF16), sds((rows, D), F32),
        sds((D, hq), BF16), sds((hd, D), BF16), sds((D, hf), BF16), sds((hf, D), BF16),
        sds((8, 2 * hq), F32), sds((8, FF), F32), sds((8, D), F32),
    )
    scratch = [
        V((D, 2 * hq), BF16), V((D, D), BF16), V((D, FF), BF16), V((FF, D), BF16), V((8, 2 * hq), F32), V((8, FF), F32),
        V((rows, D), BF16), V((rows, 3 * D), BF16), V((rows, D), BF16), V((rows, D), BF16), V((rows, D), BF16), V((rows, D), BF16),
        V((rows, FF), BF16), V((rows, FF), BF16), V((2 * (D // HEAD_DIM) * S, S), BF16),
        V((rows, D), BF16), V((rows, D), BF16), V((S, D), BF16), V((rows, 3 * D), BF16),
        V((rows, 128), F32), V((rows, 128), F32), V((S, D), F32), V((S, D), F32), V((2, S, S), F32),
        V((rows, D), BF16), V((rows, D), BF16), V((rows, D), BF16), V((rows, D), F32),
        V((D, rows), BF16), V((D, rows), BF16), V((D, rows), BF16),
        V((D, hq), BF16), V((hd, D), BF16), V((D, hf), BF16), V((hf, D), BF16),
        V((8, 2 * hq), F32), V((8, FF), F32), V((8, D), F32), V((8, 2 * hq), F32), V((8, FF), F32), V((8, D), F32),
        pltpu.SemaphoreType.DMA((8,)), pltpu.SemaphoreType.DMA((6,)), pltpu.SemaphoreType.DMA((6,)),
        pltpu.SemaphoreType.DMA((2,)), pltpu.SemaphoreType.DMA((2,)),
        pltpu.SemaphoreType.DMA((7,)), pltpu.SemaphoreType.DMA((7,)), pltpu.SemaphoreType.DMA((11,)),
    ]
    return pl.pallas_call(
        partial(main_kernel, D, FF, S),
        out_shape=out_shape,
        in_specs=[any_spec, any_spec, vm_spec, vm_spec] + [any_spec] * 6 + [vm_spec],
        out_specs=(any_spec,) * 9,
        scratch_shapes=scratch,
        compiler_params=pltpu.CompilerParams(collective_id=0, has_side_effects=True, vmem_limit_bytes=60 * 2**20),
        name="layer_pass",
    )(tok, cot, segk, segq, wq, wo, wu, wd, bq, bu, vec)


def shards(tokens, segment_ids, out_cotangent, w_qkv, qv_bias, w_out, w_up, up_bias, w_down, add_bias, norm_gain, norm_bias):
    c = lax.axis_index("tensor")
    D = tokens.shape[1]
    hd = D // 2
    S = segment_ids.shape[1]
    seqs = tokens.shape[0] // S
    seg = lax.dynamic_slice_in_dim(segment_ids, c * seqs, seqs, axis=0)
    vec = jnp.concatenate([add_bias[0], norm_gain[0], norm_bias[0], jnp.zeros((2, D), F32)], axis=0)
    qv = qv_bias[0].astype(F32)
    bq = jnp.concatenate([qv[0], jnp.zeros((hd,), F32), qv[1]])
    bq = jnp.broadcast_to(bq[None], (8, 3 * hd))
    bu = jnp.broadcast_to(up_bias.astype(F32), (8, up_bias.shape[1]))
    lo, ig, gq, go, gu, gd, gsq, gsu, gsv = main_call(
        tokens, out_cotangent, seg[:, :, None], seg[:, None, :],
        w_qkv[0].reshape(D, 3 * hd), w_out[0], w_up[0], w_down[0], bq, bu, vec, S,
    )
    def own(v, size):
        return lax.dynamic_slice_in_dim(v, c * size, size, axis=-1)
    sq = own(gsq[0], 3 * hd)
    small = [jnp.concatenate([sq[:hd], sq[2 * hd :]]), own(gsu[0], up_bias.shape[1]), own(gsv[:6], hd).reshape(-1)]
    tot = lax.psum(tuple(v.astype(BF16) for v in (gq, go, gu, gd, *small)), "dp")
    gq, go, gu, gd, gqv, gub, gsv = (v.astype(F32) for v in tot)
    gsv = gsv.reshape(6, hd)
    return (
        lo[None], ig[None],
        gq.reshape(1, D, 3, hd), gqv.reshape(1, 2, hd), go[None], gu[None], gub[None], gd[None],
        gsv[None, 0:2], gsv[None, 2:4], gsv[None, 4:6],
    )


def solution(mesh):
    return jax.shard_map(
        shards,
        mesh=mesh,
        in_specs=(
            P(("dp", "tensor"), None), P("dp", None), P(("dp", "tensor"), None),
            P("section", None, None, "tensor"), P("section", None, "tensor"), P("section", "tensor", None),
            P("section", None, "tensor"), P("section", "tensor"), P("section", "tensor", None),
            P("section", None, None), P("section", None, None), P("section", None, None),
        ),
        out_specs=(
            P("section", ("dp", "tensor"), None), P("section", ("dp", "tensor"), None),
            P("section", None, None, "tensor"), P("section", None, "tensor"), P("section", "tensor", None),
            P("section", None, "tensor"), P("section", "tensor"), P("section", "tensor", None),
            P("section", None, "tensor"), P("section", None, "tensor"), P("section", None, "tensor"),
        ),
        check_vma=False,
    )
```

```python
from functools import partial

import jax
import jax.numpy as jnp
from jax import lax
from jax.experimental import pallas as pl
from jax.experimental.pallas import tpu as pltpu
from jax.sharding import PartitionSpec as P

HEAD_DIM = 64
norm_eps = 1e-12
masked_score = -1e30
LINE = 4
BUCKETS = 12
A_ROWS = 512
MESH = pl.DeviceIdType.MESH
F32 = jnp.float32
BF16 = jnp.bfloat16


def mm(a, b):
    return lax.dot_general(a, b, (((1,), (0,)), ((), ())), preferred_element_type=F32)


def mm_nt(a, b):
    return lax.dot_general(a, b, (((1,), (1,)), ((), ())), preferred_element_type=F32)


def mm_tn(a, b):
    return lax.dot_general(a, b, (((0,), (0,)), ((), ())), preferred_element_type=F32)


def ds(start, size, align=None):
    return pl.ds(pl.multiple_of(start, align or size), size)


def row_mean(v):
    return jnp.sum(v, axis=-1, keepdims=True) * (1.0 / v.shape[-1])


class Line:
    def __init__(self, red, base, size, landing, sems):
        self.red, self.base, self.size, self.landing, self.sems = red, base, size, landing, sems

    def own(self, b, j):
        return ds(self.base(b) + j * self.size, self.size, 16)

    def slot(self, b, j):
        return ds((b * (LINE + 1) + j) * self.size, self.size, 16)

    def sum_up(self, b, j):
        r = self.red
        return r.remote(r.G.at[self.own(b, j)], self.landing.at[self.slot(b, j)], b, self.sems + j, r.above)

    def sum_down(self, b, j):
        r = self.red
        place = jnp.where(j == r.z - 1, LINE, j)
        return r.remote(r.G.at[self.own(b, j)], self.landing.at[self.slot(b, place)], b, self.sems + LINE + j, r.below)

    def from_above(self, b, j):
        r = self.red
        place = jnp.where(j == r.z, LINE, j)
        return r.remote(r.G.at[self.own(b, j)], self.landing.at[self.slot(b, place)], b, self.sems + LINE + j, r.below)

    def out_up(self, b, j, own=False):
        r = self.red
        return r.remote(r.place(own).at[self.own(b, j)], r.out.at[self.own(b, j)], b, self.sems + 2 * LINE + j, r.above)

    def out_down(self, b, j, own=False):
        r = self.red
        return r.remote(r.place(own).at[self.own(b, j)], r.out.at[self.own(b, j)], b, self.sems + 3 * LINE + j, r.below)

    def add(self, b, j, *places):
        G = self.red.G
        rows = self.own(b, j)
        total = G[rows, :].astype(F32)
        for place in places:
            total = total + self.landing[self.slot(b, place), :].astype(F32)
        G[rows, :] = total.astype(BF16)

    def begin(self, b):
        z = self.red.z

        @pl.when(z == 0)
        def _():
            for i in range(LINE - 1):
                self.sum_up(b, LINE - 1 - i).start()

        @pl.when(z == LINE - 1)
        def _():
            for i in range(LINE - 1):
                self.sum_down(b, i).start()

    def pass_on(self, b, i):
        z = self.red.z
        end = LINE - 1 - z
        up, down = LINE - 2 - i + z, 1 + i - end

        @pl.when((up > z) & (up < LINE) & (z > 0))
        def _():
            self.sum_up(b, up).wait_recv()
            self.add(b, up, up)
            self.sum_up(b, up).start()

        @pl.when((down < z) & (down >= 0) & (end > 0))
        def _():
            self.from_above(b, down).wait_recv()
            self.add(b, down, down)
            self.sum_down(b, down).start()

    def finish_own(self, b):
        z = self.red.z

        @pl.when(z > 0)
        def _():
            self.sum_up(b, z).wait_recv()

        @pl.when(z < LINE - 1)
        def _():
            self.from_above(b, z).wait_recv()

        @pl.when(z == 0)
        def _():
            self.add(b, 0, LINE)

        @pl.when(z == LINE - 1)
        def _():
            self.add(b, LINE - 1, LINE - 1)

        @pl.when((z > 0) & (z < LINE - 1))
        def _():
            self.add(b, z, z, LINE)

    def spread(self, b):
        z = self.red.z

        @pl.when(z < LINE - 1)
        def _():
            self.out_up(b, z, True).start()

        @pl.when(z > 0)
        def _():
            self.out_down(b, z, True).start()

        self.keep(b).start()

    def keep(self, b):
        r = self.red
        rows = self.own(b, r.z)
        return pltpu.make_async_copy(r.G.at[rows], r.out.at[rows], r.csem.at[b, self.sems // (4 * LINE)])

    def spread_on(self, b, i):
        z = self.red.z

        @pl.when(z - i >= 0)
        def _():
            self.out_up(b, z - i).wait_recv()

            @pl.when(z < LINE - 1)
            def _():
                self.out_up(b, z - i).start()

        @pl.when(z + i < LINE)
        def _():
            self.out_down(b, z + i).wait_recv()

            @pl.when(z > 0)
            def _():
                self.out_down(b, z + i).start()

    def drain(self, b):
        z = self.red.z
        for j in range(LINE):
            @pl.when(j > z)
            def _():
                self.sum_up(b, j).wait_send()

            @pl.when(j < z)
            def _():
                self.sum_down(b, j).wait_send()

            @pl.when((j <= z) & (z < LINE - 1))
            def _():
                self.out_up(b, j).wait_send()

            @pl.when((j >= z) & (z > 0))
            def _():
                self.out_down(b, j).wait_send()


class Reduction:
    stages = 9

    def __init__(self, D, s, d, c, G, out, LA1, LA, LB, LS, SM, SML, asend, arecv, ssend, srecv, csem):
        self.out, self.csem = out, csem
        self.G, self.LA1, self.LS, self.SM, self.SML = G, LA1, LS, SM, SML
        self.asend, self.arecv, self.ssend, self.srecv = asend, arecv, ssend, srecv
        self.z, self.y = d // 2, d % 2
        self.s, self.d, self.c = s, d, c
        self.above = (s, jnp.minimum(d + 2, 2 * LINE - 1), c)
        self.below = (s, jnp.maximum(d - 2, 0), c)
        self.beside = (s, d + 1 - 2 * self.y, c)
        self.half = A_ROWS // 2
        self.D = D
        self.a = Line(self, lambda b: b * D + self.y * self.half, self.half // LINE, LA, 0)
        self.b = Line(self, lambda b: b * D + A_ROWS, (D - A_ROWS) // LINE, LB, 4 * LINE)
        z = self.z
        pair = z + 1 - 2 * (z % 2)
        far = (z + 2) % 4
        self.small_peers = [None, self.beside, (s, pair * 2 + self.y, c), (s, far * 2 + self.y, c)]

    def place(self, own):
        return self.G if own else self.out

    def remote(self, src, dst, b, sem, to):
        return pltpu.make_async_remote_copy(src, dst, self.asend.at[b, sem], self.arecv.at[b, sem], device_id=to, device_id_type=MESH)

    def greet(self, barrier):
        def hello(to):
            pl.semaphore_signal(barrier, inc=1, device_id=to, device_id_type=MESH)
        for to in self.small_peers[1:]:
            hello(to)
        @pl.when((self.z == 1))
        def _():
            hello(self.above)

        @pl.when((self.z == 2))
        def _():
            hello(self.below)

    def greetings(self):
        return 3 + ((self.z == 1) | (self.z == 2)).astype(jnp.int32)

    def small_copy(self, k):
        return pltpu.make_async_remote_copy(self.SM, self.SML.at[k], self.ssend.at[k], self.srecv.at[k], device_id=self.small_peers[k], device_id_type=MESH)

    def small_start(self, k):
        self.small_copy(k).start()

    def small_finish(self, k):
        self.small_copy(k).wait()
        self.SM[...] += self.SML[k]

    def give_side(self, b):
        rows = ds(b * self.D + (1 - self.y) * self.half, self.half, 16)
        return self.remote(self.G.at[rows], self.LA1.at[ds(b * self.half, self.half, 16)], b, 8 * LINE, self.beside)

    def share_side(self, b):
        rows = ds(b * self.D + self.y * self.half, self.half, 16)
        return self.remote(self.out.at[rows], self.out.at[rows], b, 8 * LINE + 1, self.beside)

    def swap(self, b):
        size = self.b.size
        return self.remote(self.G.at[self.b.own(b, self.z)], self.LS.at[ds(b * size, size, 16)], b, 8 * LINE + 2, self.beside)

    def stage(self, k, b):
        A, B = self.a, self.b
        if k == 0:
            self.give_side(b).start()
            B.begin(b)
        elif k == 1:
            B.pass_on(b, 0)
            self.give_side(b).wait_recv()
            rows = ds(b * self.D + self.y * self.half, self.half, 16)
            land = ds(b * self.half, self.half, 16)
            self.G[rows, :] = (self.G[rows, :].astype(F32) + self.LA1[land, :].astype(F32)).astype(BF16)
            A.begin(b)
        elif k == 2:
            B.pass_on(b, 1)
            A.pass_on(b, 0)
        elif k == 3:
            B.finish_own(b)
            self.swap(b).start()
            A.pass_on(b, 1)
        elif k == 4:
            A.finish_own(b)
            A.spread(b)
            size = B.size
            self.swap(b).wait()
            rows, land = B.own(b, self.z), ds(b * size, size, 16)
            self.G[rows, :] = (self.G[rows, :].astype(F32) + self.LS[land, :].astype(F32)).astype(BF16)
            B.spread(b)
        elif k <= 7:
            A.spread_on(b, k - 4)
            B.spread_on(b, k - 4)
            if k == 7:
                A.keep(b).wait()
                self.share_side(b).start()
        else:
            self.share_side(b).wait_recv()

    def slot(self, tau):
        for k in range(self.stages - 1, -1, -1):
            b = tau - k

            @pl.when((b >= 0) & (b < BUCKETS))
            def _():
                self.stage(k, b)

    def drain(self):
        def one(b, _):
            self.a.drain(b)
            self.b.drain(b)
            self.give_side(b).wait_send()
            self.share_side(b).wait_send()
            self.b.keep(b).wait()
            return 0
        lax.fori_loop(0, BUCKETS, one, 0)


def main_kernel(
    D, FF, S, grid,
    tok, cot, segk, segq, wq_in, wo_in, wu_in, wd_in, bq_in, bu_in, vec,
    lo, ig, gall, gsm,
    wq, wo, wu, wd, bq, bu,
    X, QKV, O, N1, N2, Hr, U, GP, R, dB, dA, dOs, dQKV,
    r1s, r2s, Hf, Zf, bias, dY, YB, IGB, IGF,
    sq, su, sv, SM, SML, G, LA1, LA, LB, LS,
    lsem, wsend, wrecv, rsend, rrecv, gsend, grecv, osem, ssend, srecv, asend, arecv, csem,
):
    s = lax.axis_index("section")
    d = lax.axis_index("dp")
    c = lax.axis_index("tensor")
    other = 1 - c
    core_peer = (s, d, other)
    x_peer = (1 - s, d, c)
    half_d, half_f, half_q = D // 2, FF // 2, 3 * D // 2
    pairs = D // 128
    lo_pairs = pairs // 2

    barrier = pltpu.get_barrier_semaphore()
    pl.semaphore_signal(barrier, inc=1, device_id=core_peer, device_id_type=MESH)
    pl.semaphore_signal(barrier, inc=1, device_id=x_peer, device_id_type=MESH)
    if grid:
        ring = Reduction(D, s, d, c, G, gall, LA1, LA, LB, LS, SM, SML, asend, arecv, ssend, srecv, csem)
        ring.greet(barrier)

    def places(k):
        return [
            (wq_in, wq.at[:, ds(k * half_q, half_q, 128)]),
            (bq_in, bq.at[:, ds(k * half_q, half_q, 128)]),
            (wo_in, wo.at[ds(k * half_d, half_d), :]),
            (bu_in, bu.at[:, ds(k * half_f, half_f, 128)]),
            (wu_in, wu.at[:, ds(k * half_f, half_f, 128)]),
            (wd_in, wd.at[ds(k * half_f, half_f), :]),
        ]

    own_places = places(c)
    local = [pltpu.make_async_copy(src, dst, lsem.at[i]) for i, (src, dst) in enumerate(own_places)]
    remote = [
        pltpu.make_async_remote_copy(src, dst, wsend.at[i], wrecv.at[i], device_id=core_peer, device_id_type=MESH)
        for i, (src, dst) in enumerate(own_places)
    ]
    tok_copy = pltpu.make_async_copy(tok, X, lsem.at[6])
    cot_copy = pltpu.make_async_copy(cot, dY, lsem.at[7])

    @pl.when(s == 0)
    def _():
        tok_copy.start()

    @pl.when(s == 1)
    def _():
        cot_copy.start()

    local[0].start()
    local[1].start()
    pl.semaphore_wait(barrier, 2 + ring.greetings() if grid else 2)
    for i in range(6):
        remote[i].start()
        if i >= 2:
            local[i].start()

    def need(*which):
        for i in which:
            local[i].wait()
            remote[i].wait_recv()

    for q in range(2):
        bias[q] = jnp.where(segk[q] == segq[q], 0.0, masked_score)
    sq[...] = jnp.zeros_like(sq)
    su[...] = jnp.zeros_like(su)
    sv[...] = jnp.zeros_like(sv)
    lane = lax.broadcasted_iota(jnp.int32, (1, 128), 1)
    first_scaled = jnp.where(lane < HEAD_DIM, 0.125, 0.0).astype(BF16)
    second_scaled = jnp.where(lane < HEAD_DIM, 0.0, 0.125).astype(BF16)
    first_half = jnp.where(lane < HEAD_DIM, 1.0, 0.0).astype(BF16)
    second_half = jnp.where(lane < HEAD_DIM, 0.0, 1.0).astype(BF16)

    def relay(m):
        rows = ds(m * S, S)
        return pltpu.make_async_remote_copy(YB.at[rows], X.at[rows], rsend.at[m], rrecv.at[m], device_id=x_peer, device_id_type=MESH)

    def relay_back(m):
        rows = ds(m * S, S)
        return pltpu.make_async_remote_copy(IGB.at[rows], dY.at[rows], rsend.at[m], rrecv.at[m], device_id=x_peer, device_id_type=MESH)

    def pair_columns(p):
        base = (p // lo_pairs) * half_q + (p % lo_pairs) * 128
        return ds(base, 128), ds(base + half_d, 128), ds(base + 2 * half_d, 128)

    def normed(z, which):
        centered = z - row_mean(z)
        scaled = lax.rsqrt(row_mean(centered * centered) + norm_eps)
        n = centered * scaled
        return n, scaled, n * vec[2 + which : 3 + which, :] + vec[4 + which : 5 + which, :]

    def forward(t, m):
        rows = ds(m * S, S)

        @pl.when(t == 0)
        def _():
            @pl.when(s == 0)
            def _():
                tok_copy.wait()
            need(0, 1)

        @pl.when(s == 1)
        def _():
            relay(m).wait_recv()

        def qkv_tile(i, _):
            cols = ds(i * 256, 256)
            QKV[rows, cols] = (mm(X[rows, :], wq[:, cols]) + bq[0:1, cols]).astype(BF16)
            return 0

        lax.fori_loop(0, 3 * D // 256, qkv_tile, 0)

        def attend(p, _):
            qc, kc, vc = pair_columns(p)
            q2, k2, v2 = QKV[rows, qc], QKV[rows, kc], QKV[rows, vc]
            vt = v2.T
            outs = []
            for h, mask in enumerate((first_scaled, second_scaled)):
                st = mm_nt(k2 * mask, q2) + bias[m]
                e = jnp.exp(st - jnp.max(st, axis=0, keepdims=True))
                r = (e * (1.0 / jnp.sum(e, axis=0, keepdims=True))).astype(BF16)
                R[ds((m * pairs + p) * 2 * S + h * S, S), :] = r
                outs.append(mm(vt[h * HEAD_DIM : (h + 1) * HEAD_DIM], r))
            O[rows, ds(p * 128, 128)] = jnp.concatenate(outs, axis=0).T.astype(BF16)
            return 0

        lax.fori_loop(0, pairs, attend, 0)

        @pl.when(t == 0)
        def _():
            need(2)

        def out_tile(i, _):
            cols = ds(i * 256, 256)
            Zf[:, cols] = mm(O[rows, :], wo[:, cols]) + X[rows, cols].astype(F32) + vec[0:1, cols]
            return 0

        lax.fori_loop(0, D // 256, out_tile, 0)
        n, r, h = normed(Zf[...], 0)
        N1[rows, :] = n.astype(BF16)
        r1s[rows, :] = jnp.broadcast_to(r, (S, 128))
        Hf[...] = h
        Hr[rows, :] = h.astype(BF16)

        @pl.when(t == 0)
        def _():
            need(3, 4)

        def up_tile(i, _):
            cols = ds(i * 256, 256)
            g = mm(Hr[rows, :], wu[:, cols]) + bu[0:1, cols]
            cdf = 0.5 + 0.5 * lax.erf(g * 0.7071067811865476)
            U[rows, cols] = (g * cdf).astype(BF16)
            GP[rows, cols] = (cdf + g * (0.3989422804014327 * jnp.exp(g * g * -0.5))).astype(BF16)
            return 0

        lax.fori_loop(0, FF // 256, up_tile, 0)

        @pl.when(t == 0)
        def _():
            need(5)

        def down_tile(i, _):
            cols = ds(i * 256, 256)
            Zf[:, cols] = mm(U[rows, :], wd[:, cols]) + Hf[:, cols] + vec[1:2, cols]
            return 0

        lax.fori_loop(0, D // 256, down_tile, 0)
        n, r, y = normed(Zf[...], 1)
        N2[rows, :] = n.astype(BF16)
        r2s[rows, :] = jnp.broadcast_to(r, (S, 128))
        YB[rows, :] = y.astype(BF16)
        pltpu.make_async_copy(YB.at[rows], lo.at[rows], osem.at[m]).start()

        @pl.when(s == 0)
        def _():
            relay(m).start()

    def column_sum(v):
        return jnp.sum(v, axis=0, keepdims=True)

    def norm_back(dy, n, r, which):
        e = dy * vec[2 + which : 3 + which, :]
        dz = r * (e - row_mean(e) - n * row_mean(e * n))
        sv[0 + which : 1 + which, :] += column_sum(dz)
        sv[2 + which : 3 + which, :] += column_sum(dy * n)
        sv[4 + which : 5 + which, :] += column_sum(dy)
        return dz

    def backward(t, m):
        rows = ds(m * S, S)

        @pl.when(s == 0)
        def _():
            relay_back(m).wait_recv()

        @pl.when((s == 1) & (m == 0))
        def _():
            cot_copy.wait()

        dz2 = norm_back(dY[rows, :].astype(F32), N2[rows, :].astype(F32), r2s[rows, 0:1], 1)
        Zf[...] = dz2
        dB[rows, :] = dz2.astype(BF16)

        def down_back(i, _):
            cols = ds(i * 256, 256)
            dg = mm_nt(dB[rows, :], wd[cols, :]) * GP[rows, cols].astype(F32)
            su[0:1, cols] += column_sum(dg)
            GP[rows, cols] = dg.astype(BF16)
            return 0

        lax.fori_loop(0, FF // 256, down_back, 0)

        def up_back(i, _):
            cols = ds(i * 256, 256)
            Hf[:, cols] = mm_nt(GP[rows, :], wu[cols, :]) + Zf[:, cols]
            return 0

        lax.fori_loop(0, D // 256, up_back, 0)
        dz1 = norm_back(Hf[...], N1[rows, :].astype(F32), r1s[rows, 0:1], 0)
        Zf[...] = dz1
        dA[rows, :] = dz1.astype(BF16)

        def out_back(i, _):
            cols = ds(i * 256, 256)
            dOs[:, cols] = mm_nt(dA[rows, :], wo[cols, :]).astype(BF16)
            return 0

        lax.fori_loop(0, D // 256, out_back, 0)

        def attend_back(p, _):
            qc, kc, vc = pair_columns(p)
            q2, k2, v2 = QKV[rows, qc], QKV[rows, kc], QKV[rows, vc]
            do2 = dOs[:, ds(p * 128, 128)]
            kt = k2.T
            dk, dv, dqt = 0.0, 0.0, []
            for h, (scaled, half) in enumerate(((first_scaled, first_half), (second_scaled, second_half))):
                r = R[ds((m * pairs + p) * 2 * S + h * S, S), :]
                drt = mm_nt(v2 * half, do2)
                rf = r.astype(F32)
                w = rf * drt
                dst = (w - rf * jnp.sum(w, axis=0, keepdims=True)).astype(BF16)
                dk += mm(dst, q2 * scaled)
                dv += mm(r, do2 * half)
                dqt.append(mm(kt[h * HEAD_DIM : (h + 1) * HEAD_DIM], dst))
            dq = (jnp.concatenate(dqt, axis=0) * 0.125).T.astype(BF16)
            dvb = dv.astype(BF16)
            dQKV[rows, qc] = dq
            dQKV[rows, kc] = dk.astype(BF16)
            dQKV[rows, vc] = dvb
            sq[0:1, qc] += column_sum(dq.astype(F32))
            sq[0:1, vc] += column_sum(dvb.astype(F32))
            return 0

        lax.fori_loop(0, pairs, attend_back, 0)

        def in_back(i, _):
            cols = ds(i * 256, 256)
            dx = mm_nt(dQKV[rows, :], wq[cols, :]) + Zf[:, cols]
            IGF[rows, cols] = dx
            IGB[rows, cols] = dx.astype(BF16)
            return 0

        lax.fori_loop(0, D // 256, in_back, 0)
        pltpu.make_async_copy(IGF.at[rows], ig.at[rows], osem.at[2 + m]).start()

        @pl.when(s == 1)
        def _():
            relay_back(m).start()

    def step(t, _):
        back = jnp.where(s == 0, t // 2, t % 2)
        m = jnp.where(s == 0, t % 2, t // 2)

        @pl.when(back == 0)
        def _():
            forward(t, m)

        @pl.when(back == 1)
        def _():
            backward(t, m)

        return 0

    lax.fori_loop(0, 4, step, 0)
    for i in range(6):
        remote[i].wait_send()

    W = D // 2

    def grad_tiles(k, kind, i):
        if kind == "down" or kind == "out":
            rows = ds(k * half_f + i * W, W, 128) if kind == "down" else ds(k * half_d, W)
            if kind == "out":
                return [across(1, k * half_d, W, dA[:, q * W : (q + 1) * W]) for q in range(2)]
            left = U[:, rows].T
            return [mm(left, dB[:, q * W : (q + 1) * W]) for q in range(2)]
        cols = ds(k * (half_f if kind == "up" else half_q) + i * W, W, 128)
        i, right = (0, GP) if kind == "up" else (2, dQKV)
        return [across(i, q * W, W, right[:, cols]) for q in range(2)]

    first = {"down": 0, "up": 4, "qkv": 8, "out": 11}

    def halves(k, kind, i):
        if kind == "down":
            return [wd.at[ds(k * half_f + i * W, W), q * W : (q + 1) * W] for q in range(2)]
        if kind == "out":
            return [wo.at[ds(k * half_d, W), q * W : (q + 1) * W] for q in range(2)]
        cols = ds(k * (half_f if kind == "up" else half_q) + i * W, W, 128)
        ref = wu if kind == "up" else wq
        return [ref.at[q * W : (q + 1) * W, cols] for q in range(2)]

    def exchange(kind, i):
        b = first[kind] + i
        return [
            pltpu.make_async_remote_copy(part, G.at[ds(b * D + q * W, W)], gsend.at[b, q], grecv.at[b, q], device_id=core_peer, device_id_type=MESH)
            for q, part in enumerate(halves(other, kind, i))
        ]

    def give(kind, i):
        tiles = grad_tiles(other, kind, i)
        for q, copy in enumerate(exchange(kind, i)):
            halves(other, kind, i)[q][...] = tiles[q].astype(BF16)
            copy.start()

    def keep(kind, i):
        tiles = grad_tiles(c, kind, i)
        b = first[kind] + i
        for q, copy in enumerate(exchange(kind, i)):
            copy.wait_recv()
            rows = ds(b * D + q * W, W)
            G[rows, :] = (tiles[q] + G[rows, :].astype(F32)).astype(BF16)

    def slot(tau):
        if grid:
            ring.slot(tau)

    for i in range(3):
        SM[i : i + 1, :] = sq[0:1, i * D : (i + 1) * D]
    for i in range(4):
        SM[3 + i : 4 + i, :] = su[0:1, i * D : (i + 1) * D]
    SM[7:8, :] = jnp.zeros((1, D), F32)
    SM[8:16, :] = sv[...]
    small_core = pltpu.make_async_remote_copy(SM, SML.at[0], ssend.at[0], srecv.at[0], device_id=core_peer, device_id_type=MESH)
    small_core.start()
    for i, whole in enumerate((Hr, O, X)):
        for m in range(2):
            R[(2 * i + m) * D : (2 * i + m + 1) * D, :] = whole[m * S : (m + 1) * S, :].T

    def across(i, start, size, right):
        return sum(mm(R[ds((2 * i + m) * D + start, size, 128), :], right[m * S : (m + 1) * S]) for m in range(2))


    def first_loop(i, _):
        give("down", i)
        return 0

    def second_loop(i, _):
        keep("down", i)
        slot(i)
        give("up", i)
        return 0

    def third_loop(i, _):
        keep("up", i)
        slot(4 + i)

        @pl.when(i < 3)
        def _():
            give("qkv", i)

        @pl.when(i == 3)
        def _():
            give("out", 0)

        return 0

    def fourth_loop(i, _):
        @pl.when(i < 3)
        def _():
            keep("qkv", i)

        @pl.when(i == 3)
        def _():
            keep("out", 0)

        slot(8 + i)
        return 0

    lax.fori_loop(0, 4, first_loop, 0)
    small_core.wait()
    SM[...] += SML[0]
    if grid:
        ring.small_start(1)
    lax.fori_loop(0, 4, second_loop, 0)
    if grid:
        ring.small_finish(1)
        ring.small_start(2)
    lax.fori_loop(0, 4, third_loop, 0)
    if grid:
        ring.small_finish(2)
        ring.small_start(3)
    lax.fori_loop(0, 4, fourth_loop, 0)
    if grid:
        ring.small_finish(3)

        def last_loop(tau, _):
            slot(tau)
            return 0

        lax.fori_loop(12, 12 + ring.stages - 1, last_loop, 0)
        ring.drain()
    if not grid:
        result = pltpu.make_async_copy(G, gall, osem.at[4])
        result.start()
        result.wait()
    small_result = pltpu.make_async_copy(SM, gsm, osem.at[5])
    small_result.start()
    for kind, n in (("down", 4), ("up", 4), ("qkv", 3), ("out", 1)):
        for i in range(n):
            for copy in exchange(kind, i):
                copy.wait_send()
    small_result.wait()
    for m in range(2):
        rows = ds(m * S, S)
        pltpu.make_async_copy(YB.at[rows], lo.at[rows], osem.at[m]).wait()
        pltpu.make_async_copy(IGF.at[rows], ig.at[rows], osem.at[2 + m]).wait()

    @pl.when(s == 0)
    def _():
        for m in range(2):
            relay(m).wait_send()

    @pl.when(s == 1)
    def _():
        for m in range(2):
            relay_back(m).wait_send()


def main_call(tok, cot, segk, segq, wq, wo, wu, wd, bq, bu, vec, S, grid):
    rows, D = tok.shape
    FF = 2 * wu.shape[1]
    hd, hf, hq = D // 2, FF // 2, 3 * D // 2
    any_spec = pl.BlockSpec(memory_space=pl.ANY)
    vm_spec = pl.BlockSpec(memory_space=pltpu.VMEM)
    sds = jax.ShapeDtypeStruct
    V = pltpu.VMEM
    out_shape = (
        sds((rows, D), BF16), sds((rows, D), F32),
        sds((BUCKETS * D, hd), BF16), sds((16, D), F32),
    )
    scratch = [
        V((D, 2 * hq), BF16), V((D, D), BF16), V((D, FF), BF16), V((FF, D), BF16), V((8, 2 * hq), F32), V((8, FF), F32),
        V((rows, D), BF16), V((rows, 3 * D), BF16), V((rows, D), BF16), V((rows, D), BF16), V((rows, D), BF16), V((rows, D), BF16),
        V((rows, FF), BF16), V((rows, FF), BF16), V((2 * (D // HEAD_DIM) * S, S), BF16),
        V((rows, D), BF16), V((rows, D), BF16), V((S, D), BF16), V((rows, 3 * D), BF16),
        V((rows, 128), F32), V((rows, 128), F32), V((S, D), F32), V((S, D), F32), V((2, S, S), F32),
        V((rows, D), BF16), V((rows, D), BF16), V((rows, D), BF16), V((rows, D), F32),
        V((8, 2 * hq), F32), V((8, FF), F32), V((8, D), F32), V((16, D), F32), V((4, 16, D), F32),
        V((BUCKETS * D, hd), BF16), V((BUCKETS * A_ROWS // 2, hd), BF16), V((BUCKETS * (A_ROWS // 2) // 4 * 5, hd), BF16),
        V((BUCKETS * (D - A_ROWS) // 4 * 5, hd), BF16), V((BUCKETS * (D - A_ROWS) // 4, hd), BF16),
        pltpu.SemaphoreType.DMA((8,)), pltpu.SemaphoreType.DMA((6,)), pltpu.SemaphoreType.DMA((6,)),
        pltpu.SemaphoreType.DMA((2,)), pltpu.SemaphoreType.DMA((2,)),
        pltpu.SemaphoreType.DMA((BUCKETS, 2)), pltpu.SemaphoreType.DMA((BUCKETS, 2)), pltpu.SemaphoreType.DMA((6,)),
        pltpu.SemaphoreType.DMA((4,)), pltpu.SemaphoreType.DMA((4,)),
        pltpu.SemaphoreType.DMA((BUCKETS, 8 * LINE + 3)), pltpu.SemaphoreType.DMA((BUCKETS, 8 * LINE + 3)),
        pltpu.SemaphoreType.DMA((BUCKETS, 2)),
    ]
    return pl.pallas_call(
        partial(main_kernel, D, FF, S, grid),
        out_shape=out_shape,
        in_specs=[any_spec, any_spec, vm_spec, vm_spec] + [any_spec] * 6 + [vm_spec],
        out_specs=(any_spec,) * 4,
        scratch_shapes=scratch,
        compiler_params=pltpu.CompilerParams(collective_id=0, has_side_effects=True, vmem_limit_bytes=60 * 2**20),
        name="layer_pass",
    )(tok, cot, segk, segq, wq, wo, wu, wd, bq, bu, vec)


def shards(tokens, segment_ids, out_cotangent, w_qkv, qv_bias, w_out, w_up, up_bias, w_down, add_bias, norm_gain, norm_bias):
    c = lax.axis_index("tensor")
    D = tokens.shape[1]
    hd = D // 2
    S = segment_ids.shape[1]
    seqs = tokens.shape[0] // S
    seg = lax.dynamic_slice_in_dim(segment_ids, c * seqs, seqs, axis=0)
    vec = jnp.concatenate([add_bias[0], norm_gain[0], norm_bias[0], jnp.zeros((2, D), F32)], axis=0)
    qv = qv_bias[0].astype(F32)
    bq = jnp.concatenate([qv[0], jnp.zeros((hd,), F32), qv[1]])
    bq = jnp.broadcast_to(bq[None], (8, 3 * hd))
    bu = jnp.broadcast_to(up_bias.astype(F32), (8, up_bias.shape[1]))
    grid = lax.axis_size("dp") == 2 * LINE
    lo, ig, gall, gsm = main_call(
        tokens, out_cotangent, seg[:, :, None], seg[:, None, :],
        w_qkv[0].reshape(D, 3 * hd), w_out[0], w_up[0], w_down[0], bq, bu, vec, S, grid,
    )
    def own(v, size):
        return lax.dynamic_slice_in_dim(v, c * size, size, axis=-1)
    if not grid:
        gall, gsm = lax.psum(gall, "dp"), lax.psum(gsm, "dp")
    F = up_bias.shape[1]
    block = gall.astype(F32).reshape(BUCKETS, 2, hd, hd)
    gd = block[0:4].transpose(0, 2, 1, 3).reshape(F, D)
    gu = block[4:8].reshape(4, D, hd).transpose(1, 0, 2).reshape(D, F)
    gq = block[8:11].reshape(3, D, hd).transpose(1, 0, 2)
    go = block[11].transpose(1, 0, 2).reshape(hd, D)
    sq = own(gsm[0:3].reshape(-1), 3 * hd)
    gqv = jnp.concatenate([sq[:hd], sq[2 * hd :]])
    gub = own(gsm[3:7].reshape(-1), F)
    gsv = own(gsm[8:14], hd)
    return (
        lo[None], ig[None],
        gq.reshape(1, D, 3, hd), gqv.reshape(1, 2, hd), go[None], gu[None], gub[None], gd[None],
        gsv[None, 0:2], gsv[None, 2:4], gsv[None, 4:6],
    )


def solution(mesh):
    return jax.shard_map(
        shards,
        mesh=mesh,
        in_specs=(
            P(("dp", "tensor"), None), P("dp", None), P(("dp", "tensor"), None),
            P("section", None, None, "tensor"), P("section", None, "tensor"), P("section", "tensor", None),
            P("section", None, "tensor"), P("section", "tensor"), P("section", "tensor", None),
            P("section", None, None), P("section", None, None), P("section", None, None),
        ),
        out_specs=(
            P("section", ("dp", "tensor"), None), P("section", ("dp", "tensor"), None),
            P("section", None, None, "tensor"), P("section", None, "tensor"), P("section", "tensor", None),
            P("section", None, "tensor"), P("section", "tensor"), P("section", "tensor", None),
            P("section", None, "tensor"), P("section", None, "tensor"), P("section", None, "tensor"),
        ),
        check_vma=False,
    )
```

```python
from functools import partial

import jax
import jax.numpy as jnp
from jax import lax
from jax.experimental import pallas as pl
from jax.experimental.pallas import tpu as pltpu
from jax.sharding import PartitionSpec as P

HEAD_DIM = 64
norm_eps = 1e-12
masked_score = -1e30
LINE = 4
BUCKETS = 12
A_ROWS = 512
MESH = pl.DeviceIdType.MESH
F32 = jnp.float32
BF16 = jnp.bfloat16


def mm(a, b):
    return lax.dot_general(a, b, (((1,), (0,)), ((), ())), preferred_element_type=F32)


def mm_nt(a, b):
    return lax.dot_general(a, b, (((1,), (1,)), ((), ())), preferred_element_type=F32)


def mm_tn(a, b):
    return lax.dot_general(a, b, (((0,), (0,)), ((), ())), preferred_element_type=F32)


def ds(start, size, align=None):
    return pl.ds(pl.multiple_of(start, align or size), size)


def eights(v):
    return jnp.sum(v.reshape(v.shape[0] // 8, 8, v.shape[1]), axis=0)


def gelu_and_slope(g):
    size = jnp.abs(g)
    x = 1.0 + 0.2316419 * size
    t = pl.reciprocal(x, approx=True)
    t = t * (2.0 - x * t)
    density = 0.3989422804014327 * jnp.exp2(g * g * -0.7213475204444817)
    tail = ((((1.330274429 * t - 1.821255978) * t + 1.781477937) * t - 0.356563782) * t + 0.319381530) * t * density
    cdf = jnp.where(g > 0.0, 1.0 - tail, tail)
    return g * cdf, cdf + g * density


def row_mean(v):
    return jnp.sum(v, axis=-1, keepdims=True) * (1.0 / v.shape[-1])


class Line:
    def __init__(self, red, base, size, landing, sems):
        self.red, self.base, self.size, self.landing, self.sems = red, base, size, landing, sems

    def own(self, b, j):
        return ds(self.base(b) + j * self.size, self.size, 16)

    def slot(self, b, j):
        return ds((b * (LINE + 1) + j) * self.size, self.size, 16)

    def sum_up(self, b, j):
        r = self.red
        return r.remote(r.G.at[self.own(b, j)], self.landing.at[self.slot(b, j)], b, self.sems + j, r.above)

    def sum_down(self, b, j):
        r = self.red
        place = jnp.where(j == r.z - 1, LINE, j)
        return r.remote(r.G.at[self.own(b, j)], self.landing.at[self.slot(b, place)], b, self.sems + LINE + j, r.below)

    def from_above(self, b, j):
        r = self.red
        place = jnp.where(j == r.z, LINE, j)
        return r.remote(r.G.at[self.own(b, j)], self.landing.at[self.slot(b, place)], b, self.sems + LINE + j, r.below)

    def out_up(self, b, j, own=False):
        r = self.red
        return r.remote(r.place(own).at[self.own(b, j)], r.out.at[self.own(b, j)], b, self.sems + 2 * LINE + j, r.above)

    def out_down(self, b, j, own=False):
        r = self.red
        return r.remote(r.place(own).at[self.own(b, j)], r.out.at[self.own(b, j)], b, self.sems + 3 * LINE + j, r.below)

    def add(self, b, j, *places):
        G = self.red.G
        rows = self.own(b, j)
        total = G[rows, :].astype(F32)
        for place in places:
            total = total + self.landing[self.slot(b, place), :].astype(F32)
        G[rows, :] = total.astype(BF16)

    def begin(self, b):
        z = self.red.z

        @pl.when(z == 0)
        def _():
            for i in range(LINE - 1):
                self.sum_up(b, LINE - 1 - i).start()

        @pl.when(z == LINE - 1)
        def _():
            for i in range(LINE - 1):
                self.sum_down(b, i).start()

    def pass_on(self, b, i):
        z = self.red.z
        end = LINE - 1 - z
        up, down = LINE - 2 - i + z, 1 + i - end

        @pl.when((up > z) & (up < LINE) & (z > 0))
        def _():
            self.sum_up(b, up).wait_recv()
            self.add(b, up, up)
            self.sum_up(b, up).start()

        @pl.when((down < z) & (down >= 0) & (end > 0))
        def _():
            self.from_above(b, down).wait_recv()
            self.add(b, down, down)
            self.sum_down(b, down).start()

    def finish_own(self, b):
        z = self.red.z

        @pl.when(z > 0)
        def _():
            self.sum_up(b, z).wait_recv()

        @pl.when(z < LINE - 1)
        def _():
            self.from_above(b, z).wait_recv()

        @pl.when(z == 0)
        def _():
            self.add(b, 0, LINE)

        @pl.when(z == LINE - 1)
        def _():
            self.add(b, LINE - 1, LINE - 1)

        @pl.when((z > 0) & (z < LINE - 1))
        def _():
            self.add(b, z, z, LINE)

    def spread(self, b):
        z = self.red.z

        @pl.when(z < LINE - 1)
        def _():
            self.out_up(b, z, True).start()

        @pl.when(z > 0)
        def _():
            self.out_down(b, z, True).start()

        self.keep(b).start()

    def keep(self, b):
        r = self.red
        rows = self.own(b, r.z)
        return pltpu.make_async_copy(r.G.at[rows], r.out.at[rows], r.csem.at[b, self.sems // (4 * LINE)])

    def spread_on(self, b, i):
        z = self.red.z

        @pl.when(z - i >= 0)
        def _():
            self.out_up(b, z - i).wait_recv()

            @pl.when(z < LINE - 1)
            def _():
                self.out_up(b, z - i).start()

        @pl.when(z + i < LINE)
        def _():
            self.out_down(b, z + i).wait_recv()

            @pl.when(z > 0)
            def _():
                self.out_down(b, z + i).start()

    def drain(self, b):
        z = self.red.z
        for j in range(LINE):
            @pl.when(j > z)
            def _():
                self.sum_up(b, j).wait_send()

            @pl.when(j < z)
            def _():
                self.sum_down(b, j).wait_send()

            @pl.when((j <= z) & (z < LINE - 1))
            def _():
                self.out_up(b, j).wait_send()

            @pl.when((j >= z) & (z > 0))
            def _():
                self.out_down(b, j).wait_send()


class Reduction:
    stages = 9

    def __init__(self, D, s, d, c, G, out, LA1, LA, LB, LS, SM, SML, asend, arecv, ssend, srecv, csem):
        self.out, self.csem = out, csem
        self.G, self.LA1, self.LS, self.SM, self.SML = G, LA1, LS, SM, SML
        self.asend, self.arecv, self.ssend, self.srecv = asend, arecv, ssend, srecv
        self.z, self.y = d // 2, d % 2
        self.s, self.d, self.c = s, d, c
        self.above = (s, jnp.minimum(d + 2, 2 * LINE - 1), c)
        self.below = (s, jnp.maximum(d - 2, 0), c)
        self.beside = (s, d + 1 - 2 * self.y, c)
        self.half = A_ROWS // 2
        self.D = D
        self.a = Line(self, lambda b: b * D + self.y * self.half, self.half // LINE, LA, 0)
        self.b = Line(self, lambda b: b * D + A_ROWS, (D - A_ROWS) // LINE, LB, 4 * LINE)
        z = self.z
        pair = z + 1 - 2 * (z % 2)
        far = (z + 2) % 4
        self.small_peers = [None, self.beside, (s, pair * 2 + self.y, c), (s, far * 2 + self.y, c)]

    def place(self, own):
        return self.G if own else self.out

    def remote(self, src, dst, b, sem, to):
        return pltpu.make_async_remote_copy(src, dst, self.asend.at[b, sem], self.arecv.at[b, sem], device_id=to, device_id_type=MESH)

    def greet(self, barrier):
        def hello(to):
            pl.semaphore_signal(barrier, inc=1, device_id=to, device_id_type=MESH)
        for to in self.small_peers[1:]:
            hello(to)
        @pl.when((self.z == 1))
        def _():
            hello(self.above)

        @pl.when((self.z == 2))
        def _():
            hello(self.below)

    def greetings(self):
        return 3 + ((self.z == 1) | (self.z == 2)).astype(jnp.int32)

    def small_copy(self, k):
        return pltpu.make_async_remote_copy(self.SM, self.SML.at[k], self.ssend.at[k], self.srecv.at[k], device_id=self.small_peers[k], device_id_type=MESH)

    def small_start(self, k):
        self.small_copy(k).start()

    def small_finish(self, k):
        self.small_copy(k).wait()
        self.SM[...] += self.SML[k]

    def give_side(self, b):
        rows = ds(b * self.D + (1 - self.y) * self.half, self.half, 16)
        return self.remote(self.G.at[rows], self.LA1.at[ds(b * self.half, self.half, 16)], b, 8 * LINE, self.beside)

    def share_side(self, b):
        rows = ds(b * self.D + self.y * self.half, self.half, 16)
        return self.remote(self.out.at[rows], self.out.at[rows], b, 8 * LINE + 1, self.beside)

    def swap(self, b):
        size = self.b.size
        return self.remote(self.G.at[self.b.own(b, self.z)], self.LS.at[ds(b * size, size, 16)], b, 8 * LINE + 2, self.beside)

    def stage(self, k, b):
        A, B = self.a, self.b
        if k == 0:
            self.give_side(b).start()
            B.begin(b)
        elif k == 1:
            B.pass_on(b, 0)
            self.give_side(b).wait_recv()
            rows = ds(b * self.D + self.y * self.half, self.half, 16)
            land = ds(b * self.half, self.half, 16)
            self.G[rows, :] = (self.G[rows, :].astype(F32) + self.LA1[land, :].astype(F32)).astype(BF16)
            A.begin(b)
        elif k == 2:
            B.pass_on(b, 1)
            A.pass_on(b, 0)
        elif k == 3:
            B.finish_own(b)
            self.swap(b).start()
            A.pass_on(b, 1)
        elif k == 4:
            A.finish_own(b)
            A.spread(b)
            size = B.size
            self.swap(b).wait()
            rows, land = B.own(b, self.z), ds(b * size, size, 16)
            self.G[rows, :] = (self.G[rows, :].astype(F32) + self.LS[land, :].astype(F32)).astype(BF16)
            B.spread(b)
        elif k <= 7:
            A.spread_on(b, k - 4)
            B.spread_on(b, k - 4)
            if k == 7:
                A.keep(b).wait()
                self.share_side(b).start()
        else:
            self.share_side(b).wait_recv()

    def slot(self, tau):
        for k in range(self.stages - 1, -1, -1):
            b = tau - k

            @pl.when((b >= 0) & (b < BUCKETS))
            def _():
                self.stage(k, b)

    def drain(self):
        def one(b, _):
            self.a.drain(b)
            self.b.drain(b)
            self.give_side(b).wait_send()
            self.share_side(b).wait_send()
            self.b.keep(b).wait()
            return 0
        lax.fori_loop(0, BUCKETS, one, 0)


def main_kernel(
    D, FF, S, grid,
    tok, cot, seg, wq_in, qv_in, wo_in, wu_in, ub_in, wd_in, add_in, gain, shift,
    lo, ig, gall, gsm,
    wq, wo, wu, wd, bq, bu,
    X, QKV, O, N1, N2, Hr, U, GP, R, DST, dB, dA, dOs, dQKV,
    r1s, r2s, Hf, Zf, bias, dY, YB, IGB, IGF,
    sq, su, sv, SM, SML, G, LA1, LA, LB, LS,
    lsem, wsend, wrecv, rsend, rrecv, gsend, grecv, osem, ssend, srecv, asend, arecv, csem,
):
    s = lax.axis_index("section")
    d = lax.axis_index("dp")
    c = lax.axis_index("tensor")
    other = 1 - c
    core_peer = (s, d, other)
    x_peer = (1 - s, d, c)
    half_d, half_f, half_q = D // 2, FF // 2, 3 * D // 2
    pairs = D // 128
    lo_pairs = pairs // 2

    barrier = pltpu.get_barrier_semaphore()
    pl.semaphore_signal(barrier, inc=1, device_id=core_peer, device_id_type=MESH)
    pl.semaphore_signal(barrier, inc=1, device_id=x_peer, device_id_type=MESH)
    if grid:
        ring = Reduction(D, s, d, c, G, gall, LA1, LA, LB, LS, SM, SML, asend, arecv, ssend, srecv, csem)
        ring.greet(barrier)

    weights = [(wq_in.at[j], wq.at[:, ds(c * half_q + j * half_d, half_d)]) for j in range(3)] + [
        (wo_in, wo.at[ds(c * half_d, half_d), :]),
        (wu_in, wu.at[:, ds(c * half_f, half_f, 128)]),
        (wd_in, wd.at[ds(c * half_f, half_f), :]),
    ]
    biases = [bq.at[:, ds(c * half_q, half_q, 128)], bu.at[:, ds(c * half_f, half_f, 128)]]
    local = [pltpu.make_async_copy(src, dst, lsem.at[i]) for i, (src, dst) in enumerate(weights)]
    remote = [
        pltpu.make_async_remote_copy(src, dst, wsend.at[i], wrecv.at[i], device_id=core_peer, device_id_type=MESH)
        for i, (src, dst) in enumerate(weights + [(b, b) for b in biases])
    ]
    tok_copy = pltpu.make_async_copy(tok, X, lsem.at[6])
    cot_copy = pltpu.make_async_copy(cot, dY, lsem.at[7])

    @pl.when(s == 0)
    def _():
        tok_copy.start()

    @pl.when(s == 1)
    def _():
        cot_copy.start()

    for copy in local:
        copy.start()
    bq[:, ds(c * half_q, half_d)] = jnp.broadcast_to(qv_in[0:1, :].astype(F32), (8, half_d))
    bq[:, ds(c * half_q + half_d, half_d)] = jnp.zeros((8, half_d), F32)
    bq[:, ds(c * half_q + 2 * half_d, half_d)] = jnp.broadcast_to(qv_in[1:2, :].astype(F32), (8, half_d))
    bu[:, ds(c * half_f, half_f)] = jnp.broadcast_to(ub_in[...].astype(F32), (8, half_f))
    pl.semaphore_wait(barrier, 2 + ring.greetings() if grid else 2)
    for i in (0, 1, 2, 6, 7):
        remote[i].start()

    for q in range(2):
        row = jnp.broadcast_to(seg[pl.ds(2 * c + q, 1), :].astype(F32), (S, S))
        bias[q] = jnp.where(row.T == row, 0.0, masked_score)
    sq[...] = jnp.zeros_like(sq)
    su[...] = jnp.zeros_like(su)
    sv[...] = jnp.zeros_like(sv)
    lane = lax.broadcasted_iota(jnp.int32, (1, 128), 1)
    first_scaled = jnp.where(lane < HEAD_DIM, 0.125, 0.0).astype(BF16)
    second_scaled = jnp.where(lane < HEAD_DIM, 0.0, 0.125).astype(BF16)
    first_half = jnp.where(lane < HEAD_DIM, 1.0, 0.0).astype(BF16)
    second_half = jnp.where(lane < HEAD_DIM, 0.0, 1.0).astype(BF16)

    def need(*which):
        for i in which:
            if i < 6:
                local[i].wait()
            remote[i].wait_recv()

    def relay(m):
        rows = ds(m * S, S)
        return pltpu.make_async_remote_copy(YB.at[rows], X.at[rows], rsend.at[m], rrecv.at[m], device_id=x_peer, device_id_type=MESH)

    def relay_back(m):
        rows = ds(m * S, S)
        return pltpu.make_async_remote_copy(IGB.at[rows], dY.at[rows], rsend.at[m], rrecv.at[m], device_id=x_peer, device_id_type=MESH)

    def pair_columns(p):
        base = (p // lo_pairs) * half_q + (p % lo_pairs) * 128
        return ds(base, 128), ds(base + half_d, 128), ds(base + 2 * half_d, 128)

    def normed(m, which, N, rs, finish):
        def norm_rows(j, _):
            near, rows = ds(j * 32, 32), ds(m * S + j * 32, 32)
            z = Zf[near, :]
            centered = z - row_mean(z)
            scaled = lax.rsqrt(row_mean(centered * centered) + norm_eps)
            n = centered * scaled
            N[rows, :] = n.astype(BF16)
            rs[rows, :] = jnp.broadcast_to(scaled, (32, 128))
            finish(near, rows, n * gain[which : which + 1, :] + shift[which : which + 1, :])
            return 0

        lax.fori_loop(0, S // 32, norm_rows, 0, unroll=4)

    def forward(t, m):
        rows = ds(m * S, S)

        @pl.when(t == 0)
        def _():
            @pl.when(s == 0)
            def _():
                tok_copy.wait()
            need(0, 1, 2, 6, 7)
            remote[3].start()
            remote[4].start()

        @pl.when(s == 1)
        def _():
            relay(m).wait_recv()

        def qkv_tile(i, _):
            cols = ds(i * 256, 256)
            QKV[rows, cols] = (mm(X[rows, :], wq[:, cols]) + bq[0:1, cols]).astype(BF16)
            return 0

        lax.fori_loop(0, 3 * D // 256, qkv_tile, 0, unroll=3)

        def attend(p, _):
            qc, kc, vc = pair_columns(p)
            q2, k2, v2 = QKV[rows, qc], QKV[rows, kc], QKV[rows, vc]
            vt = v2.T
            weights = ds((m * pairs + p) * S, S)
            outs = []
            for h, mask in enumerate((first_scaled, second_scaled)):
                kh = k2 * mask
                for part in range(0, S, 128):
                    st = mm_nt(kh, q2[part : part + 128, :]) + bias[m, :, part : part + 128]
                    e = jnp.exp(st - jnp.max(st, axis=0, keepdims=True))
                    R[weights, h * S + part : h * S + part + 128] = (e * (1.0 / jnp.sum(e, axis=0, keepdims=True))).astype(BF16)
                outs.append(mm(vt[h * HEAD_DIM : (h + 1) * HEAD_DIM], R[weights, h * S : (h + 1) * S]))
            O[rows, ds(p * 128, 128)] = jnp.concatenate(outs, axis=0).T.astype(BF16)
            return 0

        lax.fori_loop(0, pairs, attend, 0, unroll=2)

        @pl.when(t == 0)
        def _():
            need(3)
            remote[5].start()

        def out_tile(i, _):
            cols = ds(i * 256, 256)
            Zf[:, cols] = mm(O[rows, :], wo[:, cols]) + X[rows, cols].astype(F32) + add_in[0:1, cols]
            return 0

        lax.fori_loop(0, D // 256, out_tile, 0, unroll=3)

        def first_done(near, rows, h):
            Hf[near, :] = h
            Hr[rows, :] = h.astype(BF16)

        normed(m, 0, N1, r1s, first_done)

        @pl.when(t == 0)
        def _():
            need(4)

        def up_tile(i, _):
            cols = ds(i * 256, 256)
            u, slope = gelu_and_slope(mm(Hr[rows, :], wu[:, cols]) + bu[0:1, cols])
            U[rows, cols] = u.astype(BF16)
            GP[rows, cols] = slope.astype(BF16)
            return 0

        lax.fori_loop(0, FF // 256, up_tile, 0, unroll=4)

        @pl.when(t == 0)
        def _():
            need(5)

        def down_tile(i, _):
            cols = ds(i * 256, 256)
            Zf[:, cols] = mm(U[rows, :], wd[:, cols]) + Hf[:, cols] + add_in[1:2, cols]
            return 0

        lax.fori_loop(0, D // 256, down_tile, 0, unroll=3)

        def second_done(near, rows, y):
            YB[rows, :] = y.astype(BF16)

        normed(m, 1, N2, r2s, second_done)
        pltpu.make_async_copy(YB.at[rows], lo.at[rows], osem.at[m]).start()

        @pl.when(s == 0)
        def _():
            relay(m).start()

    def norm_back(m, which, get, N, rs, low):
        def back_rows(j, sums):
            near, rows = ds(j * 32, 32), ds(m * S + j * 32, 32)
            dy, n = get(near, rows), N[rows, :].astype(F32)
            e = dy * gain[which : which + 1, :]
            dz = rs[rows, 0:1] * (e - row_mean(e) - n * row_mean(e * n))
            Zf[near, :] = dz
            low[rows, :] = dz.astype(BF16)
            return sums[0] + eights(dz), sums[1] + eights(dy * n), sums[2] + eights(dy)

        sums = lax.fori_loop(0, S // 32, back_rows, (jnp.zeros((8, D), F32),) * 3, unroll=2)
        for i in range(3):
            sv[2 * i + which] += sums[i]

    def backward(t, m, last):
        rows = ds(m * S, S)

        @pl.when(s == 0)
        def _():
            relay_back(m).wait_recv()

        @pl.when((s == 1) & (m == 0))
        def _():
            cot_copy.wait()

        norm_back(m, 1, lambda near, rows: dY[rows, :].astype(F32), N2, r2s, dB)

        def down_back(i, _):
            cols = ds(i * 256, 256)
            dg = mm_nt(dB[rows, :], wd[cols, :]) * GP[rows, cols].astype(F32)
            su[:, cols] += eights(dg)
            GP[rows, cols] = dg.astype(BF16)
            return 0

        lax.fori_loop(0, FF // 256, down_back, 0, unroll=4)
        last(0)

        def up_back(i, _):
            cols = ds(i * 256, 256)
            Hf[:, cols] = mm_nt(GP[rows, :], wu[cols, :]) + Zf[:, cols]
            return 0

        lax.fori_loop(0, D // 256, up_back, 0, unroll=3)
        norm_back(m, 0, lambda near, rows: Hf[near, :], N1, r1s, dA)
        last(1)

        def out_back(i, _):
            cols = ds(i * 256, 256)
            dOs[:, cols] = mm_nt(dA[rows, :], wo[cols, :]).astype(BF16)
            return 0

        lax.fori_loop(0, D // 256, out_back, 0, unroll=3)
        last(2)

        def attend_back(p, _):
            qc, kc, vc = pair_columns(p)
            q2, k2, v2 = QKV[rows, qc], QKV[rows, kc], QKV[rows, vc]
            do2 = dOs[:, ds(p * 128, 128)]
            kt = k2.T
            weights = ds((m * pairs + p) * S, S)
            turn = p % 2
            for h, half in enumerate((first_half, second_half)):
                vh = v2 * half
                for part in range(0, S, 128):
                    cols = slice(h * S + part, h * S + part + 128)
                    drt = mm_nt(vh, do2[part : part + 128, :])
                    rf = R[weights, cols].astype(F32)
                    DST[turn, :, cols] = (rf * (drt - jnp.sum(rf * drt, axis=0, keepdims=True))).astype(BF16)
            dst = DST[turn]
            dk = mm(dst, jnp.concatenate([q2 * first_scaled, q2 * second_scaled], axis=0))
            dv = mm(R[weights, :], jnp.concatenate([do2 * first_half, do2 * second_half], axis=0))
            dqt = [mm(kt[h * HEAD_DIM : (h + 1) * HEAD_DIM], dst[:, h * S : (h + 1) * S]) for h in range(2)]
            dq = (jnp.concatenate(dqt, axis=0) * 0.125).T.astype(BF16)
            dvb = dv.astype(BF16)
            dQKV[rows, qc] = dq
            dQKV[rows, kc] = dk.astype(BF16)
            dQKV[rows, vc] = dvb
            sq[:, qc] += eights(dq.astype(F32))
            sq[:, vc] += eights(dvb.astype(F32))
            return 0

        lax.fori_loop(0, pairs, attend_back, 0, unroll=2)
        last(3)

        def in_back(i, _):
            cols = ds(i * 256, 256)
            dx = mm_nt(dQKV[rows, :], wq[cols, :]) + Zf[:, cols]
            IGF[rows, cols] = dx
            IGB[rows, cols] = dx.astype(BF16)
            return 0

        lax.fori_loop(0, D // 256, in_back, 0, unroll=3)
        pltpu.make_async_copy(IGF.at[rows], ig.at[rows], osem.at[2 + m]).start()

        @pl.when(s == 1)
        def _():
            relay_back(m).start()

    W = D // 2

    def across(i, start, size, right):
        return mm(R[ds(i * D + start, size, 128), :], right)

    def grad_tiles(k, kind, i):
        if kind == "down":
            left = U[:, ds(k * half_f + i * W, W, 128)].T
            return [mm(left, dB[:, q * W : (q + 1) * W]) for q in range(2)]
        if kind == "out":
            return [across(1, k * half_d, W, dA[:, q * W : (q + 1) * W]) for q in range(2)]
        cols = ds(k * (half_f if kind == "up" else half_q) + i * W, W, 128)
        which, right = (0, GP) if kind == "up" else (2, dQKV)
        return [across(which, q * W, W, right[:, cols]) for q in range(2)]

    first = {"down": 0, "up": 4, "qkv": 8, "out": 11}

    def halves(k, kind, i):
        if kind == "down":
            return [wd.at[ds(k * half_f + i * W, W), q * W : (q + 1) * W] for q in range(2)]
        if kind == "out":
            return [wo.at[ds(k * half_d, W), q * W : (q + 1) * W] for q in range(2)]
        cols = ds(k * (half_f if kind == "up" else half_q) + i * W, W, 128)
        ref = wu if kind == "up" else wq
        return [ref.at[q * W : (q + 1) * W, cols] for q in range(2)]

    def exchange(kind, i):
        b = first[kind] + i
        return [
            pltpu.make_async_remote_copy(part, G.at[ds(b * D + q * W, W)], gsend.at[b, q], grecv.at[b, q], device_id=core_peer, device_id_type=MESH)
            for q, part in enumerate(halves(other, kind, i))
        ]

    def give(kind, i):
        tiles = grad_tiles(other, kind, i)
        for q, copy in enumerate(exchange(kind, i)):
            halves(other, kind, i)[q][...] = tiles[q].astype(BF16)
            copy.start()

    def keep(kind, i):
        tiles = grad_tiles(c, kind, i)
        b = first[kind] + i
        for q, copy in enumerate(exchange(kind, i)):
            copy.wait_recv()
            rows = ds(b * D + q * W, W)
            G[rows, :] = (tiles[q] + G[rows, :].astype(F32)).astype(BF16)

    def slot(tau):
        if grid:
            ring.slot(tau)

    def give_all_down():
        def give_down(i, _):
            give("down", i)
            return 0

        lax.fori_loop(0, 4, give_down, 0)

    def step(t, _):
        back = jnp.where(s == 0, t // 2, t % 2)
        m = jnp.where(s == 0, t % 2, t // 2)

        def last(i):
            @pl.when((s == 0) & (m == 1))
            def _():
                if i == 0:
                    give_all_down()
                keep("down", i)
                slot(i)

        @pl.when(back == 0)
        def _():
            forward(t, m)

        @pl.when(back == 1)
        def _():
            backward(t, m, last)

        return 0

    lax.fori_loop(0, 4, step, 0)

    @pl.when(s == 1)
    def _():
        give_all_down()

        def keep_down(i, _):
            keep("down", i)
            slot(i)
            return 0

        lax.fori_loop(0, 4, keep_down, 0)

    for i, whole in enumerate((Hr, O, X)):
        R[i * D : (i + 1) * D, :] = whole[...].T

    def give_up(i, _):
        give("up", i)
        return 0

    lax.fori_loop(0, 4, give_up, 0)

    def total(v):
        return jnp.sum(v, axis=0, keepdims=True)

    for i in range(3):
        SM[i : i + 1, :] = total(sq[:, i * D : (i + 1) * D])
    for i in range(4):
        SM[3 + i : 4 + i, :] = total(su[:, i * D : (i + 1) * D])
    SM[7:8, :] = jnp.zeros((1, D), F32)
    for i in range(6):
        SM[8 + i : 9 + i, :] = total(sv[i])
    SM[14:16, :] = jnp.zeros((2, D), F32)
    small_core = pltpu.make_async_remote_copy(SM, SML.at[0], ssend.at[0], srecv.at[0], device_id=core_peer, device_id_type=MESH)
    small_core.start()

    def keep_up(i, _):
        keep("up", i)
        slot(4 + i)

        @pl.when(i < 3)
        def _():
            give("qkv", i)

        @pl.when(i == 3)
        def _():
            give("out", 0)

        return 0

    lax.fori_loop(0, 4, keep_up, 0)
    small_core.wait()
    SM[...] += SML[0]
    if grid:
        ring.small_start(1)

    def keep_rest(i, _):
        @pl.when(i < 3)
        def _():
            keep("qkv", i)

        @pl.when(i == 3)
        def _():
            keep("out", 0)

        slot(8 + i)
        return 0

    lax.fori_loop(0, 4, keep_rest, 0)
    if grid:
        def last_slot(tau, _):
            slot(tau)
            return 0

        ring.small_finish(1)
        ring.small_start(2)
        lax.fori_loop(12, 14, last_slot, 0)
        ring.small_finish(2)
        ring.small_start(3)
        lax.fori_loop(14, BUCKETS + ring.stages - 1, last_slot, 0)
        ring.small_finish(3)
        ring.drain()
    else:
        result = pltpu.make_async_copy(G, gall, osem.at[4])
        result.start()
        result.wait()
    small_result = pltpu.make_async_copy(SM, gsm, osem.at[5])
    small_result.start()
    for kind, n in (("down", 4), ("up", 4), ("qkv", 3), ("out", 1)):
        for i in range(n):
            for copy in exchange(kind, i):
                copy.wait_send()
    small_result.wait()
    for copy in remote:
        copy.wait_send()
    for m in range(2):
        rows = ds(m * S, S)
        pltpu.make_async_copy(YB.at[rows], lo.at[rows], osem.at[m]).wait()
        pltpu.make_async_copy(IGF.at[rows], ig.at[rows], osem.at[2 + m]).wait()

    @pl.when(s == 0)
    def _():
        for m in range(2):
            relay(m).wait_send()

    @pl.when(s == 1)
    def _():
        for m in range(2):
            relay_back(m).wait_send()


def main_call(grid, S, tok, cot, seg, wq, qv, wo, wu, ub, wd, add, gain, shift):
    rows, D = tok.shape
    FF = 2 * wu.shape[1]
    hd, hq = D // 2, 3 * D // 2
    any_spec = pl.BlockSpec(memory_space=pl.ANY)
    vm_spec = pl.BlockSpec(memory_space=pltpu.VMEM)
    sds = jax.ShapeDtypeStruct
    V, DMA = pltpu.VMEM, pltpu.SemaphoreType.DMA
    line_a, line_b = A_ROWS // 2 // LINE, (D - A_ROWS) // LINE
    scratch = [
        V((D, 2 * hq), BF16), V((D, D), BF16), V((D, FF), BF16), V((FF, D), BF16), V((8, 2 * hq), F32), V((8, FF), F32),
        V((rows, D), BF16), V((rows, 3 * D), BF16), V((rows, D), BF16), V((rows, D), BF16), V((rows, D), BF16), V((rows, D), BF16),
        V((rows, FF), BF16), V((rows, FF), BF16), V((2 * (D // 128) * S, 2 * S), BF16), V((2, S, 2 * S), BF16),
        V((rows, D), BF16), V((rows, D), BF16), V((S, D), BF16), V((rows, 3 * D), BF16),
        V((rows, 128), F32), V((rows, 128), F32), V((S, D), F32), V((S, D), F32), V((2, S, S), F32),
        V((rows, D), BF16), V((rows, D), BF16), V((rows, D), BF16), V((rows, D), F32),
        V((8, 2 * hq), F32), V((8, FF), F32), V((6, 8, D), F32), V((16, D), F32), V((4, 16, D), F32),
        V((BUCKETS * D, hd), BF16), V((BUCKETS * A_ROWS // 2, hd), BF16), V((BUCKETS * line_a * (LINE + 1), hd), BF16),
        V((BUCKETS * line_b * (LINE + 1), hd), BF16), V((BUCKETS * line_b, hd), BF16),
        DMA((8,)), DMA((8,)), DMA((8,)), DMA((2,)), DMA((2,)),
        DMA((BUCKETS, 2)), DMA((BUCKETS, 2)), DMA((6,)), DMA((4,)), DMA((4,)),
        DMA((BUCKETS, 8 * LINE + 3)), DMA((BUCKETS, 8 * LINE + 3)), DMA((BUCKETS, 2)),
    ]
    return pl.pallas_call(
        partial(main_kernel, D, FF, S, grid),
        out_shape=(sds((rows, D), BF16), sds((rows, D), F32), sds((BUCKETS * D, hd), BF16), sds((16, D), F32)),
        in_specs=[any_spec, any_spec, vm_spec, any_spec, vm_spec, any_spec, any_spec, vm_spec, any_spec, vm_spec, vm_spec, vm_spec],
        out_specs=(any_spec,) * 4,
        scratch_shapes=scratch,
        compiler_params=pltpu.CompilerParams(collective_id=0, has_side_effects=True, vmem_limit_bytes=60 * 2**20),
        name="layer_pass",
    )(tok, cot, seg, wq, qv, wo, wu, ub, wd, add, gain, shift)


def unpack_kernel(D, block, sums, gq, gqv, go, gu, gub, gd, ga, gg, gs):
    b = pl.program_id(0)
    c = lax.axis_index("tensor")
    W = D // 2

    @pl.when(b < 4)
    def _():
        for q in range(2):
            gd[:, q * W : (q + 1) * W] = block[q * W : (q + 1) * W, :].astype(F32)

    @pl.when((b >= 4) & (b < 8))
    def _():
        gu[...] = block[...].astype(F32)

    @pl.when((b >= 8) & (b < 11))
    def _():
        gq[0] = block[...].astype(F32)

    @pl.when(b == 11)
    def _():
        for q in range(2):
            go[:, q * W : (q + 1) * W] = block[q * W : (q + 1) * W, :].astype(F32)
        own = ds(c * W, W)
        gqv[0:1, :] = sums[pl.ds(c, 1), own]
        gqv[1:2, :] = sums[pl.ds(1 + c, 1), own]
        for i in range(2):
            gub[:, i * D : (i + 1) * D] = sums[pl.ds(3 + 2 * c + i, 1), :]
            ga[i : i + 1, :] = sums[8 + i : 9 + i, own]
            gg[i : i + 1, :] = sums[10 + i : 11 + i, own]
            gs[i : i + 1, :] = sums[12 + i : 13 + i, own]


def unpack_call(gall, gsm, D, FF):
    W, F = D // 2, FF // 2
    sds = jax.ShapeDtypeStruct

    def whole(*shape):
        return pl.BlockSpec(shape, lambda b: (0,) * len(shape))

    return pl.pallas_call(
        partial(unpack_kernel, D),
        grid=(BUCKETS,),
        in_specs=[pl.BlockSpec((D, W), lambda b: (b, 0)), whole(16, D)],
        out_specs=(
            pl.BlockSpec((1, D, W), lambda b: (jnp.clip(b - 8, 0, 2), 0, 0)), whole(2, W), whole(W, D),
            pl.BlockSpec((D, W), lambda b: (0, jnp.clip(b - 4, 0, 3))), whole(1, F),
            pl.BlockSpec((W, D), lambda b: (jnp.minimum(b, 3), 0)), whole(2, W), whole(2, W), whole(2, W),
        ),
        out_shape=(
            sds((3, D, W), F32), sds((2, W), F32), sds((W, D), F32), sds((D, F), F32), sds((1, F), F32),
            sds((F, D), F32), sds((2, W), F32), sds((2, W), F32), sds((2, W), F32),
        ),
        compiler_params=pltpu.CompilerParams(vmem_limit_bytes=48 * 2**20),
        name="unpack",
    )(gall, gsm)


def shards(tokens, segment_ids, out_cotangent, w_qkv, qv_bias, w_out, w_up, up_bias, w_down, add_bias, norm_gain, norm_bias):
    D = tokens.shape[1]
    FF = 2 * w_up.shape[2]
    S = segment_ids.shape[1]
    grid = lax.axis_size("dp") == 2 * LINE
    lo, ig, gall, gsm = main_call(
        grid, S, tokens, out_cotangent, segment_ids, w_qkv[0].transpose(1, 0, 2), qv_bias[0],
        w_out[0], w_up[0], up_bias, w_down[0], add_bias[0], norm_gain[0], norm_bias[0],
    )
    if not grid:
        gall, gsm = lax.psum(gall, "dp"), lax.psum(gsm, "dp")
    gq, gqv, go, gu, gub, gd, ga, gg, gs = unpack_call(gall, gsm, D, FF)
    return (
        lo[None], ig[None], gq.transpose(1, 0, 2)[None], gqv[None], go[None], gu[None], gub, gd[None],
        ga[None], gg[None], gs[None],
    )


def solution(mesh):
    return jax.shard_map(
        shards,
        mesh=mesh,
        in_specs=(
            P(("dp", "tensor"), None), P("dp", None), P(("dp", "tensor"), None),
            P("section", None, None, "tensor"), P("section", None, "tensor"), P("section", "tensor", None),
            P("section", None, "tensor"), P("section", "tensor"), P("section", "tensor", None),
            P("section", None, None), P("section", None, None), P("section", None, None),
        ),
        out_specs=(
            P("section", ("dp", "tensor"), None), P("section", ("dp", "tensor"), None),
            P("section", None, None, "tensor"), P("section", None, "tensor"), P("section", "tensor", None),
            P("section", None, "tensor"), P("section", "tensor"), P("section", "tensor", None),
            P("section", None, "tensor"), P("section", None, "tensor"), P("section", None, "tensor"),
        ),
        check_vma=False,
    )
```

```python
from functools import partial

import jax
import jax.numpy as jnp
from jax import lax
from jax.experimental import pallas as pl
from jax.experimental.pallas import tpu as pltpu
from jax.sharding import PartitionSpec as P

HEAD_DIM = 64
norm_eps = 1e-12
masked_score = -1e30
LINE = 4
BUCKETS = 12
A_ROWS = (512,)
MOST_A, MOST_B = 512, 256
MESH = pl.DeviceIdType.MESH
F32 = jnp.float32
BF16 = jnp.bfloat16


def mm(a, b):
    return lax.dot_general(a, b, (((1,), (0,)), ((), ())), preferred_element_type=F32)


def mm_nt(a, b):
    return lax.dot_general(a, b, (((1,), (1,)), ((), ())), preferred_element_type=F32)


def mm_tn(a, b):
    return lax.dot_general(a, b, (((0,), (0,)), ((), ())), preferred_element_type=F32)


def ds(start, size, align=None):
    return pl.ds(pl.multiple_of(start, align or size), size)


def eights(v):
    return jnp.sum(v.reshape(v.shape[0] // 8, 8, v.shape[1]), axis=0)


def gelu_and_slope(g):
    size = jnp.abs(g)
    x = 1.0 + 0.2316419 * size
    t = pl.reciprocal(x, approx=True)
    t = t * (2.0 - x * t)
    density = 0.3989422804014327 * jnp.exp2(g * g * -0.7213475204444817)
    tail = ((((1.330274429 * t - 1.821255978) * t + 1.781477937) * t - 0.356563782) * t + 0.319381530) * t * density
    cdf = jnp.where(g > 0.0, 1.0 - tail, tail)
    return g * cdf, cdf + g * density


def row_mean(v):
    return jnp.sum(v, axis=-1, keepdims=True) * (1.0 / v.shape[-1])


class Line:
    def __init__(self, red, base, size, most, landing, sems):
        self.red, self.base, self.size, self.most, self.landing, self.sems = red, base, size, most, landing, sems

    def own(self, b, j):
        return ds(self.base(b) + j * self.size, self.size, 16)

    def slot(self, b, j):
        return ds(b * (LINE + 1) * self.most + j * self.size, self.size, 16)

    def sum_up(self, b, j):
        r = self.red
        return r.remote(r.G.at[self.own(b, j)], self.landing.at[self.slot(b, j)], b, self.sems + j, r.above)

    def sum_down(self, b, j):
        r = self.red
        place = jnp.where(j == r.z - 1, LINE, j)
        return r.remote(r.G.at[self.own(b, j)], self.landing.at[self.slot(b, place)], b, self.sems + LINE + j, r.below)

    def from_above(self, b, j):
        r = self.red
        place = jnp.where(j == r.z, LINE, j)
        return r.remote(r.G.at[self.own(b, j)], self.landing.at[self.slot(b, place)], b, self.sems + LINE + j, r.below)

    def out_up(self, b, j, own=False):
        r = self.red
        return r.remote(r.place(own).at[self.own(b, j)], r.out.at[self.own(b, j)], b, self.sems + 2 * LINE + j, r.above)

    def out_down(self, b, j, own=False):
        r = self.red
        return r.remote(r.place(own).at[self.own(b, j)], r.out.at[self.own(b, j)], b, self.sems + 3 * LINE + j, r.below)

    def add(self, b, j, *places):
        G = self.red.G
        rows = self.own(b, j)
        total = G[rows, :].astype(F32)
        for place in places:
            total = total + self.landing[self.slot(b, place), :].astype(F32)
        G[rows, :] = total.astype(BF16)

    def begin(self, b):
        z = self.red.z

        @pl.when(z == 0)
        def _():
            for i in range(LINE - 1):
                self.sum_up(b, LINE - 1 - i).start()

        @pl.when(z == LINE - 1)
        def _():
            for i in range(LINE - 1):
                self.sum_down(b, i).start()

    def pass_on(self, b, i):
        z = self.red.z
        end = LINE - 1 - z
        up, down = LINE - 2 - i + z, 1 + i - end

        @pl.when((up > z) & (up < LINE) & (z > 0))
        def _():
            self.sum_up(b, up).wait_recv()
            self.add(b, up, up)
            self.sum_up(b, up).start()

        @pl.when((down < z) & (down >= 0) & (end > 0))
        def _():
            self.from_above(b, down).wait_recv()
            self.add(b, down, down)
            self.sum_down(b, down).start()

    def finish_own(self, b):
        z = self.red.z

        @pl.when(z > 0)
        def _():
            self.sum_up(b, z).wait_recv()

        @pl.when(z < LINE - 1)
        def _():
            self.from_above(b, z).wait_recv()

        @pl.when(z == 0)
        def _():
            self.add(b, 0, LINE)

        @pl.when(z == LINE - 1)
        def _():
            self.add(b, LINE - 1, LINE - 1)

        @pl.when((z > 0) & (z < LINE - 1))
        def _():
            self.add(b, z, z, LINE)

    def spread(self, b):
        z = self.red.z

        @pl.when(z < LINE - 1)
        def _():
            self.out_up(b, z, True).start()

        @pl.when(z > 0)
        def _():
            self.out_down(b, z, True).start()

        self.keep(b).start()

    def keep(self, b):
        r = self.red
        rows = self.own(b, r.z)
        return pltpu.make_async_copy(r.G.at[rows], r.out.at[rows], r.csem.at[b, self.sems // (4 * LINE)])

    def spread_on(self, b, i):
        z = self.red.z

        @pl.when(z - i >= 0)
        def _():
            self.out_up(b, z - i).wait_recv()

            @pl.when(z < LINE - 1)
            def _():
                self.out_up(b, z - i).start()

        @pl.when(z + i < LINE)
        def _():
            self.out_down(b, z + i).wait_recv()

            @pl.when(z > 0)
            def _():
                self.out_down(b, z + i).start()

    def drain(self, b):
        z = self.red.z
        for j in range(LINE):
            @pl.when(j > z)
            def _():
                self.sum_up(b, j).wait_send()

            @pl.when(j < z)
            def _():
                self.sum_down(b, j).wait_send()

            @pl.when((j <= z) & (z < LINE - 1))
            def _():
                self.out_up(b, j).wait_send()

            @pl.when((j >= z) & (z > 0))
            def _():
                self.out_down(b, j).wait_send()


class Reduction:
    stages = 9

    def __init__(self, D, s, d, c, G, out, LA1, LA, LB, LS, SM, SML, asend, arecv, ssend, srecv, csem):
        self.out, self.csem = out, csem
        self.G, self.LA1, self.LS, self.SM, self.SML = G, LA1, LS, SM, SML
        self.asend, self.arecv, self.ssend, self.srecv = asend, arecv, ssend, srecv
        self.z, self.y = d // 2, d % 2
        self.s, self.d, self.c = s, d, c
        self.above = (s, jnp.minimum(d + 2, 2 * LINE - 1), c)
        self.below = (s, jnp.maximum(d - 2, 0), c)
        self.beside = (s, d + 1 - 2 * self.y, c)
        self.D = D
        self.kinds = []
        for a_rows in A_ROWS:
            half = a_rows // 2
            base = partial(lambda half, b: b * D + self.y * half, half)
            a = Line(self, base, half // LINE, MOST_A // 2 // LINE, LA, 0)
            base = partial(lambda a_rows, b: b * D + a_rows, a_rows)
            self.kinds.append((half, a, Line(self, base, (D - a_rows) // LINE, MOST_B // LINE, LB, 4 * LINE)))
        z = self.z
        pair = z + 1 - 2 * (z % 2)
        far = (z + 2) % 4
        self.small_peers = [None, self.beside, (s, pair * 2 + self.y, c), (s, far * 2 + self.y, c)]

    def place(self, own):
        return self.G if own else self.out

    def remote(self, src, dst, b, sem, to):
        return pltpu.make_async_remote_copy(src, dst, self.asend.at[b, sem], self.arecv.at[b, sem], device_id=to, device_id_type=MESH)

    def greet(self, barrier):
        def hello(to):
            pl.semaphore_signal(barrier, inc=1, device_id=to, device_id_type=MESH)
        for to in self.small_peers[1:]:
            hello(to)
        @pl.when((self.z == 1))
        def _():
            hello(self.above)

        @pl.when((self.z == 2))
        def _():
            hello(self.below)

    def greetings(self):
        return 3 + ((self.z == 1) | (self.z == 2)).astype(jnp.int32)

    def small_copy(self, k):
        return pltpu.make_async_remote_copy(self.SM, self.SML.at[k], self.ssend.at[k], self.srecv.at[k], device_id=self.small_peers[k], device_id_type=MESH)

    def small_start(self, k):
        self.small_copy(k).start()

    def small_finish(self, k):
        self.small_copy(k).wait()
        self.SM[...] += self.SML[k]

    def give_side(self, b, half):
        rows = ds(b * self.D + (1 - self.y) * half, half, 16)
        return self.remote(self.G.at[rows], self.LA1.at[ds(b * (MOST_A // 2), half, 16)], b, 8 * LINE, self.beside)

    def share_side(self, b, half):
        rows = ds(b * self.D + self.y * half, half, 16)
        return self.remote(self.out.at[rows], self.out.at[rows], b, 8 * LINE + 1, self.beside)

    def swap(self, b, B):
        return self.remote(self.G.at[B.own(b, self.z)], self.LS.at[ds(b * B.most, B.size, 16)], b, 8 * LINE + 2, self.beside)

    def stage(self, k, b, kind):
        half, A, B = kind
        if k == 0:
            self.give_side(b, half).start()
            B.begin(b)
        elif k == 1:
            B.pass_on(b, 0)
            self.give_side(b, half).wait_recv()
            rows = ds(b * self.D + self.y * half, half, 16)
            land = ds(b * (MOST_A // 2), half, 16)
            self.G[rows, :] = (self.G[rows, :].astype(F32) + self.LA1[land, :].astype(F32)).astype(BF16)
            A.begin(b)
        elif k == 2:
            B.pass_on(b, 1)
            A.pass_on(b, 0)
        elif k == 3:
            B.finish_own(b)
            self.swap(b, B).start()
            A.pass_on(b, 1)
        elif k == 4:
            A.finish_own(b)
            A.spread(b)
            self.swap(b, B).wait()
            rows, land = B.own(b, self.z), ds(b * B.most, B.size, 16)
            self.G[rows, :] = (self.G[rows, :].astype(F32) + self.LS[land, :].astype(F32)).astype(BF16)
            B.spread(b)
        elif k <= 7:
            A.spread_on(b, k - 4)
            B.spread_on(b, k - 4)
            if k == 7:
                A.keep(b).wait()
                self.share_side(b, half).start()
        else:
            self.share_side(b, half).wait_recv()

    def slot(self, tau):
        for k in range(self.stages - 1, -1, -1):
            b = tau - k
            for i, kind in enumerate(self.kinds):
                @pl.when((b >= 0) & (b < BUCKETS) & (b % len(self.kinds) == i))
                def _():
                    self.stage(k, b, kind)

    def drain(self):
        def one(b, _):
            for i, (half, A, B) in enumerate(self.kinds):
                @pl.when(b % len(self.kinds) == i)
                def _():
                    A.drain(b)
                    B.drain(b)
                    self.give_side(b, half).wait_send()
                    self.share_side(b, half).wait_send()
                    B.keep(b).wait()
            return 0
        lax.fori_loop(0, BUCKETS, one, 0)


def main_kernel(
    D, FF, S, grid,
    tok, cot, seg, wq_in, qv_in, wo_in, wu_in, ub_in, wd_in, add_in, gain, shift,
    lo, ig, gall, gsm,
    wq, wo, wu, wd, bq, bu,
    X, QKV, O, N1, N2, Hr, U, GP, R, dB, dA, dOs, dQKV,
    r1s, r2s, Hf, Zf, bias, dY, YB, IGB, IGF,
    sq, su, sv, SM, SML, G, LA1, LA, LB, LS,
    lsem, wsend, wrecv, rsend, rrecv, gsend, grecv, osem, ssend, srecv, asend, arecv, csem,
):
    s = lax.axis_index("section")
    d = lax.axis_index("dp")
    c = lax.axis_index("tensor")
    other = 1 - c
    core_peer = (s, d, other)
    x_peer = (1 - s, d, c)
    half_d, half_f, half_q = D // 2, FF // 2, 3 * D // 2
    pairs = D // 128
    lo_pairs = pairs // 2

    barrier = pltpu.get_barrier_semaphore()
    pl.semaphore_signal(barrier, inc=1, device_id=core_peer, device_id_type=MESH)
    pl.semaphore_signal(barrier, inc=1, device_id=x_peer, device_id_type=MESH)
    if grid:
        ring = Reduction(D, s, d, c, G, gall, LA1, LA, LB, LS, SM, SML, asend, arecv, ssend, srecv, csem)
        ring.greet(barrier)

    weights = [(wq_in.at[j], wq.at[:, ds(c * half_q + j * half_d, half_d)]) for j in range(3)] + [
        (wo_in, wo.at[ds(c * half_d, half_d), :]),
        (wu_in, wu.at[:, ds(c * half_f, half_f, 128)]),
        (wd_in, wd.at[ds(c * half_f, half_f), :]),
    ]
    biases = [bq.at[:, ds(c * half_q, half_q, 128)], bu.at[:, ds(c * half_f, half_f, 128)]]
    local = [pltpu.make_async_copy(src, dst, lsem.at[i]) for i, (src, dst) in enumerate(weights)]
    remote = [
        pltpu.make_async_remote_copy(src, dst, wsend.at[i], wrecv.at[i], device_id=core_peer, device_id_type=MESH)
        for i, (src, dst) in enumerate(weights + [(b, b) for b in biases])
    ]
    tok_copy = pltpu.make_async_copy(tok, X, lsem.at[6])
    cot_copy = pltpu.make_async_copy(cot, dY, lsem.at[7])

    @pl.when(s == 0)
    def _():
        tok_copy.start()

    @pl.when(s == 1)
    def _():
        cot_copy.start()

    for copy in local:
        copy.start()
    bq[:, ds(c * half_q, half_d)] = jnp.broadcast_to(qv_in[0:1, :].astype(F32), (8, half_d))
    bq[:, ds(c * half_q + half_d, half_d)] = jnp.zeros((8, half_d), F32)
    bq[:, ds(c * half_q + 2 * half_d, half_d)] = jnp.broadcast_to(qv_in[1:2, :].astype(F32), (8, half_d))
    bu[:, ds(c * half_f, half_f)] = jnp.broadcast_to(ub_in[...].astype(F32), (8, half_f))
    pl.semaphore_wait(barrier, 2 + ring.greetings() if grid else 2)
    for i in (0, 1, 2, 6, 7):
        remote[i].start()

    for q in range(2):
        row = jnp.broadcast_to(seg[pl.ds(2 * c + q, 1), :].astype(F32), (S, S))
        bias[q] = jnp.where(row.T == row, 0.0, masked_score)
    sq[...] = jnp.zeros_like(sq)
    su[...] = jnp.zeros_like(su)
    sv[...] = jnp.zeros_like(sv)
    lane = lax.broadcasted_iota(jnp.int32, (1, 128), 1)
    first_scaled = jnp.where(lane < HEAD_DIM, 0.125, 0.0).astype(BF16)
    second_scaled = jnp.where(lane < HEAD_DIM, 0.0, 0.125).astype(BF16)
    first_half = jnp.where(lane < HEAD_DIM, 1.0, 0.0).astype(BF16)
    second_half = jnp.where(lane < HEAD_DIM, 0.0, 1.0).astype(BF16)

    def need(*which):
        for i in which:
            if i < 6:
                local[i].wait()
            remote[i].wait_recv()

    def relay(m):
        rows = ds(m * S, S)
        return pltpu.make_async_remote_copy(YB.at[rows], X.at[rows], rsend.at[m], rrecv.at[m], device_id=x_peer, device_id_type=MESH)

    def relay_back(m):
        rows = ds(m * S, S)
        return pltpu.make_async_remote_copy(IGB.at[rows], dY.at[rows], rsend.at[m], rrecv.at[m], device_id=x_peer, device_id_type=MESH)

    def pair_columns(p):
        base = (p // lo_pairs) * half_q + (p % lo_pairs) * 128
        return ds(base, 128), ds(base + half_d, 128), ds(base + 2 * half_d, 128)

    def normed(m, which, N, rs, finish):
        def norm_rows(j, _):
            near, rows = ds(j * 32, 32), ds(m * S + j * 32, 32)
            z = Zf[near, :]
            centered = z - row_mean(z)
            scaled = lax.rsqrt(row_mean(centered * centered) + norm_eps)
            n = centered * scaled
            N[rows, :] = n.astype(BF16)
            rs[rows, :] = jnp.broadcast_to(scaled, (32, 128))
            finish(near, rows, n * gain[which : which + 1, :] + shift[which : which + 1, :])
            return 0

        lax.fori_loop(0, S // 32, norm_rows, 0, unroll=True)

    def forward(t, m):
        rows = ds(m * S, S)

        @pl.when(t == 0)
        def _():
            @pl.when(s == 0)
            def _():
                tok_copy.wait()
            need(0, 1, 2, 6, 7)
            remote[3].start()
            remote[4].start()

        @pl.when(s == 1)
        def _():
            relay(m).wait_recv()

        def qkv_tile(i, _):
            cols = ds(i * 256, 256)
            QKV[rows, cols] = (mm(X[rows, :], wq[:, cols]) + bq[0:1, cols]).astype(BF16)
            return 0

        lax.fori_loop(0, 3 * D // 256, qkv_tile, 0, unroll=True)

        def attend(p, _):
            qc, kc, vc = pair_columns(p)
            q2, k2, v2 = QKV[rows, qc], QKV[rows, kc], QKV[rows, vc]
            weights = ds((m * pairs + p) * S, S)
            outs = []
            for h, (mask, half) in enumerate(((first_scaled, first_half), (second_scaled, second_half))):
                kh = k2 * mask
                shares = []
                for part in range(0, S, 128):
                    st = mm_nt(kh, q2[part : part + 128, :]) + bias[m, :, part : part + 128]
                    e = jnp.exp(st - jnp.max(st, axis=0, keepdims=True))
                    share = (e * (1.0 / jnp.sum(e, axis=0, keepdims=True))).astype(BF16)
                    R[weights, h * S + part : h * S + part + 128] = share
                    shares.append(share)
                outs.append(mm_tn(jnp.concatenate(shares, axis=1), v2 * half))
            O[rows, ds(p * 128, 128)] = (outs[0] + outs[1]).astype(BF16)
            return 0

        lax.fori_loop(0, pairs, attend, 0, unroll=True)

        @pl.when(t == 0)
        def _():
            need(3)
            remote[5].start()

        def out_tile(i, _):
            cols = ds(i * 256, 256)
            Zf[:, cols] = mm(O[rows, :], wo[:, cols]) + X[rows, cols].astype(F32) + add_in[0:1, cols]
            return 0

        lax.fori_loop(0, D // 256, out_tile, 0, unroll=3)

        def first_done(near, rows, h):
            Hf[near, :] = h
            Hr[rows, :] = h.astype(BF16)

        normed(m, 0, N1, r1s, first_done)

        @pl.when(t == 0)
        def _():
            need(4)

        def up_tile(i, _):
            cols = ds(i * 256, 256)
            g = mm(Hr[rows, :], wu[:, cols])
            for j in range(0, S, 32):
                u, slope = gelu_and_slope(g[j : j + 32] + bu[0:1, cols])
                U[ds(m * S + j, 32), cols] = u.astype(BF16)
                GP[ds(m * S + j, 32), cols] = slope.astype(BF16)
            return 0

        lax.fori_loop(0, FF // 256, up_tile, 0, unroll=True)

        @pl.when(t == 0)
        def _():
            need(5)

        def down_tile(i, _):
            cols = ds(i * 256, 256)
            Zf[:, cols] = mm(U[rows, :], wd[:, cols]) + Hf[:, cols] + add_in[1:2, cols]
            return 0

        lax.fori_loop(0, D // 256, down_tile, 0, unroll=3)

        def second_done(near, rows, y):
            YB[rows, :] = y.astype(BF16)

        normed(m, 1, N2, r2s, second_done)
        pltpu.make_async_copy(YB.at[rows], lo.at[rows], osem.at[m]).start()

        @pl.when(s == 0)
        def _():
            relay(m).start()

    def norm_back(m, which, get, N, rs, low):
        def back_rows(j, sums):
            near, rows = ds(j * 32, 32), ds(m * S + j * 32, 32)
            dy, n = get(near, rows), N[rows, :].astype(F32)
            e = dy * gain[which : which + 1, :]
            dz = rs[rows, 0:1] * (e - row_mean(e) - n * row_mean(e * n))
            Zf[near, :] = dz
            low[rows, :] = dz.astype(BF16)
            return sums[0] + eights(dz), sums[1] + eights(dy * n), sums[2] + eights(dy)

        sums = lax.fori_loop(0, S // 32, back_rows, (jnp.zeros((8, D), F32),) * 3, unroll=4)
        for i in range(3):
            sv[2 * i + which] += sums[i]

    def backward(t, m, last):
        rows = ds(m * S, S)

        @pl.when(s == 0)
        def _():
            relay_back(m).wait_recv()

        @pl.when((s == 1) & (m == 0))
        def _():
            cot_copy.wait()

        norm_back(m, 1, lambda near, rows: dY[rows, :].astype(F32), N2, r2s, dB)

        def down_back(i, _):
            cols = ds(i * 256, 256)
            dg = mm_nt(dB[rows, :], wd[cols, :]) * GP[rows, cols].astype(F32)
            su[:, cols] += eights(dg)
            GP[rows, cols] = dg.astype(BF16)
            return 0

        lax.fori_loop(0, FF // 256, down_back, 0, unroll=True)
        last(0)

        def up_back(i, _):
            cols = ds(i * 256, 256)
            Hf[:, cols] = mm_nt(GP[rows, :], wu[cols, :]) + Zf[:, cols]
            return 0

        lax.fori_loop(0, D // 256, up_back, 0, unroll=3)
        norm_back(m, 0, lambda near, rows: Hf[near, :], N1, r1s, dA)
        last(1)

        def out_back(i, _):
            cols = ds(i * 256, 256)
            dOs[:, cols] = mm_nt(dA[rows, :], wo[cols, :]).astype(BF16)
            return 0

        lax.fori_loop(0, D // 256, out_back, 0, unroll=3)
        last(2)

        def attend_back(p, _):
            qc, kc, vc = pair_columns(p)
            q2, k2, v2 = QKV[rows, qc], QKV[rows, kc], QKV[rows, vc]
            do2 = dOs[:, ds(p * 128, 128)]
            kt = k2.T
            weights = ds((m * pairs + p) * S, S)
            parts = []
            for h, half in enumerate((first_half, second_half)):
                vh = v2 * half
                for part in range(0, S, 128):
                    cols = slice(h * S + part, h * S + part + 128)
                    drt = mm_nt(vh, do2[part : part + 128, :])
                    rf = R[weights, cols].astype(F32)
                    parts.append((rf * (drt - jnp.sum(rf * drt, axis=0, keepdims=True))).astype(BF16))
            dst = jnp.concatenate(parts, axis=1)
            dk = mm(dst, jnp.concatenate([q2 * first_scaled, q2 * second_scaled], axis=0))
            dv = mm(R[weights, :], jnp.concatenate([do2 * first_half, do2 * second_half], axis=0))
            dqt = [mm(kt[h * HEAD_DIM : (h + 1) * HEAD_DIM], dst[:, h * S : (h + 1) * S]) for h in range(2)]
            dq = (jnp.concatenate(dqt, axis=0) * 0.125).T.astype(BF16)
            dvb = dv.astype(BF16)
            dQKV[rows, qc] = dq
            dQKV[rows, kc] = dk.astype(BF16)
            dQKV[rows, vc] = dvb
            sq[:, qc] += eights(dq.astype(F32))
            sq[:, vc] += eights(dvb.astype(F32))
            return 0

        lax.fori_loop(0, pairs, attend_back, 0, unroll=True)
        last(3)

        def in_back(i, _):
            cols = ds(i * 256, 256)
            dx = mm_nt(dQKV[rows, :], wq[cols, :]) + Zf[:, cols]
            IGF[rows, cols] = dx
            IGB[rows, cols] = dx.astype(BF16)
            return 0

        lax.fori_loop(0, D // 256, in_back, 0, unroll=3)
        pltpu.make_async_copy(IGF.at[rows], ig.at[rows], osem.at[2 + m]).start()

        @pl.when(s == 1)
        def _():
            relay_back(m).start()

    W = D // 2

    def across(i, start, size, right):
        return mm(R[ds(i * D + start, size, 128), :], right)

    def grad_tiles(k, kind, i):
        if kind == "down":
            left = U[:, ds(k * half_f + i * W, W, 128)].T
            return [mm(left, dB[:, q * W : (q + 1) * W]) for q in range(2)]
        if kind == "out":
            return [across(1, k * half_d, W, dA[:, q * W : (q + 1) * W]) for q in range(2)]
        cols = ds(k * (half_f if kind == "up" else half_q) + i * W, W, 128)
        which, right = (0, GP) if kind == "up" else (2, dQKV)
        return [across(which, q * W, W, right[:, cols]) for q in range(2)]

    first = {"down": 0, "up": 4, "qkv": 8, "out": 11}

    def halves(k, kind, i):
        if kind == "down":
            return [wd.at[ds(k * half_f + i * W, W), q * W : (q + 1) * W] for q in range(2)]
        if kind == "out":
            return [wo.at[ds(k * half_d, W), q * W : (q + 1) * W] for q in range(2)]
        cols = ds(k * (half_f if kind == "up" else half_q) + i * W, W, 128)
        ref = wu if kind == "up" else wq
        return [ref.at[q * W : (q + 1) * W, cols] for q in range(2)]

    def exchange(kind, i):
        b = first[kind] + i
        return [
            pltpu.make_async_remote_copy(part, G.at[ds(b * D + q * W, W)], gsend.at[b, q], grecv.at[b, q], device_id=core_peer, device_id_type=MESH)
            for q, part in enumerate(halves(other, kind, i))
        ]

    def give(kind, i):
        tiles = grad_tiles(other, kind, i)
        for q, copy in enumerate(exchange(kind, i)):
            halves(other, kind, i)[q][...] = tiles[q].astype(BF16)
            copy.start()

    def keep(kind, i):
        tiles = grad_tiles(c, kind, i)
        b = first[kind] + i
        for q, copy in enumerate(exchange(kind, i)):
            copy.wait_recv()
            rows = ds(b * D + q * W, W)
            G[rows, :] = (tiles[q] + G[rows, :].astype(F32)).astype(BF16)

    def slot(tau):
        if grid:
            ring.slot(tau)

    def give_all_down():
        def give_down(i, _):
            give("down", i)
            return 0

        lax.fori_loop(0, 4, give_down, 0)

    def step(t, _):
        back = jnp.where(s == 0, t // 2, t % 2)
        m = jnp.where(s == 0, t % 2, t // 2)

        def last(i):
            @pl.when((s == 0) & (m == 1))
            def _():
                if i == 0:
                    give_all_down()
                keep("down", i)
                slot(i)

        @pl.when(back == 0)
        def _():
            forward(t, m)

        @pl.when(back == 1)
        def _():
            backward(t, m, last)

        return 0

    lax.fori_loop(0, 4, step, 0)

    @pl.when(s == 1)
    def _():
        give_all_down()

        def keep_down(i, _):
            keep("down", i)
            slot(i)
            return 0

        lax.fori_loop(0, 4, keep_down, 0)

    for i, whole in enumerate((Hr, O, X)):
        R[i * D : (i + 1) * D, :] = whole[...].T

    def give_up(i, _):
        give("up", i)
        return 0

    lax.fori_loop(0, 4, give_up, 0)

    def total(v):
        return jnp.sum(v, axis=0, keepdims=True)

    for i in range(3):
        SM[i : i + 1, :] = total(sq[:, i * D : (i + 1) * D])
    for i in range(4):
        SM[3 + i : 4 + i, :] = total(su[:, i * D : (i + 1) * D])
    SM[7:8, :] = jnp.zeros((1, D), F32)
    for i in range(6):
        SM[8 + i : 9 + i, :] = total(sv[i])
    SM[14:16, :] = jnp.zeros((2, D), F32)
    small_core = pltpu.make_async_remote_copy(SM, SML.at[0], ssend.at[0], srecv.at[0], device_id=core_peer, device_id_type=MESH)
    small_core.start()

    def keep_rest(i, _):
        @pl.when(i < 2)
        def _():
            keep("up", 2 * i)
            keep("up", 2 * i + 1)

        @pl.when(i == 0)
        def _():
            give("qkv", 0)
            give("qkv", 1)

        @pl.when(i == 1)
        def _():
            give("qkv", 2)
            give("out", 0)

        @pl.when(i == 2)
        def _():
            keep("qkv", 0)
            keep("qkv", 1)

        @pl.when(i == 3)
        def _():
            keep("qkv", 2)
            keep("out", 0)

        slot(4 + i)
        return 0

    lax.fori_loop(0, 4, keep_rest, 0)
    small_core.wait()
    SM[...] += SML[0]
    if grid:
        ring.small_start(1)

    if grid:
        def last_slot(tau, _):
            slot(tau)
            return 0

        ring.small_finish(1)
        ring.small_start(2)
        lax.fori_loop(8, 10, last_slot, 0)
        ring.small_finish(2)
        ring.small_start(3)
        lax.fori_loop(10, BUCKETS + ring.stages - 1, last_slot, 0)
        ring.small_finish(3)
        ring.drain()
    else:
        result = pltpu.make_async_copy(G, gall, osem.at[4])
        result.start()
        result.wait()
    small_result = pltpu.make_async_copy(SM, gsm, osem.at[5])
    small_result.start()
    for kind, n in (("down", 4), ("up", 4), ("qkv", 3), ("out", 1)):
        for i in range(n):
            for copy in exchange(kind, i):
                copy.wait_send()
    small_result.wait()
    for copy in remote:
        copy.wait_send()
    for m in range(2):
        rows = ds(m * S, S)
        pltpu.make_async_copy(YB.at[rows], lo.at[rows], osem.at[m]).wait()
        pltpu.make_async_copy(IGF.at[rows], ig.at[rows], osem.at[2 + m]).wait()

    @pl.when(s == 0)
    def _():
        for m in range(2):
            relay(m).wait_send()

    @pl.when(s == 1)
    def _():
        for m in range(2):
            relay_back(m).wait_send()


def main_call(grid, S, tok, cot, seg, wq, qv, wo, wu, ub, wd, add, gain, shift):
    rows, D = tok.shape
    FF = 2 * wu.shape[1]
    hd, hq = D // 2, 3 * D // 2
    any_spec = pl.BlockSpec(memory_space=pl.ANY)
    vm_spec = pl.BlockSpec(memory_space=pltpu.VMEM)
    sds = jax.ShapeDtypeStruct
    V, DMA = pltpu.VMEM, pltpu.SemaphoreType.DMA
    line_a, line_b = MOST_A // 2 // LINE, MOST_B // LINE
    scratch = [
        V((D, 2 * hq), BF16), V((D, D), BF16), V((D, FF), BF16), V((FF, D), BF16), V((8, 2 * hq), F32), V((8, FF), F32),
        V((rows, D), BF16), V((rows, 3 * D), BF16), V((rows, D), BF16), V((rows, D), BF16), V((rows, D), BF16), V((rows, D), BF16),
        V((rows, FF), BF16), V((rows, FF), BF16), V((2 * (D // 128) * S, 2 * S), BF16),
        V((rows, D), BF16), V((rows, D), BF16), V((S, D), BF16), V((rows, 3 * D), BF16),
        V((rows, 128), F32), V((rows, 128), F32), V((S, D), F32), V((S, D), F32), V((2, S, S), F32),
        V((rows, D), BF16), V((rows, D), BF16), V((rows, D), BF16), V((rows, D), F32),
        V((8, 2 * hq), F32), V((8, FF), F32), V((6, 8, D), F32), V((16, D), F32), V((4, 16, D), F32),
        V((BUCKETS * D, hd), BF16), V((BUCKETS * MOST_A // 2, hd), BF16), V((BUCKETS * line_a * (LINE + 1), hd), BF16),
        V((BUCKETS * line_b * (LINE + 1), hd), BF16), V((BUCKETS * line_b, hd), BF16),
        DMA((8,)), DMA((8,)), DMA((8,)), DMA((2,)), DMA((2,)),
        DMA((BUCKETS, 2)), DMA((BUCKETS, 2)), DMA((6,)), DMA((4,)), DMA((4,)),
        DMA((BUCKETS, 8 * LINE + 3)), DMA((BUCKETS, 8 * LINE + 3)), DMA((BUCKETS, 2)),
    ]
    return pl.pallas_call(
        partial(main_kernel, D, FF, S, grid),
        out_shape=(sds((rows, D), BF16), sds((rows, D), F32), sds((BUCKETS * D, hd), BF16), sds((16, D), F32)),
        in_specs=[any_spec, any_spec, vm_spec, any_spec, vm_spec, any_spec, any_spec, vm_spec, any_spec, vm_spec, vm_spec, vm_spec],
        out_specs=(any_spec,) * 4,
        scratch_shapes=scratch,
        compiler_params=pltpu.CompilerParams(collective_id=0, has_side_effects=True, vmem_limit_bytes=60 * 2**20),
        name="layer_pass",
    )(tok, cot, seg, wq, qv, wo, wu, ub, wd, add, gain, shift)


def unpack_kernel(D, FF, gall, sums, gq, gqv, go, gu, gub, gd, ga, gg, gs, low, wide, in_sem, out_sem):
    c = lax.axis_index("tensor")
    W = D // 2
    reads = [pltpu.make_async_copy(gall.at[b * D : (b + 1) * D], low.at[b], in_sem.at[b]) for b in range(BUCKETS)]
    for read in reads:
        read.start()
    writes = []
    for b in range(BUCKETS):
        if b < 4 or b == 11:
            rows = wide.at[b]
            place = gd.at[b * W : (b + 1) * W, :] if b < 4 else go
            parts = [(rows.at[q * W : (q + 1) * W], place.at[:, q * W : (q + 1) * W]) for q in range(2)]
        elif b < 8:
            parts = [(wide.at[b], gu.at[:, (b - 4) * W : (b - 3) * W])]
        else:
            parts = [(wide.at[b], gq.at[b - 8])]
        writes.append([pltpu.make_async_copy(src, dst, out_sem.at[b, q]) for q, (src, dst) in enumerate(parts)])
    own = ds(c * W, W)
    gqv[0:1, :] = sums[pl.ds(c, 1), own]
    gqv[1:2, :] = sums[pl.ds(1 + c, 1), own]
    for i in range(2):
        gub[:, i * D : (i + 1) * D] = sums[pl.ds(3 + 2 * c + i, 1), :]
        ga[i : i + 1, :] = sums[8 + i : 9 + i, own]
        gg[i : i + 1, :] = sums[10 + i : 11 + i, own]
        gs[i : i + 1, :] = sums[12 + i : 13 + i, own]
    for b in range(BUCKETS):
        reads[b].wait()
        wide[b] = low[b].astype(F32)
        for copy in writes[b]:
            copy.start()
    for copies in writes:
        for copy in copies:
            copy.wait()


def unpack_call(gall, gsm, D, FF):
    W, F = D // 2, FF // 2
    sds = jax.ShapeDtypeStruct
    any_spec = pl.BlockSpec(memory_space=pl.ANY)
    vm_spec = pl.BlockSpec(memory_space=pltpu.VMEM)
    return pl.pallas_call(
        partial(unpack_kernel, D, FF),
        in_specs=[any_spec, vm_spec],
        out_specs=(any_spec, vm_spec, any_spec, any_spec, vm_spec, any_spec, vm_spec, vm_spec, vm_spec),
        out_shape=(
            sds((3, D, W), F32), sds((2, W), F32), sds((W, D), F32), sds((D, F), F32), sds((1, F), F32),
            sds((F, D), F32), sds((2, W), F32), sds((2, W), F32), sds((2, W), F32),
        ),
        scratch_shapes=[
            pltpu.VMEM((BUCKETS, D, W), BF16), pltpu.VMEM((BUCKETS, D, W), F32),
            pltpu.SemaphoreType.DMA((BUCKETS,)), pltpu.SemaphoreType.DMA((BUCKETS, 2)),
        ],
        compiler_params=pltpu.CompilerParams(vmem_limit_bytes=60 * 2**20),
        name="unpack",
    )(gall, gsm)


def shards(tokens, segment_ids, out_cotangent, w_qkv, qv_bias, w_out, w_up, up_bias, w_down, add_bias, norm_gain, norm_bias):
    D = tokens.shape[1]
    FF = 2 * w_up.shape[2]
    S = segment_ids.shape[1]
    grid = lax.axis_size("dp") == 2 * LINE
    lo, ig, gall, gsm = main_call(
        grid, S, tokens, out_cotangent, segment_ids, w_qkv[0].transpose(1, 0, 2), qv_bias[0],
        w_out[0], w_up[0], up_bias, w_down[0], add_bias[0], norm_gain[0], norm_bias[0],
    )
    if not grid:
        gall, gsm = lax.psum(gall, "dp"), lax.psum(gsm, "dp")
    gq, gqv, go, gu, gub, gd, ga, gg, gs = unpack_call(gall, gsm, D, FF)
    return (
        lo[None], ig[None], gq.transpose(1, 0, 2)[None], gqv[None], go[None], gu[None], gub, gd[None],
        ga[None], gg[None], gs[None],
    )


def solution(mesh):
    return jax.shard_map(
        shards,
        mesh=mesh,
        in_specs=(
            P(("dp", "tensor"), None), P("dp", None), P(("dp", "tensor"), None),
            P("section", None, None, "tensor"), P("section", None, "tensor"), P("section", "tensor", None),
            P("section", None, "tensor"), P("section", "tensor"), P("section", "tensor", None),
            P("section", None, None), P("section", None, None), P("section", None, None),
        ),
        out_specs=(
            P("section", ("dp", "tensor"), None), P("section", ("dp", "tensor"), None),
            P("section", None, None, "tensor"), P("section", None, "tensor"), P("section", "tensor", None),
            P("section", None, "tensor"), P("section", "tensor"), P("section", "tensor", None),
            P("section", None, "tensor"), P("section", None, "tensor"), P("section", None, "tensor"),
        ),
        check_vma=False,
    )
```

```python
from functools import partial

import jax
import jax.numpy as jnp
from jax import lax
from jax.experimental import pallas as pl
from jax.experimental.pallas import tpu as pltpu
from jax.sharding import PartitionSpec as P

HEAD_DIM = 64
norm_eps = 1e-12
masked_score = -1e30
LINE = 4
BUCKETS = 12
A_ROWS = (512,)
MOST_A, MOST_B = 512, 256
MESH = pl.DeviceIdType.MESH
F32 = jnp.float32
BF16 = jnp.bfloat16


def mm(a, b):
    return lax.dot_general(a, b, (((1,), (0,)), ((), ())), preferred_element_type=F32)


def mm_nt(a, b):
    return lax.dot_general(a, b, (((1,), (1,)), ((), ())), preferred_element_type=F32)


def mm_tn(a, b):
    return lax.dot_general(a, b, (((0,), (0,)), ((), ())), preferred_element_type=F32)


def ds(start, size, align=None):
    return pl.ds(pl.multiple_of(start, align or size), size)


def eights(v):
    return jnp.sum(v.reshape(v.shape[0] // 8, 8, v.shape[1]), axis=0)


def gelu_and_slope(g):
    size = jnp.abs(g)
    x = 1.0 + 0.2316419 * size
    t = pl.reciprocal(x, approx=True)
    t = t * (2.0 - x * t)
    density = 0.3989422804014327 * jnp.exp2(g * g * -0.7213475204444817)
    tail = ((((1.330274429 * t - 1.821255978) * t + 1.781477937) * t - 0.356563782) * t + 0.319381530) * t * density
    cdf = jnp.where(g > 0.0, 1.0 - tail, tail)
    return g * cdf, cdf + g * density


def row_mean(v):
    return jnp.sum(v, axis=-1, keepdims=True) * (1.0 / v.shape[-1])


class Line:
    def __init__(self, red, base, size, most, landing, sems):
        self.red, self.base, self.size, self.most, self.landing, self.sems = red, base, size, most, landing, sems

    def own(self, b, j):
        return ds(self.base(b) + j * self.size, self.size, 16)

    def slot(self, b, j):
        return ds(b * (LINE + 1) * self.most + j * self.size, self.size, 16)

    def sum_up(self, b, j):
        r = self.red
        return r.remote(r.G.at[self.own(b, j)], self.landing.at[self.slot(b, j)], b, self.sems + j, r.above)

    def sum_down(self, b, j):
        r = self.red
        place = jnp.where(j == r.z - 1, LINE, j)
        return r.remote(r.G.at[self.own(b, j)], self.landing.at[self.slot(b, place)], b, self.sems + LINE + j, r.below)

    def from_above(self, b, j):
        r = self.red
        place = jnp.where(j == r.z, LINE, j)
        return r.remote(r.G.at[self.own(b, j)], self.landing.at[self.slot(b, place)], b, self.sems + LINE + j, r.below)

    def out_up(self, b, j, own=False):
        r = self.red
        return r.remote(r.place(own).at[self.own(b, j)], r.out.at[self.own(b, j)], b, self.sems + 2 * LINE + j, r.above)

    def out_down(self, b, j, own=False):
        r = self.red
        return r.remote(r.place(own).at[self.own(b, j)], r.out.at[self.own(b, j)], b, self.sems + 3 * LINE + j, r.below)

    def add(self, b, j, *places):
        G = self.red.G
        rows = self.own(b, j)
        total = G[rows, :].astype(F32)
        for place in places:
            total = total + self.landing[self.slot(b, place), :].astype(F32)
        G[rows, :] = total.astype(BF16)

    def begin(self, b):
        z = self.red.z

        @pl.when(z == 0)
        def _():
            for i in range(LINE - 1):
                self.sum_up(b, LINE - 1 - i).start()

        @pl.when(z == LINE - 1)
        def _():
            for i in range(LINE - 1):
                self.sum_down(b, i).start()

    def pass_on(self, b, i):
        z = self.red.z
        end = LINE - 1 - z
        up, down = LINE - 2 - i + z, 1 + i - end

        @pl.when((up > z) & (up < LINE) & (z > 0))
        def _():
            self.sum_up(b, up).wait_recv()
            self.add(b, up, up)
            self.sum_up(b, up).start()

        @pl.when((down < z) & (down >= 0) & (end > 0))
        def _():
            self.from_above(b, down).wait_recv()
            self.add(b, down, down)
            self.sum_down(b, down).start()

    def finish_own(self, b):
        z = self.red.z

        @pl.when(z > 0)
        def _():
            self.sum_up(b, z).wait_recv()

        @pl.when(z < LINE - 1)
        def _():
            self.from_above(b, z).wait_recv()

        @pl.when(z == 0)
        def _():
            self.add(b, 0, LINE)

        @pl.when(z == LINE - 1)
        def _():
            self.add(b, LINE - 1, LINE - 1)

        @pl.when((z > 0) & (z < LINE - 1))
        def _():
            self.add(b, z, z, LINE)

    def spread(self, b):
        z = self.red.z

        @pl.when(z < LINE - 1)
        def _():
            self.out_up(b, z, True).start()

        @pl.when(z > 0)
        def _():
            self.out_down(b, z, True).start()

        self.keep(b).start()

    def keep(self, b):
        r = self.red
        rows = self.own(b, r.z)
        return pltpu.make_async_copy(r.G.at[rows], r.out.at[rows], r.csem.at[b, self.sems // (4 * LINE)])

    def spread_on(self, b, i):
        z = self.red.z

        @pl.when(z - i >= 0)
        def _():
            self.out_up(b, z - i).wait_recv()

            @pl.when(z < LINE - 1)
            def _():
                self.out_up(b, z - i).start()

        @pl.when(z + i < LINE)
        def _():
            self.out_down(b, z + i).wait_recv()

            @pl.when(z > 0)
            def _():
                self.out_down(b, z + i).start()

    def drain(self, b):
        z = self.red.z
        for j in range(LINE):
            @pl.when(j > z)
            def _():
                self.sum_up(b, j).wait_send()

            @pl.when(j < z)
            def _():
                self.sum_down(b, j).wait_send()

            @pl.when((j <= z) & (z < LINE - 1))
            def _():
                self.out_up(b, j).wait_send()

            @pl.when((j >= z) & (z > 0))
            def _():
                self.out_down(b, j).wait_send()


class Reduction:
    stages = 9

    def __init__(self, D, s, d, c, G, out, LA1, LA, LB, LS, SM, SML, asend, arecv, ssend, srecv, csem):
        self.out, self.csem = out, csem
        self.G, self.LA1, self.LS, self.SM, self.SML = G, LA1, LS, SM, SML
        self.asend, self.arecv, self.ssend, self.srecv = asend, arecv, ssend, srecv
        self.z, self.y = d // 2, d % 2
        self.s, self.d, self.c = s, d, c
        self.above = (s, jnp.minimum(d + 2, 2 * LINE - 1), c)
        self.below = (s, jnp.maximum(d - 2, 0), c)
        self.beside = (s, d + 1 - 2 * self.y, c)
        self.D = D
        self.kinds = []
        for a_rows in A_ROWS:
            half = a_rows // 2
            base = partial(lambda half, b: b * D + self.y * half, half)
            a = Line(self, base, half // LINE, MOST_A // 2 // LINE, LA, 0)
            base = partial(lambda a_rows, b: b * D + a_rows, a_rows)
            self.kinds.append((half, a, Line(self, base, (D - a_rows) // LINE, MOST_B // LINE, LB, 4 * LINE)))
        z = self.z
        pair = z + 1 - 2 * (z % 2)
        far = (z + 2) % 4
        self.small_peers = [None, self.beside, (s, pair * 2 + self.y, c), (s, far * 2 + self.y, c)]

    def place(self, own):
        return self.G if own else self.out

    def remote(self, src, dst, b, sem, to):
        return pltpu.make_async_remote_copy(src, dst, self.asend.at[b, sem], self.arecv.at[b, sem], device_id=to, device_id_type=MESH)

    def greet(self, barrier):
        def hello(to):
            pl.semaphore_signal(barrier, inc=1, device_id=to, device_id_type=MESH)
        for to in self.small_peers[1:]:
            hello(to)
        @pl.when((self.z == 1))
        def _():
            hello(self.above)

        @pl.when((self.z == 2))
        def _():
            hello(self.below)

    def greetings(self):
        return 3 + ((self.z == 1) | (self.z == 2)).astype(jnp.int32)

    def small_copy(self, k):
        return pltpu.make_async_remote_copy(self.SM, self.SML.at[k], self.ssend.at[k], self.srecv.at[k], device_id=self.small_peers[k], device_id_type=MESH)

    def small_start(self, k):
        self.small_copy(k).start()

    def small_finish(self, k):
        self.small_copy(k).wait()
        self.SM[...] += self.SML[k]

    def give_side(self, b, half):
        rows = ds(b * self.D + (1 - self.y) * half, half, 16)
        return self.remote(self.G.at[rows], self.LA1.at[ds(b * (MOST_A // 2), half, 16)], b, 8 * LINE, self.beside)

    def share_side(self, b, half):
        rows = ds(b * self.D + self.y * half, half, 16)
        return self.remote(self.out.at[rows], self.out.at[rows], b, 8 * LINE + 1, self.beside)

    def swap(self, b, B):
        return self.remote(self.G.at[B.own(b, self.z)], self.LS.at[ds(b * B.most, B.size, 16)], b, 8 * LINE + 2, self.beside)

    def stage(self, k, b, kind):
        half, A, B = kind
        if k == 0:
            self.give_side(b, half).start()
            B.begin(b)
        elif k == 1:
            B.pass_on(b, 0)
            self.give_side(b, half).wait_recv()
            rows = ds(b * self.D + self.y * half, half, 16)
            land = ds(b * (MOST_A // 2), half, 16)
            self.G[rows, :] = (self.G[rows, :].astype(F32) + self.LA1[land, :].astype(F32)).astype(BF16)
            A.begin(b)
        elif k == 2:
            B.pass_on(b, 1)
            A.pass_on(b, 0)
        elif k == 3:
            B.finish_own(b)
            self.swap(b, B).start()
            A.pass_on(b, 1)
        elif k == 4:
            A.finish_own(b)
            A.spread(b)
            self.swap(b, B).wait()
            rows, land = B.own(b, self.z), ds(b * B.most, B.size, 16)
            self.G[rows, :] = (self.G[rows, :].astype(F32) + self.LS[land, :].astype(F32)).astype(BF16)
            B.spread(b)
        elif k <= 7:
            A.spread_on(b, k - 4)
            B.spread_on(b, k - 4)
            if k == 7:
                A.keep(b).wait()
                self.share_side(b, half).start()
        else:
            self.share_side(b, half).wait_recv()

    def slot(self, tau):
        for k in (7, 0, 6, 4, 3, 5, 2, 1, 8):
            b = tau - k
            for i, kind in enumerate(self.kinds):
                @pl.when((b >= 0) & (b < BUCKETS) & (b % len(self.kinds) == i))
                def _():
                    self.stage(k, b, kind)

    def drain(self):
        def one(b, _):
            for i, (half, A, B) in enumerate(self.kinds):
                @pl.when(b % len(self.kinds) == i)
                def _():
                    A.drain(b)
                    B.drain(b)
                    self.give_side(b, half).wait_send()
                    self.share_side(b, half).wait_send()
                    B.keep(b).wait()
            return 0
        lax.fori_loop(0, BUCKETS, one, 0)


def main_kernel(
    D, FF, S, grid,
    tok, cot, seg, wq_in, qv_in, wo_in, wu_in, ub_in, wd_in, add_in, gain, shift,
    lo, ig, gall, gsm,
    wq, wo, wu, wd, bq, bu,
    X, QKV, O, N1, N2, Hr, U, GP, R, dB, dA, dOs, dQKV,
    r1s, r2s, Hf, Zf, bias, dY, YB, IGB, IGF,
    sq, su, sv, SM, SML, G, LA1, LA, LB, LS,
    lsem, wsend, wrecv, rsend, rrecv, gsend, grecv, osem, ssend, srecv, asend, arecv, csem,
):
    s = lax.axis_index("section")
    d = lax.axis_index("dp")
    c = lax.axis_index("tensor")
    other = 1 - c
    core_peer = (s, d, other)
    x_peer = (1 - s, d, c)
    half_d, half_f, half_q = D // 2, FF // 2, 3 * D // 2
    pairs = D // 128
    lo_pairs = pairs // 2

    barrier = pltpu.get_barrier_semaphore()
    pl.semaphore_signal(barrier, inc=1, device_id=core_peer, device_id_type=MESH)
    pl.semaphore_signal(barrier, inc=1, device_id=x_peer, device_id_type=MESH)
    if grid:
        ring = Reduction(D, s, d, c, G, gall, LA1, LA, LB, LS, SM, SML, asend, arecv, ssend, srecv, csem)
        ring.greet(barrier)

    weights = [(wq_in.at[j], wq.at[:, ds(c * half_q + j * half_d, half_d)]) for j in range(3)] + [
        (wo_in, wo.at[ds(c * half_d, half_d), :]),
        (wu_in, wu.at[:, ds(c * half_f, half_f, 128)]),
        (wd_in, wd.at[ds(c * half_f, half_f), :]),
    ]
    biases = [bq.at[:, ds(c * half_q, half_q, 128)], bu.at[:, ds(c * half_f, half_f, 128)]]
    local = [pltpu.make_async_copy(src, dst, lsem.at[i]) for i, (src, dst) in enumerate(weights)]
    remote = [
        pltpu.make_async_remote_copy(src, dst, wsend.at[i], wrecv.at[i], device_id=core_peer, device_id_type=MESH)
        for i, (src, dst) in enumerate(weights + [(b, b) for b in biases])
    ]
    tok_copy = pltpu.make_async_copy(tok, X, lsem.at[6])
    cot_copy = pltpu.make_async_copy(cot, dY, lsem.at[7])

    @pl.when(s == 0)
    def _():
        tok_copy.start()

    @pl.when(s == 1)
    def _():
        cot_copy.start()

    for copy in local:
        copy.start()
    bq[:, ds(c * half_q, half_d)] = jnp.broadcast_to(qv_in[0:1, :].astype(F32), (8, half_d))
    bq[:, ds(c * half_q + half_d, half_d)] = jnp.zeros((8, half_d), F32)
    bq[:, ds(c * half_q + 2 * half_d, half_d)] = jnp.broadcast_to(qv_in[1:2, :].astype(F32), (8, half_d))
    bu[:, ds(c * half_f, half_f)] = jnp.broadcast_to(ub_in[...].astype(F32), (8, half_f))
    pl.semaphore_wait(barrier, 2 + ring.greetings() if grid else 2)
    for i in (0, 1, 2, 6, 7):
        remote[i].start()

    for q in range(2):
        row = jnp.broadcast_to(seg[pl.ds(2 * c + q, 1), :].astype(F32), (S, S))
        bias[q] = jnp.where(row.T == row, 0.0, masked_score)
    sq[...] = jnp.zeros_like(sq)
    su[...] = jnp.zeros_like(su)
    sv[...] = jnp.zeros_like(sv)
    lane = lax.broadcasted_iota(jnp.int32, (1, 128), 1)
    first_scaled = jnp.where(lane < HEAD_DIM, 0.125, 0.0).astype(BF16)
    second_scaled = jnp.where(lane < HEAD_DIM, 0.0, 0.125).astype(BF16)
    first_half = jnp.where(lane < HEAD_DIM, 1.0, 0.0).astype(BF16)
    second_half = jnp.where(lane < HEAD_DIM, 0.0, 1.0).astype(BF16)

    def need(*which):
        for i in which:
            if i < 6:
                local[i].wait()
            remote[i].wait_recv()

    def relay(m, part):
        rows = ds(m * S + part * (S // 2), S // 2)
        sem = 2 * m + part
        return pltpu.make_async_remote_copy(YB.at[rows], X.at[rows], rsend.at[sem], rrecv.at[sem], device_id=x_peer, device_id_type=MESH)

    def relay_back(m):
        rows = ds(m * S, S)
        return pltpu.make_async_remote_copy(IGB.at[rows], dY.at[rows], rsend.at[2 * m], rrecv.at[2 * m], device_id=x_peer, device_id_type=MESH)

    def pair_columns(p):
        base = (p // lo_pairs) * half_q + (p % lo_pairs) * 128
        return ds(base, 128), ds(base + half_d, 128), ds(base + 2 * half_d, 128)

    def normed(m, which, N, rs, finish, sent=None):
        def norm_rows(j, _):
            near, rows = ds(j * 32, 32), ds(m * S + j * 32, 32)
            z = Zf[near, :]
            centered = z - row_mean(z)
            scaled = lax.rsqrt(row_mean(centered * centered) + norm_eps)
            n = centered * scaled
            N[rows, :] = n.astype(BF16)
            rs[rows, :] = jnp.broadcast_to(scaled, (32, 128))
            finish(near, rows, n * gain[which : which + 1, :] + shift[which : which + 1, :])
            return 0

        for part in range(2):
            lax.fori_loop(part * S // 64, (part + 1) * S // 64, norm_rows, 0, unroll=True)
            if sent is not None:
                sent(part)

    def forward(t, m):
        rows = ds(m * S, S)

        @pl.when(t == 0)
        def _():
            @pl.when(s == 0)
            def _():
                tok_copy.wait()
            need(0, 1, 2, 6, 7)
            remote[3].start()
            remote[4].start()

        @pl.when(s == 1)
        def _():
            relay(m, 0).wait_recv()
            relay(m, 1).wait_recv()

        def qkv_tile(i, _):
            cols = ds(i * 256, 256)
            QKV[rows, cols] = (mm(X[rows, :], wq[:, cols]) + bq[0:1, cols]).astype(BF16)
            return 0

        lax.fori_loop(0, 3 * D // 256, qkv_tile, 0, unroll=True)

        def attend(p, _):
            qc, kc, vc = pair_columns(p)
            q2, k2, v2 = QKV[rows, qc], QKV[rows, kc], QKV[rows, vc]
            weights = ds((m * pairs + p) * S, S)
            outs = []
            for h, (mask, half) in enumerate(((first_scaled, first_half), (second_scaled, second_half))):
                kh = k2 * mask
                shares = []
                for part in range(0, S, 128):
                    st = mm_nt(kh, q2[part : part + 128, :]) + bias[m, :, part : part + 128]
                    e = jnp.exp(st - jnp.max(st, axis=0, keepdims=True))
                    share = (e * (1.0 / jnp.sum(e, axis=0, keepdims=True))).astype(BF16)
                    R[weights, h * S + part : h * S + part + 128] = share
                    shares.append(share)
                outs.append(mm_tn(jnp.concatenate(shares, axis=1), v2 * half))
            O[rows, ds(p * 128, 128)] = (outs[0] + outs[1]).astype(BF16)
            return 0

        lax.fori_loop(0, pairs, attend, 0, unroll=True)

        @pl.when(t == 0)
        def _():
            need(3)
            remote[5].start()

        def out_tile(i, _):
            cols = ds(i * 256, 256)
            Zf[:, cols] = mm(O[rows, :], wo[:, cols]) + X[rows, cols].astype(F32) + add_in[0:1, cols]
            return 0

        lax.fori_loop(0, D // 256, out_tile, 0, unroll=3)

        def first_done(near, rows, h):
            Hf[near, :] = h
            Hr[rows, :] = h.astype(BF16)

        normed(m, 0, N1, r1s, first_done)

        @pl.when(t == 0)
        def _():
            need(4)

        def up_tile(i, _):
            cols = ds(i * 256, 256)
            g = mm(Hr[rows, :], wu[:, cols])
            for j in range(0, S, 32):
                u, slope = gelu_and_slope(g[j : j + 32] + bu[0:1, cols])
                U[ds(m * S + j, 32), cols] = u.astype(BF16)
                GP[ds(m * S + j, 32), cols] = slope.astype(BF16)
            return 0

        lax.fori_loop(0, FF // 256, up_tile, 0, unroll=True)

        @pl.when(t == 0)
        def _():
            need(5)

        def down_tile(i, _):
            cols = ds(i * 256, 256)
            Zf[:, cols] = mm(U[rows, :], wd[:, cols]) + Hf[:, cols] + add_in[1:2, cols]
            return 0

        lax.fori_loop(0, D // 256, down_tile, 0, unroll=3)

        def second_done(near, rows, y):
            YB[rows, :] = y.astype(BF16)

        def send(part):
            @pl.when(s == 0)
            def _():
                relay(m, part).start()

        normed(m, 1, N2, r2s, second_done, send)
        pltpu.make_async_copy(YB.at[rows], lo.at[rows], osem.at[m]).start()

    def norm_back(m, which, get, N, rs, low):
        def back_rows(j, sums):
            near, rows = ds(j * 32, 32), ds(m * S + j * 32, 32)
            dy, n = get(near, rows), N[rows, :].astype(F32)
            e = dy * gain[which : which + 1, :]
            dz = rs[rows, 0:1] * (e - row_mean(e) - n * row_mean(e * n))
            Zf[near, :] = dz
            low[rows, :] = dz.astype(BF16)
            return sums[0] + eights(dz), sums[1] + eights(dy * n), sums[2] + eights(dy)

        sums = lax.fori_loop(0, S // 32, back_rows, (jnp.zeros((8, D), F32),) * 3, unroll=4)
        for i in range(3):
            sv[2 * i + which] += sums[i]

    def backward(t, m, last):
        rows = ds(m * S, S)

        @pl.when(s == 0)
        def _():
            relay_back(m).wait_recv()

        @pl.when((s == 1) & (m == 0))
        def _():
            cot_copy.wait()

        norm_back(m, 1, lambda near, rows: dY[rows, :].astype(F32), N2, r2s, dB)

        def down_back(i, _):
            cols = ds(i * 256, 256)
            dg = mm_nt(dB[rows, :], wd[cols, :]) * GP[rows, cols].astype(F32)
            su[:, cols] += eights(dg)
            GP[rows, cols] = dg.astype(BF16)
            return 0

        lax.fori_loop(0, FF // 256, down_back, 0, unroll=True)
        last(0)

        def up_back(i, _):
            cols = ds(i * 256, 256)
            Hf[:, cols] = mm_nt(GP[rows, :], wu[cols, :]) + Zf[:, cols]
            return 0

        lax.fori_loop(0, D // 256, up_back, 0, unroll=3)
        norm_back(m, 0, lambda near, rows: Hf[near, :], N1, r1s, dA)
        last(1)

        def out_back(i, _):
            cols = ds(i * 256, 256)
            dOs[:, cols] = mm_nt(dA[rows, :], wo[cols, :]).astype(BF16)
            return 0

        lax.fori_loop(0, D // 256, out_back, 0, unroll=3)
        last(2)

        def attend_back(p, _):
            qc, kc, vc = pair_columns(p)
            q2, k2, v2 = QKV[rows, qc], QKV[rows, kc], QKV[rows, vc]
            do2 = dOs[:, ds(p * 128, 128)]
            kt = k2.T
            weights = ds((m * pairs + p) * S, S)
            parts = []
            for h, half in enumerate((first_half, second_half)):
                vh = v2 * half
                for part in range(0, S, 128):
                    cols = slice(h * S + part, h * S + part + 128)
                    drt = mm_nt(vh, do2[part : part + 128, :])
                    rf = R[weights, cols].astype(F32)
                    parts.append((rf * (drt - jnp.sum(rf * drt, axis=0, keepdims=True))).astype(BF16))
            dst = jnp.concatenate(parts, axis=1)
            dk = mm(dst, jnp.concatenate([q2 * first_scaled, q2 * second_scaled], axis=0))
            dv = mm(R[weights, :], jnp.concatenate([do2 * first_half, do2 * second_half], axis=0))
            dqt = [mm(kt[h * HEAD_DIM : (h + 1) * HEAD_DIM], dst[:, h * S : (h + 1) * S]) for h in range(2)]
            dq = (jnp.concatenate(dqt, axis=0) * 0.125).T.astype(BF16)
            dvb = dv.astype(BF16)
            dQKV[rows, qc] = dq
            dQKV[rows, kc] = dk.astype(BF16)
            dQKV[rows, vc] = dvb
            sq[:, qc] += eights(dq.astype(F32))
            sq[:, vc] += eights(dvb.astype(F32))
            return 0

        lax.fori_loop(0, pairs, attend_back, 0, unroll=True)
        last(3)

        def in_back(i, _):
            cols = ds(i * 256, 256)
            dx = mm_nt(dQKV[rows, :], wq[cols, :]) + Zf[:, cols]
            IGF[rows, cols] = dx
            IGB[rows, cols] = dx.astype(BF16)
            return 0

        lax.fori_loop(0, D // 256, in_back, 0, unroll=3)
        pltpu.make_async_copy(IGF.at[rows], ig.at[rows], osem.at[2 + m]).start()

        @pl.when(s == 1)
        def _():
            relay_back(m).start()

    W = D // 2

    def across(i, start, size, right):
        return mm(R[ds(i * D + start, size, 128), :], right)

    def grad_tiles(k, kind, i):
        if kind == "down":
            left = U[:, ds(k * half_f + i * W, W, 128)].T
            return [mm(left, dB[:, q * W : (q + 1) * W]) for q in range(2)]
        if kind == "out":
            return [across(1, k * half_d, W, dA[:, q * W : (q + 1) * W]) for q in range(2)]
        cols = ds(k * (half_f if kind == "up" else half_q) + i * W, W, 128)
        which, right = (0, GP) if kind == "up" else (2, dQKV)
        return [across(which, q * W, W, right[:, cols]) for q in range(2)]

    first = {"down": 0, "up": 4, "qkv": 8, "out": 11}

    def halves(k, kind, i):
        if kind == "down":
            return [wd.at[ds(k * half_f + i * W, W), q * W : (q + 1) * W] for q in range(2)]
        if kind == "out":
            return [wo.at[ds(k * half_d, W), q * W : (q + 1) * W] for q in range(2)]
        cols = ds(k * (half_f if kind == "up" else half_q) + i * W, W, 128)
        ref = wu if kind == "up" else wq
        return [ref.at[q * W : (q + 1) * W, cols] for q in range(2)]

    def exchange(kind, i):
        b = first[kind] + i
        return [
            pltpu.make_async_remote_copy(part, G.at[ds(b * D + q * W, W)], gsend.at[b, q], grecv.at[b, q], device_id=core_peer, device_id_type=MESH)
            for q, part in enumerate(halves(other, kind, i))
        ]

    def give(kind, i):
        tiles = grad_tiles(other, kind, i)
        for q, copy in enumerate(exchange(kind, i)):
            halves(other, kind, i)[q][...] = tiles[q].astype(BF16)
            copy.start()

    def keep(kind, i):
        tiles = grad_tiles(c, kind, i)
        b = first[kind] + i
        for q, copy in enumerate(exchange(kind, i)):
            copy.wait_recv()
            rows = ds(b * D + q * W, W)
            G[rows, :] = (tiles[q] + G[rows, :].astype(F32)).astype(BF16)

    def slot(tau):
        if grid:
            ring.slot(tau)

    def give_all_down():
        def give_down(i, _):
            give("down", i)
            return 0

        lax.fori_loop(0, 4, give_down, 0)

    def step(t, _):
        back = jnp.where(s == 0, t // 2, t % 2)
        m = jnp.where(s == 0, t % 2, t // 2)

        def last(i):
            @pl.when((s == 0) & (m == 1))
            def _():
                if i == 0:
                    give_all_down()
                keep("down", i)
                slot(i)

        @pl.when(back == 0)
        def _():
            forward(t, m)

        @pl.when(back == 1)
        def _():
            backward(t, m, last)

        return 0

    lax.fori_loop(0, 4, step, 0)

    @pl.when(s == 1)
    def _():
        give_all_down()

        def keep_down(i, _):
            keep("down", i)
            slot(i)
            return 0

        lax.fori_loop(0, 4, keep_down, 0)

    for i, whole in enumerate((Hr, O, X)):
        R[i * D : (i + 1) * D, :] = whole[...].T

    def give_up(i, _):
        give("up", i)
        return 0

    lax.fori_loop(0, 4, give_up, 0)

    def total(v):
        return jnp.sum(v, axis=0, keepdims=True)

    for i in range(3):
        SM[i : i + 1, :] = total(sq[:, i * D : (i + 1) * D])
    for i in range(4):
        SM[3 + i : 4 + i, :] = total(su[:, i * D : (i + 1) * D])
    SM[7:8, :] = jnp.zeros((1, D), F32)
    for i in range(6):
        SM[8 + i : 9 + i, :] = total(sv[i])
    SM[14:16, :] = jnp.zeros((2, D), F32)
    small_core = pltpu.make_async_remote_copy(SM, SML.at[0], ssend.at[0], srecv.at[0], device_id=core_peer, device_id_type=MESH)
    small_core.start()

    def keep_rest(i, _):
        @pl.when(i < 2)
        def _():
            keep("up", 2 * i)
            keep("up", 2 * i + 1)

        @pl.when(i == 0)
        def _():
            give("qkv", 0)
            give("qkv", 1)

        @pl.when(i == 1)
        def _():
            give("qkv", 2)
            give("out", 0)

        @pl.when(i == 2)
        def _():
            keep("qkv", 0)
            keep("qkv", 1)

        @pl.when(i == 3)
        def _():
            keep("qkv", 2)
            keep("out", 0)

        slot(4 + i)
        return 0

    lax.fori_loop(0, 4, keep_rest, 0)
    small_core.wait()
    SM[...] += SML[0]
    if grid:
        ring.small_start(1)

    if grid:
        def last_slot(tau, _):
            slot(tau)
            return 0

        ring.small_finish(1)
        ring.small_start(2)
        lax.fori_loop(8, 10, last_slot, 0)
        ring.small_finish(2)
        ring.small_start(3)
        lax.fori_loop(10, BUCKETS + ring.stages - 1, last_slot, 0)
        ring.small_finish(3)
        ring.drain()
    else:
        result = pltpu.make_async_copy(G, gall, osem.at[4])
        result.start()
        result.wait()
    small_result = pltpu.make_async_copy(SM, gsm, osem.at[5])
    small_result.start()
    for kind, n in (("down", 4), ("up", 4), ("qkv", 3), ("out", 1)):
        for i in range(n):
            for copy in exchange(kind, i):
                copy.wait_send()
    small_result.wait()
    for copy in remote:
        copy.wait_send()
    for m in range(2):
        rows = ds(m * S, S)
        pltpu.make_async_copy(YB.at[rows], lo.at[rows], osem.at[m]).wait()
        pltpu.make_async_copy(IGF.at[rows], ig.at[rows], osem.at[2 + m]).wait()

    @pl.when(s == 0)
    def _():
        for m in range(2):
            relay(m, 0).wait_send()
            relay(m, 1).wait_send()

    @pl.when(s == 1)
    def _():
        for m in range(2):
            relay_back(m).wait_send()


def main_call(grid, S, tok, cot, seg, wq, qv, wo, wu, ub, wd, add, gain, shift):
    rows, D = tok.shape
    FF = 2 * wu.shape[1]
    hd, hq = D // 2, 3 * D // 2
    any_spec = pl.BlockSpec(memory_space=pl.ANY)
    vm_spec = pl.BlockSpec(memory_space=pltpu.VMEM)
    sds = jax.ShapeDtypeStruct
    V, DMA = pltpu.VMEM, pltpu.SemaphoreType.DMA
    line_a, line_b = MOST_A // 2 // LINE, MOST_B // LINE
    scratch = [
        V((D, 2 * hq), BF16), V((D, D), BF16), V((D, FF), BF16), V((FF, D), BF16), V((8, 2 * hq), F32), V((8, FF), F32),
        V((rows, D), BF16), V((rows, 3 * D), BF16), V((rows, D), BF16), V((rows, D), BF16), V((rows, D), BF16), V((rows, D), BF16),
        V((rows, FF), BF16), V((rows, FF), BF16), V((2 * (D // 128) * S, 2 * S), BF16),
        V((rows, D), BF16), V((rows, D), BF16), V((S, D), BF16), V((rows, 3 * D), BF16),
        V((rows, 128), F32), V((rows, 128), F32), V((S, D), F32), V((S, D), F32), V((2, S, S), F32),
        V((rows, D), BF16), V((rows, D), BF16), V((rows, D), BF16), V((rows, D), F32),
        V((8, 2 * hq), F32), V((8, FF), F32), V((6, 8, D), F32), V((16, D), F32), V((4, 16, D), F32),
        V((BUCKETS * D, hd), BF16), V((BUCKETS * MOST_A // 2, hd), BF16), V((BUCKETS * line_a * (LINE + 1), hd), BF16),
        V((BUCKETS * line_b * (LINE + 1), hd), BF16), V((BUCKETS * line_b, hd), BF16),
        DMA((8,)), DMA((8,)), DMA((8,)), DMA((4,)), DMA((4,)),
        DMA((BUCKETS, 2)), DMA((BUCKETS, 2)), DMA((6,)), DMA((4,)), DMA((4,)),
        DMA((BUCKETS, 8 * LINE + 3)), DMA((BUCKETS, 8 * LINE + 3)), DMA((BUCKETS, 2)),
    ]
    return pl.pallas_call(
        partial(main_kernel, D, FF, S, grid),
        out_shape=(sds((rows, D), BF16), sds((rows, D), F32), sds((BUCKETS * D, hd), BF16), sds((16, D), F32)),
        in_specs=[any_spec, any_spec, vm_spec, any_spec, vm_spec, any_spec, any_spec, vm_spec, any_spec, vm_spec, vm_spec, vm_spec],
        out_specs=(any_spec,) * 4,
        scratch_shapes=scratch,
        compiler_params=pltpu.CompilerParams(collective_id=0, has_side_effects=True, vmem_limit_bytes=60 * 2**20),
        name="layer_pass",
    )(tok, cot, seg, wq, qv, wo, wu, ub, wd, add, gain, shift)


def unpack_kernel(D, FF, gall, sums, lo, ig, gq, gqv, go, gu, gub, gd, ga, gg, gs, lo_out, ig_out, low, wide, lo_held, ig_held, in_sem, out_sem, pass_sem):
    c = lax.axis_index("tensor")
    W = D // 2
    reads = [pltpu.make_async_copy(gall.at[b * D : (b + 1) * D], low.at[b], in_sem.at[b]) for b in range(BUCKETS)]
    held = [pltpu.make_async_copy(src, dst, pass_sem.at[i]) for i, (src, dst) in enumerate(((lo, lo_held), (ig, ig_held)))]
    passed = [pltpu.make_async_copy(src, dst, pass_sem.at[2 + i]) for i, (src, dst) in enumerate(((lo_held, lo_out), (ig_held, ig_out)))]
    for copy in held + reads:
        copy.start()
    writes = []
    for b in range(BUCKETS):
        if b < 4 or b == 11:
            rows = wide.at[b]
            place = gd.at[b * W : (b + 1) * W, :] if b < 4 else go
            parts = [(rows.at[q * W : (q + 1) * W], place.at[:, q * W : (q + 1) * W]) for q in range(2)]
        elif b < 8:
            parts = [(wide.at[b], gu.at[:, (b - 4) * W : (b - 3) * W])]
        else:
            parts = [(wide.at[b], gq.at[b - 8])]
        writes.append([pltpu.make_async_copy(src, dst, out_sem.at[b, q]) for q, (src, dst) in enumerate(parts)])
    own = ds(c * W, W)
    gqv[0:1, :] = sums[pl.ds(c, 1), own]
    gqv[1:2, :] = sums[pl.ds(1 + c, 1), own]
    for i in range(2):
        gub[:, i * D : (i + 1) * D] = sums[pl.ds(3 + 2 * c + i, 1), :]
        ga[i : i + 1, :] = sums[8 + i : 9 + i, own]
        gg[i : i + 1, :] = sums[10 + i : 11 + i, own]
        gs[i : i + 1, :] = sums[12 + i : 13 + i, own]
    for read, write in zip(held, passed):
        read.wait()
        write.start()
    for b in range(BUCKETS):
        reads[b].wait()
        wide[b] = low[b].astype(F32)
        for copy in writes[b]:
            copy.start()
    for copies in writes + [passed]:
        for copy in copies:
            copy.wait()


def unpack_call(gall, gsm, lo, ig, D, FF):
    W, F = D // 2, FF // 2
    sds = jax.ShapeDtypeStruct
    any_spec = pl.BlockSpec(memory_space=pl.ANY)
    vm_spec = pl.BlockSpec(memory_space=pltpu.VMEM)
    return pl.pallas_call(
        partial(unpack_kernel, D, FF),
        in_specs=[any_spec, vm_spec, any_spec, any_spec],
        out_specs=(any_spec, vm_spec, any_spec, any_spec, vm_spec, any_spec, vm_spec, vm_spec, vm_spec, any_spec, any_spec),
        out_shape=(
            sds((3, D, W), F32), sds((2, W), F32), sds((W, D), F32), sds((D, F), F32), sds((1, F), F32),
            sds((F, D), F32), sds((2, W), F32), sds((2, W), F32), sds((2, W), F32), sds(lo.shape, lo.dtype), sds(ig.shape, ig.dtype),
        ),
        scratch_shapes=[
            pltpu.VMEM((BUCKETS, D, W), BF16), pltpu.VMEM((BUCKETS, D, W), F32), pltpu.VMEM(lo.shape, lo.dtype), pltpu.VMEM(ig.shape, ig.dtype),
            pltpu.SemaphoreType.DMA((BUCKETS,)), pltpu.SemaphoreType.DMA((BUCKETS, 2)), pltpu.SemaphoreType.DMA((4,)),
        ],
        compiler_params=pltpu.CompilerParams(vmem_limit_bytes=60 * 2**20),
        name="unpack",
    )(gall, gsm, lo, ig)


def shards(tokens, segment_ids, out_cotangent, w_qkv, qv_bias, w_out, w_up, up_bias, w_down, add_bias, norm_gain, norm_bias):
    D = tokens.shape[1]
    FF = 2 * w_up.shape[2]
    S = segment_ids.shape[1]
    grid = lax.axis_size("dp") == 2 * LINE
    lo, ig, gall, gsm = main_call(
        grid, S, tokens, out_cotangent, segment_ids, w_qkv[0].transpose(1, 0, 2), qv_bias[0],
        w_out[0], w_up[0], up_bias, w_down[0], add_bias[0], norm_gain[0], norm_bias[0],
    )
    if not grid:
        gall, gsm = lax.psum(gall, "dp"), lax.psum(gsm, "dp")
    gq, gqv, go, gu, gub, gd, ga, gg, gs, lo, ig = unpack_call(gall, gsm, lo, ig, D, FF)
    return (
        lo[None], ig[None], gq.transpose(1, 0, 2)[None], gqv[None], go[None], gu[None], gub, gd[None],
        ga[None], gg[None], gs[None],
    )


def solution(mesh):
    return jax.shard_map(
        shards,
        mesh=mesh,
        in_specs=(
            P(("dp", "tensor"), None), P("dp", None), P(("dp", "tensor"), None),
            P("section", None, None, "tensor"), P("section", None, "tensor"), P("section", "tensor", None),
            P("section", None, "tensor"), P("section", "tensor"), P("section", "tensor", None),
            P("section", None, None), P("section", None, None), P("section", None, None),
        ),
        out_specs=(
            P("section", ("dp", "tensor"), None), P("section", ("dp", "tensor"), None),
            P("section", None, None, "tensor"), P("section", None, "tensor"), P("section", "tensor", None),
            P("section", None, "tensor"), P("section", "tensor"), P("section", "tensor", None),
            P("section", None, "tensor"), P("section", None, "tensor"), P("section", None, "tensor"),
        ),
        check_vma=False,
    )
```

```python
from functools import partial

import jax
import jax.numpy as jnp
from jax import lax
from jax.experimental import pallas as pl
from jax.experimental.pallas import tpu as pltpu
from jax.sharding import PartitionSpec as P

HEAD_DIM = 64
norm_eps = 1e-12
masked_score = -1e30
LINE = 4
BUCKETS = 12
LENT, GUEST, GUEST_TURN = 4, 12, 8
A_ROWS = (512,)
MOST_A, MOST_B = 512, 256
MESH = pl.DeviceIdType.MESH
F32 = jnp.float32
BF16 = jnp.bfloat16


def mm(a, b):
    return lax.dot_general(a, b, (((1,), (0,)), ((), ())), preferred_element_type=F32)


def mm_nt(a, b):
    return lax.dot_general(a, b, (((1,), (1,)), ((), ())), preferred_element_type=F32)


def mm_tn(a, b):
    return lax.dot_general(a, b, (((0,), (0,)), ((), ())), preferred_element_type=F32)


def ds(start, size, align=None):
    return pl.ds(pl.multiple_of(start, align or size), size)


def eights(v):
    return jnp.sum(v.reshape(v.shape[0] // 8, 8, v.shape[1]), axis=0)


def gelu_and_slope(g):
    size = jnp.abs(g)
    x = 1.0 + 0.2316419 * size
    t = pl.reciprocal(x, approx=True)
    t = t * (2.0 - x * t)
    density = 0.3989422804014327 * jnp.exp2(g * g * -0.7213475204444817)
    tail = ((((1.330274429 * t - 1.821255978) * t + 1.781477937) * t - 0.356563782) * t + 0.319381530) * t * density
    cdf = jnp.where(g > 0.0, 1.0 - tail, tail)
    return g * cdf, cdf + g * density


def row_mean(v):
    return jnp.sum(v, axis=-1, keepdims=True) * (1.0 / v.shape[-1])


class Line:
    def __init__(self, red, base, size, most, landing, sems):
        self.red, self.base, self.size, self.most, self.landing, self.sems = red, base, size, most, landing, sems

    def own(self, b, j):
        return ds(self.base(b) + j * self.size, self.size, 16)

    def slot(self, b, j):
        return ds(b * (LINE + 1) * self.most + j * self.size, self.size, 16)

    def sum_up(self, b, j):
        r = self.red
        return r.remote(r.G.at[self.own(b, j)], self.landing.at[self.slot(b, j)], b, self.sems + j, r.above)

    def sum_down(self, b, j):
        r = self.red
        place = jnp.where(j == r.z - 1, LINE, j)
        return r.remote(r.G.at[self.own(b, j)], self.landing.at[self.slot(b, place)], b, self.sems + LINE + j, r.below)

    def from_above(self, b, j):
        r = self.red
        place = jnp.where(j == r.z, LINE, j)
        return r.remote(r.G.at[self.own(b, j)], self.landing.at[self.slot(b, place)], b, self.sems + LINE + j, r.below)

    def out_up(self, b, j, own=False):
        r = self.red
        return r.remote(r.place(own).at[self.own(b, j)], r.out.at[self.own(b, j)], b, self.sems + 2 * LINE + j, r.above)

    def out_down(self, b, j, own=False):
        r = self.red
        return r.remote(r.place(own).at[self.own(b, j)], r.out.at[self.own(b, j)], b, self.sems + 3 * LINE + j, r.below)

    def add(self, b, j, *places):
        G = self.red.G
        rows = self.own(b, j)
        total = G[rows, :].astype(F32)
        for place in places:
            total = total + self.landing[self.slot(b, place), :].astype(F32)
        G[rows, :] = total.astype(BF16)

    def begin(self, b):
        z = self.red.z

        @pl.when(z == 0)
        def _():
            for i in range(LINE - 1):
                self.sum_up(b, LINE - 1 - i).start()

        @pl.when(z == LINE - 1)
        def _():
            for i in range(LINE - 1):
                self.sum_down(b, i).start()

    def pass_on(self, b, i):
        z = self.red.z
        end = LINE - 1 - z
        up, down = LINE - 2 - i + z, 1 + i - end

        @pl.when((up > z) & (up < LINE) & (z > 0))
        def _():
            self.sum_up(b, up).wait_recv()
            self.add(b, up, up)
            self.sum_up(b, up).start()

        @pl.when((down < z) & (down >= 0) & (end > 0))
        def _():
            self.from_above(b, down).wait_recv()
            self.add(b, down, down)
            self.sum_down(b, down).start()

    def finish_own(self, b):
        z = self.red.z

        @pl.when(z > 0)
        def _():
            self.sum_up(b, z).wait_recv()

        @pl.when(z < LINE - 1)
        def _():
            self.from_above(b, z).wait_recv()

        @pl.when(z == 0)
        def _():
            self.add(b, 0, LINE)

        @pl.when(z == LINE - 1)
        def _():
            self.add(b, LINE - 1, LINE - 1)

        @pl.when((z > 0) & (z < LINE - 1))
        def _():
            self.add(b, z, z, LINE)

    def spread(self, b):
        z = self.red.z

        @pl.when(z < LINE - 1)
        def _():
            self.out_up(b, z, True).start()

        @pl.when(z > 0)
        def _():
            self.out_down(b, z, True).start()

        self.keep(b).start()

    def keep(self, b):
        r = self.red
        rows = self.own(b, r.z)
        return pltpu.make_async_copy(r.G.at[rows], r.out.at[rows], r.csem.at[b, self.sems // (4 * LINE)])

    def spread_on(self, b, i):
        z = self.red.z

        @pl.when(z - i >= 0)
        def _():
            self.out_up(b, z - i).wait_recv()

            @pl.when(z < LINE - 1)
            def _():
                self.out_up(b, z - i).start()

        @pl.when(z + i < LINE)
        def _():
            self.out_down(b, z + i).wait_recv()

            @pl.when(z > 0)
            def _():
                self.out_down(b, z + i).start()

    def drain(self, b):
        z = self.red.z
        for j in range(LINE):
            @pl.when(j > z)
            def _():
                self.sum_up(b, j).wait_send()

            @pl.when(j < z)
            def _():
                self.sum_down(b, j).wait_send()

            @pl.when((j <= z) & (z < LINE - 1))
            def _():
                self.out_up(b, j).wait_send()

            @pl.when((j >= z) & (z > 0))
            def _():
                self.out_down(b, j).wait_send()


class Reduction:
    stages = 9

    def __init__(self, D, s, d, c, G, out, LA1, LA, LB, LS, SM, SML, asend, arecv, ssend, srecv, csem, xsend, xrecv):
        self.out, self.csem, self.xsend, self.xrecv = out, csem, xsend, xrecv
        self.G, self.LA1, self.LS, self.SM, self.SML = G, LA1, LS, SM, SML
        self.asend, self.arecv, self.ssend, self.srecv = asend, arecv, ssend, srecv
        self.z, self.y = d // 2, d % 2
        self.s, self.d, self.c = s, d, c
        self.above = (s, jnp.minimum(d + 2, 2 * LINE - 1), c)
        self.below = (s, jnp.maximum(d - 2, 0), c)
        self.beside = (s, d + 1 - 2 * self.y, c)
        self.D = D
        self.kinds = []
        for a_rows in A_ROWS:
            half = a_rows // 2
            base = partial(lambda half, b: b * D + self.y * half, half)
            a = Line(self, base, half // LINE, MOST_A // 2 // LINE, LA, 0)
            base = partial(lambda a_rows, b: b * D + a_rows, a_rows)
            self.kinds.append((half, a, Line(self, base, (D - a_rows) // LINE, MOST_B // LINE, LB, 4 * LINE)))
        z = self.z
        pair = z + 1 - 2 * (z % 2)
        far = (z + 2) % 4
        self.small_peers = [None, self.beside, (s, pair * 2 + self.y, c), (s, far * 2 + self.y, c)]

    def place(self, own):
        return self.G if own else self.out

    def remote(self, src, dst, b, sem, to):
        return pltpu.make_async_remote_copy(src, dst, self.asend.at[b, sem], self.arecv.at[b, sem], device_id=to, device_id_type=MESH)

    def greet(self, barrier):
        def hello(to):
            pl.semaphore_signal(barrier, inc=1, device_id=to, device_id_type=MESH)
        for to in self.small_peers[1:]:
            hello(to)
        @pl.when((self.z == 1))
        def _():
            hello(self.above)

        @pl.when((self.z == 2))
        def _():
            hello(self.below)

    def greetings(self):
        return 3 + ((self.z == 1) | (self.z == 2)).astype(jnp.int32)

    def small_copy(self, k):
        return pltpu.make_async_remote_copy(self.SM, self.SML.at[k], self.ssend.at[k], self.srecv.at[k], device_id=self.small_peers[k], device_id_type=MESH)

    def small_start(self, k):
        self.small_copy(k).start()

    def small_finish(self, k):
        self.small_copy(k).wait()
        self.SM[...] += self.SML[k]

    def give_side(self, b, half):
        rows = ds(b * self.D + (1 - self.y) * half, half, 16)
        return self.remote(self.G.at[rows], self.LA1.at[ds(b * (MOST_A // 2), half, 16)], b, 8 * LINE, self.beside)

    def share_side(self, b, half):
        rows = ds(b * self.D + self.y * half, half, 16)
        return self.remote(self.out.at[rows], self.out.at[rows], b, 8 * LINE + 1, self.beside)

    def swap(self, b, B):
        return self.remote(self.G.at[B.own(b, self.z)], self.LS.at[ds(b * B.most, B.size, 16)], b, 8 * LINE + 2, self.beside)

    def stage(self, k, b, kind):
        half, A, B = kind
        if k == 0:
            self.give_side(b, half).start()
            B.begin(b)
        elif k == 1:
            B.pass_on(b, 0)
            self.give_side(b, half).wait_recv()
            rows = ds(b * self.D + self.y * half, half, 16)
            land = ds(b * (MOST_A // 2), half, 16)
            self.G[rows, :] = (self.G[rows, :].astype(F32) + self.LA1[land, :].astype(F32)).astype(BF16)
            A.begin(b)
        elif k == 2:
            B.pass_on(b, 1)
            A.pass_on(b, 0)
        elif k == 3:
            B.finish_own(b)
            self.swap(b, B).start()
            A.pass_on(b, 1)
        elif k == 4:
            A.finish_own(b)
            A.spread(b)
            self.swap(b, B).wait()
            rows, land = B.own(b, self.z), ds(b * B.most, B.size, 16)
            self.G[rows, :] = (self.G[rows, :].astype(F32) + self.LS[land, :].astype(F32)).astype(BF16)
            B.spread(b)
        elif k <= 7:
            A.spread_on(b, k - 4)
            B.spread_on(b, k - 4)
            if k == 7:
                A.keep(b).wait()
                self.share_side(b, half).start()
        else:
            self.share_side(b, half).wait_recv()

    def turns(self):
        return jnp.where(self.s == 0, BUCKETS - 1, BUCKETS + 1)

    def bucket(self, turn):
        lender = turn + jnp.where(turn >= LENT, 1, 0)
        keeper = jnp.where(turn == GUEST_TURN, GUEST, turn - jnp.where(turn > GUEST_TURN, 1, 0))
        return jnp.where(self.s == 0, lender, keeper)

    def lend(self):
        src, dst = self.G.at[LENT * self.D : (LENT + 1) * self.D], self.G.at[GUEST * self.D : (GUEST + 1) * self.D]
        return pltpu.make_async_remote_copy(src, dst, self.xsend.at[0], self.xrecv.at[0], device_id=(1 - self.s, self.d, self.c), device_id_type=MESH)

    def give_back(self):
        src, dst = self.out.at[GUEST * self.D : (GUEST + 1) * self.D], self.out.at[LENT * self.D : (LENT + 1) * self.D]
        return pltpu.make_async_remote_copy(src, dst, self.xsend.at[1], self.xrecv.at[1], device_id=(1 - self.s, self.d, self.c), device_id_type=MESH)

    def slot(self, tau):
        for k in (7, 0, 6, 4, 3, 5, 2, 1, 8):
            turn = tau - k
            b = self.bucket(turn)
            if k == 0:
                @pl.when((self.s == 1) & (turn == GUEST_TURN))
                def _():
                    self.lend().wait_recv()

            @pl.when((turn >= 0) & (turn < self.turns()))
            def _():
                self.stage(k, b, self.kinds[0])

    def guest_done(self):
        @pl.when(self.s == 1)
        def _():
            self.kinds[0][2].keep(GUEST).wait()
            self.give_back().start()

    def drain(self):
        half, A, B = self.kinds[0]

        def one(turn, _):
            b = self.bucket(turn)
            A.drain(b)
            B.drain(b)
            self.give_side(b, half).wait_send()
            self.share_side(b, half).wait_send()

            @pl.when(b != GUEST)
            def _():
                B.keep(b).wait()

            return 0

        lax.fori_loop(0, self.turns(), one, 0)

        @pl.when(self.s == 0)
        def _():
            self.lend().wait_send()
            self.give_back().wait_recv()

        @pl.when(self.s == 1)
        def _():
            self.give_back().wait_send()


def main_kernel(
    D, FF, S, grid,
    tok, cot, seg, wq_in, qv_in, wo_in, wu_in, ub_in, wd_in, add_in, gain, shift,
    lo, ig, gall, gsm,
    wq, wo, wu, wd, bq, bu,
    X, QKV, O, N1, N2, Hr, U, GP, R, dB, dA, dOs, dQKV,
    r1s, r2s, Hf, Zf, bias, dY, YB, IGB, IGF,
    sq, su, sv, SM, SML, G, LA1, LA, LB, LS,
    lsem, wsend, wrecv, rsend, rrecv, gsend, grecv, osem, ssend, srecv, asend, arecv, csem, xsend, xrecv,
):
    s = lax.axis_index("section")
    d = lax.axis_index("dp")
    c = lax.axis_index("tensor")
    other = 1 - c
    core_peer = (s, d, other)
    x_peer = (1 - s, d, c)
    half_d, half_f, half_q = D // 2, FF // 2, 3 * D // 2
    pairs = D // 128
    lo_pairs = pairs // 2

    barrier = pltpu.get_barrier_semaphore()
    pl.semaphore_signal(barrier, inc=1, device_id=core_peer, device_id_type=MESH)
    pl.semaphore_signal(barrier, inc=1, device_id=x_peer, device_id_type=MESH)
    if grid:
        ring = Reduction(D, s, d, c, G, gall, LA1, LA, LB, LS, SM, SML, asend, arecv, ssend, srecv, csem, xsend, xrecv)
        ring.greet(barrier)

    weights = [(wq_in.at[j], wq.at[:, ds(c * half_q + j * half_d, half_d)]) for j in range(3)] + [
        (wo_in, wo.at[ds(c * half_d, half_d), :]),
        (wu_in, wu.at[:, ds(c * half_f, half_f, 128)]),
        (wd_in, wd.at[ds(c * half_f, half_f), :]),
    ]
    biases = [bq.at[:, ds(c * half_q, half_q, 128)], bu.at[:, ds(c * half_f, half_f, 128)]]
    local = [pltpu.make_async_copy(src, dst, lsem.at[i]) for i, (src, dst) in enumerate(weights)]
    remote = [
        pltpu.make_async_remote_copy(src, dst, wsend.at[i], wrecv.at[i], device_id=core_peer, device_id_type=MESH)
        for i, (src, dst) in enumerate(weights + [(b, b) for b in biases])
    ]
    tok_copy = pltpu.make_async_copy(tok, X, lsem.at[6])
    cot_copy = pltpu.make_async_copy(cot, dY, lsem.at[7])

    @pl.when(s == 0)
    def _():
        tok_copy.start()

    @pl.when(s == 1)
    def _():
        cot_copy.start()

    for copy in local:
        copy.start()
    bq[:, ds(c * half_q, half_d)] = jnp.broadcast_to(qv_in[0:1, :].astype(F32), (8, half_d))
    bq[:, ds(c * half_q + half_d, half_d)] = jnp.zeros((8, half_d), F32)
    bq[:, ds(c * half_q + 2 * half_d, half_d)] = jnp.broadcast_to(qv_in[1:2, :].astype(F32), (8, half_d))
    bu[:, ds(c * half_f, half_f)] = jnp.broadcast_to(ub_in[...].astype(F32), (8, half_f))
    pl.semaphore_wait(barrier, 2 + ring.greetings() if grid else 2)
    for i in (0, 1, 2, 6, 7):
        remote[i].start()

    for q in range(2):
        row = jnp.broadcast_to(seg[pl.ds(2 * c + q, 1), :].astype(F32), (S, S))
        bias[q] = jnp.where(row.T == row, 0.0, masked_score)
    sq[...] = jnp.zeros_like(sq)
    su[...] = jnp.zeros_like(su)
    sv[...] = jnp.zeros_like(sv)
    lane = lax.broadcasted_iota(jnp.int32, (1, 128), 1)
    first_scaled = jnp.where(lane < HEAD_DIM, 0.125, 0.0).astype(BF16)
    second_scaled = jnp.where(lane < HEAD_DIM, 0.0, 0.125).astype(BF16)
    first_half = jnp.where(lane < HEAD_DIM, 1.0, 0.0).astype(BF16)
    second_half = jnp.where(lane < HEAD_DIM, 0.0, 1.0).astype(BF16)

    def need(*which):
        for i in which:
            if i < 6:
                local[i].wait()
            remote[i].wait_recv()

    def relay(m, part):
        rows = ds(m * S + part * (S // 2), S // 2)
        sem = 2 * m + part
        return pltpu.make_async_remote_copy(YB.at[rows], X.at[rows], rsend.at[sem], rrecv.at[sem], device_id=x_peer, device_id_type=MESH)

    def relay_back(m):
        rows = ds(m * S, S)
        return pltpu.make_async_remote_copy(IGB.at[rows], dY.at[rows], rsend.at[2 * m], rrecv.at[2 * m], device_id=x_peer, device_id_type=MESH)

    def pair_columns(p):
        base = (p // lo_pairs) * half_q + (p % lo_pairs) * 128
        return ds(base, 128), ds(base + half_d, 128), ds(base + 2 * half_d, 128)

    def normed(m, which, N, rs, finish, sent=None):
        def norm_rows(j, _):
            near, rows = ds(j * 32, 32), ds(m * S + j * 32, 32)
            z = Zf[near, :]
            centered = z - row_mean(z)
            scaled = lax.rsqrt(row_mean(centered * centered) + norm_eps)
            n = centered * scaled
            N[rows, :] = n.astype(BF16)
            rs[rows, :] = jnp.broadcast_to(scaled, (32, 128))
            finish(near, rows, n * gain[which : which + 1, :] + shift[which : which + 1, :])
            return 0

        for part in range(2):
            lax.fori_loop(part * S // 64, (part + 1) * S // 64, norm_rows, 0, unroll=True)
            if sent is not None:
                sent(part)

    def forward(t, m):
        rows = ds(m * S, S)

        @pl.when(t == 0)
        def _():
            @pl.when(s == 0)
            def _():
                tok_copy.wait()
            need(0, 1, 2, 6, 7)
            remote[3].start()
            remote[4].start()

        @pl.when(s == 1)
        def _():
            relay(m, 0).wait_recv()
            relay(m, 1).wait_recv()

        def qkv_tile(i, _):
            cols = ds(i * 256, 256)
            QKV[rows, cols] = (mm(X[rows, :], wq[:, cols]) + bq[0:1, cols]).astype(BF16)
            return 0

        lax.fori_loop(0, 3 * D // 256, qkv_tile, 0, unroll=True)

        def attend(p, _):
            qc, kc, vc = pair_columns(p)
            q2, k2, v2 = QKV[rows, qc], QKV[rows, kc], QKV[rows, vc]
            weights = ds((m * pairs + p) * S, S)
            outs = []
            for h, (mask, half) in enumerate(((first_scaled, first_half), (second_scaled, second_half))):
                kh = k2 * mask
                shares = []
                for part in range(0, S, 128):
                    st = mm_nt(kh, q2[part : part + 128, :]) + bias[m, :, part : part + 128]
                    e = jnp.exp(st - jnp.max(st, axis=0, keepdims=True))
                    share = (e * (1.0 / jnp.sum(e, axis=0, keepdims=True))).astype(BF16)
                    R[weights, h * S + part : h * S + part + 128] = share
                    shares.append(share)
                outs.append(mm_tn(jnp.concatenate(shares, axis=1), v2 * half))
            O[rows, ds(p * 128, 128)] = (outs[0] + outs[1]).astype(BF16)
            return 0

        lax.fori_loop(0, pairs, attend, 0, unroll=True)

        @pl.when(t == 0)
        def _():
            need(3)
            remote[5].start()

        def out_tile(i, _):
            cols = ds(i * 256, 256)
            Zf[:, cols] = mm(O[rows, :], wo[:, cols]) + X[rows, cols].astype(F32) + add_in[0:1, cols]
            return 0

        lax.fori_loop(0, D // 256, out_tile, 0, unroll=3)

        def first_done(near, rows, h):
            Hf[near, :] = h
            Hr[rows, :] = h.astype(BF16)

        normed(m, 0, N1, r1s, first_done)

        @pl.when(t == 0)
        def _():
            need(4)

        def up_tile(i, _):
            cols = ds(i * 256, 256)
            g = mm(Hr[rows, :], wu[:, cols])
            for j in range(0, S, 32):
                u, slope = gelu_and_slope(g[j : j + 32] + bu[0:1, cols])
                U[ds(m * S + j, 32), cols] = u.astype(BF16)
                GP[ds(m * S + j, 32), cols] = slope.astype(BF16)
            return 0

        lax.fori_loop(0, FF // 256, up_tile, 0, unroll=True)

        @pl.when(t == 0)
        def _():
            need(5)

        def down_tile(i, _):
            cols = ds(i * 256, 256)
            Zf[:, cols] = mm(U[rows, :], wd[:, cols]) + Hf[:, cols] + add_in[1:2, cols]
            return 0

        lax.fori_loop(0, D // 256, down_tile, 0, unroll=3)

        def second_done(near, rows, y):
            YB[rows, :] = y.astype(BF16)

        def send(part):
            @pl.when(s == 0)
            def _():
                relay(m, part).start()

        normed(m, 1, N2, r2s, second_done, send)
        pltpu.make_async_copy(YB.at[rows], lo.at[rows], osem.at[m]).start()

    def norm_back(m, which, get, N, rs, low):
        def back_rows(j, sums):
            near, rows = ds(j * 32, 32), ds(m * S + j * 32, 32)
            dy, n = get(near, rows), N[rows, :].astype(F32)
            e = dy * gain[which : which + 1, :]
            dz = rs[rows, 0:1] * (e - row_mean(e) - n * row_mean(e * n))
            Zf[near, :] = dz
            low[rows, :] = dz.astype(BF16)
            return sums[0] + eights(dz), sums[1] + eights(dy * n), sums[2] + eights(dy)

        sums = lax.fori_loop(0, S // 32, back_rows, (jnp.zeros((8, D), F32),) * 3, unroll=4)
        for i in range(3):
            sv[2 * i + which] += sums[i]

    def backward(t, m, last):
        rows = ds(m * S, S)

        @pl.when(s == 0)
        def _():
            relay_back(m).wait_recv()

        @pl.when((s == 1) & (m == 0))
        def _():
            cot_copy.wait()

        norm_back(m, 1, lambda near, rows: dY[rows, :].astype(F32), N2, r2s, dB)

        def down_back(i, _):
            cols = ds(i * 256, 256)
            dg = mm_nt(dB[rows, :], wd[cols, :]) * GP[rows, cols].astype(F32)
            su[:, cols] += eights(dg)
            GP[rows, cols] = dg.astype(BF16)
            return 0

        lax.fori_loop(0, FF // 256, down_back, 0, unroll=True)
        last(0)

        def up_back(i, _):
            cols = ds(i * 256, 256)
            Hf[:, cols] = mm_nt(GP[rows, :], wu[cols, :]) + Zf[:, cols]
            return 0

        lax.fori_loop(0, D // 256, up_back, 0, unroll=3)
        norm_back(m, 0, lambda near, rows: Hf[near, :], N1, r1s, dA)
        last(1)

        def out_back(i, _):
            cols = ds(i * 256, 256)
            dOs[:, cols] = mm_nt(dA[rows, :], wo[cols, :]).astype(BF16)
            return 0

        lax.fori_loop(0, D // 256, out_back, 0, unroll=3)
        last(2)

        def attend_back(p, _):
            qc, kc, vc = pair_columns(p)
            q2, k2, v2 = QKV[rows, qc], QKV[rows, kc], QKV[rows, vc]
            do2 = dOs[:, ds(p * 128, 128)]
            kt = k2.T
            weights = ds((m * pairs + p) * S, S)
            parts = []
            for h, half in enumerate((first_half, second_half)):
                vh = v2 * half
                for part in range(0, S, 128):
                    cols = slice(h * S + part, h * S + part + 128)
                    drt = mm_nt(vh, do2[part : part + 128, :])
                    rf = R[weights, cols].astype(F32)
                    parts.append((rf * (drt - jnp.sum(rf * drt, axis=0, keepdims=True))).astype(BF16))
            dst = jnp.concatenate(parts, axis=1)
            dk = mm(dst, jnp.concatenate([q2 * first_scaled, q2 * second_scaled], axis=0))
            dv = mm(R[weights, :], jnp.concatenate([do2 * first_half, do2 * second_half], axis=0))
            dqt = [mm(kt[h * HEAD_DIM : (h + 1) * HEAD_DIM], dst[:, h * S : (h + 1) * S]) for h in range(2)]
            dq = (jnp.concatenate(dqt, axis=0) * 0.125).T.astype(BF16)
            dvb = dv.astype(BF16)
            dQKV[rows, qc] = dq
            dQKV[rows, kc] = dk.astype(BF16)
            dQKV[rows, vc] = dvb
            sq[:, qc] += eights(dq.astype(F32))
            sq[:, vc] += eights(dvb.astype(F32))
            return 0

        lax.fori_loop(0, pairs, attend_back, 0, unroll=True)
        last(3)

        def in_back(i, _):
            cols = ds(i * 256, 256)
            dx = mm_nt(dQKV[rows, :], wq[cols, :]) + Zf[:, cols]
            IGF[rows, cols] = dx
            IGB[rows, cols] = dx.astype(BF16)
            return 0

        lax.fori_loop(0, D // 256, in_back, 0, unroll=3)
        pltpu.make_async_copy(IGF.at[rows], ig.at[rows], osem.at[2 + m]).start()

        @pl.when(s == 1)
        def _():
            relay_back(m).start()

    W = D // 2

    def across(i, start, size, right):
        return mm(R[ds(i * D + start, size, 128), :], right)

    def grad_tiles(k, kind, i):
        if kind == "down":
            left = U[:, ds(k * half_f + i * W, W, 128)].T
            return [mm(left, dB[:, q * W : (q + 1) * W]) for q in range(2)]
        if kind == "out":
            return [across(1, k * half_d, W, dA[:, q * W : (q + 1) * W]) for q in range(2)]
        cols = ds(k * (half_f if kind == "up" else half_q) + i * W, W, 128)
        which, right = (0, GP) if kind == "up" else (2, dQKV)
        return [across(which, q * W, W, right[:, cols]) for q in range(2)]

    first = {"down": 0, "up": 4, "qkv": 8, "out": 11}

    def halves(k, kind, i):
        if kind == "down":
            return [wd.at[ds(k * half_f + i * W, W), q * W : (q + 1) * W] for q in range(2)]
        if kind == "out":
            return [wo.at[ds(k * half_d, W), q * W : (q + 1) * W] for q in range(2)]
        cols = ds(k * (half_f if kind == "up" else half_q) + i * W, W, 128)
        ref = wu if kind == "up" else wq
        return [ref.at[q * W : (q + 1) * W, cols] for q in range(2)]

    def exchange(kind, i):
        b = first[kind] + i
        return [
            pltpu.make_async_remote_copy(part, G.at[ds(b * D + q * W, W)], gsend.at[b, q], grecv.at[b, q], device_id=core_peer, device_id_type=MESH)
            for q, part in enumerate(halves(other, kind, i))
        ]

    def give(kind, i):
        tiles = grad_tiles(other, kind, i)
        for q, copy in enumerate(exchange(kind, i)):
            halves(other, kind, i)[q][...] = tiles[q].astype(BF16)
            copy.start()

    def keep(kind, i):
        tiles = grad_tiles(c, kind, i)
        b = first[kind] + i
        for q, copy in enumerate(exchange(kind, i)):
            copy.wait_recv()
            rows = ds(b * D + q * W, W)
            G[rows, :] = (tiles[q] + G[rows, :].astype(F32)).astype(BF16)

    def slot(tau):
        if grid:
            ring.slot(tau)

    def give_all_down():
        def give_down(i, _):
            give("down", i)
            return 0

        lax.fori_loop(0, 4, give_down, 0)

    def step(t, _):
        back = jnp.where(s == 0, t // 2, t % 2)
        m = jnp.where(s == 0, t % 2, t // 2)

        def last(i):
            @pl.when((s == 0) & (m == 1))
            def _():
                if i == 0:
                    give_all_down()
                keep("down", i)
                slot(i)

        @pl.when(back == 0)
        def _():
            forward(t, m)

        @pl.when(back == 1)
        def _():
            backward(t, m, last)

        return 0

    lax.fori_loop(0, 4, step, 0)

    @pl.when(s == 1)
    def _():
        give_all_down()

        def keep_down(i, _):
            keep("down", i)
            slot(i)
            return 0

        lax.fori_loop(0, 4, keep_down, 0)

    for i, whole in enumerate((Hr, O, X)):
        R[i * D : (i + 1) * D, :] = whole[...].T

    def give_up(i, _):
        give("up", i)
        return 0

    lax.fori_loop(0, 4, give_up, 0)

    def total(v):
        return jnp.sum(v, axis=0, keepdims=True)

    for i in range(3):
        SM[i : i + 1, :] = total(sq[:, i * D : (i + 1) * D])
    for i in range(4):
        SM[3 + i : 4 + i, :] = total(su[:, i * D : (i + 1) * D])
    SM[7:8, :] = jnp.zeros((1, D), F32)
    for i in range(6):
        SM[8 + i : 9 + i, :] = total(sv[i])
    SM[14:16, :] = jnp.zeros((2, D), F32)
    small_core = pltpu.make_async_remote_copy(SM, SML.at[0], ssend.at[0], srecv.at[0], device_id=core_peer, device_id_type=MESH)
    small_core.start()

    def keep_rest(i, _):
        @pl.when(i < 2)
        def _():
            keep("up", 2 * i)
            keep("up", 2 * i + 1)

        if grid:
            @pl.when((i == 0) & (s == 0))
            def _():
                ring.lend().start()

        @pl.when(i == 0)
        def _():
            give("qkv", 0)
            give("qkv", 1)

        @pl.when(i == 1)
        def _():
            give("qkv", 2)
            give("out", 0)

        @pl.when(i == 2)
        def _():
            keep("qkv", 0)
            keep("qkv", 1)

        @pl.when(i == 3)
        def _():
            keep("qkv", 2)
            keep("out", 0)

        slot(4 + i)
        return 0

    lax.fori_loop(0, 4, keep_rest, 0)
    small_core.wait()
    SM[...] += SML[0]
    if grid:
        ring.small_start(1)

    if grid:
        def last_slot(tau, _):
            slot(tau)
            return 0

        ring.small_finish(1)
        ring.small_start(2)
        lax.fori_loop(8, 10, last_slot, 0)
        ring.small_finish(2)
        ring.small_start(3)
        lax.fori_loop(10, GUEST_TURN + ring.stages, last_slot, 0)
        ring.guest_done()
        lax.fori_loop(GUEST_TURN + ring.stages, ring.turns() + ring.stages - 1, last_slot, 0)
        ring.small_finish(3)
        ring.drain()
    else:
        result = pltpu.make_async_copy(G.at[0 : BUCKETS * D], gall.at[0 : BUCKETS * D], osem.at[4])
        result.start()
        result.wait()
    small_result = pltpu.make_async_copy(SM, gsm, osem.at[5])
    small_result.start()
    for kind, n in (("down", 4), ("up", 4), ("qkv", 3), ("out", 1)):
        for i in range(n):
            for copy in exchange(kind, i):
                copy.wait_send()
    small_result.wait()
    for copy in remote:
        copy.wait_send()
    for m in range(2):
        rows = ds(m * S, S)
        pltpu.make_async_copy(YB.at[rows], lo.at[rows], osem.at[m]).wait()
        pltpu.make_async_copy(IGF.at[rows], ig.at[rows], osem.at[2 + m]).wait()

    @pl.when(s == 0)
    def _():
        for m in range(2):
            relay(m, 0).wait_send()
            relay(m, 1).wait_send()

    @pl.when(s == 1)
    def _():
        for m in range(2):
            relay_back(m).wait_send()


def main_call(grid, S, tok, cot, seg, wq, qv, wo, wu, ub, wd, add, gain, shift):
    rows, D = tok.shape
    FF = 2 * wu.shape[1]
    hd, hq = D // 2, 3 * D // 2
    any_spec = pl.BlockSpec(memory_space=pl.ANY)
    vm_spec = pl.BlockSpec(memory_space=pltpu.VMEM)
    sds = jax.ShapeDtypeStruct
    V, DMA = pltpu.VMEM, pltpu.SemaphoreType.DMA
    slots = BUCKETS + 1
    line_a, line_b = MOST_A // 2 // LINE, MOST_B // LINE
    scratch = [
        V((D, 2 * hq), BF16), V((D, D), BF16), V((D, FF), BF16), V((FF, D), BF16), V((8, 2 * hq), F32), V((8, FF), F32),
        V((rows, D), BF16), V((rows, 3 * D), BF16), V((rows, D), BF16), V((rows, D), BF16), V((rows, D), BF16), V((rows, D), BF16),
        V((rows, FF), BF16), V((rows, FF), BF16), V((2 * (D // 128) * S, 2 * S), BF16),
        V((rows, D), BF16), V((rows, D), BF16), V((S, D), BF16), V((rows, 3 * D), BF16),
        V((rows, 128), F32), V((rows, 128), F32), V((S, D), F32), V((S, D), F32), V((2, S, S), F32),
        V((rows, D), BF16), V((rows, D), BF16), V((rows, D), BF16), V((rows, D), F32),
        V((8, 2 * hq), F32), V((8, FF), F32), V((6, 8, D), F32), V((16, D), F32), V((4, 16, D), F32),
        V((slots * D, hd), BF16), V((slots * MOST_A // 2, hd), BF16), V((slots * line_a * (LINE + 1), hd), BF16),
        V((slots * line_b * (LINE + 1), hd), BF16), V((slots * line_b, hd), BF16),
        DMA((8,)), DMA((8,)), DMA((8,)), DMA((4,)), DMA((4,)),
        DMA((BUCKETS, 2)), DMA((BUCKETS, 2)), DMA((6,)), DMA((4,)), DMA((4,)),
        DMA((slots, 8 * LINE + 3)), DMA((slots, 8 * LINE + 3)), DMA((slots, 2)), DMA((2,)), DMA((2,)),
    ]
    return pl.pallas_call(
        partial(main_kernel, D, FF, S, grid),
        out_shape=(sds((rows, D), BF16), sds((rows, D), F32), sds(((BUCKETS + 1) * D, hd), BF16), sds((16, D), F32)),
        in_specs=[any_spec, any_spec, vm_spec, any_spec, vm_spec, any_spec, any_spec, vm_spec, any_spec, vm_spec, vm_spec, vm_spec],
        out_specs=(any_spec,) * 4,
        scratch_shapes=scratch,
        compiler_params=pltpu.CompilerParams(collective_id=0, has_side_effects=True, vmem_limit_bytes=60 * 2**20),
        name="layer_pass",
    )(tok, cot, seg, wq, qv, wo, wu, ub, wd, add, gain, shift)


def unpack_kernel(D, FF, gall, sums, lo, ig, gq, gqv, go, gu, gub, gd, ga, gg, gs, lo_out, ig_out, low, wide, lo_held, ig_held, in_sem, out_sem, pass_sem):
    c = lax.axis_index("tensor")
    W = D // 2
    reads = [pltpu.make_async_copy(gall.at[b * D : (b + 1) * D], low.at[b], in_sem.at[b]) for b in range(BUCKETS)]
    held = [pltpu.make_async_copy(src, dst, pass_sem.at[i]) for i, (src, dst) in enumerate(((lo, lo_held), (ig, ig_held)))]
    passed = [pltpu.make_async_copy(src, dst, pass_sem.at[2 + i]) for i, (src, dst) in enumerate(((lo_held, lo_out), (ig_held, ig_out)))]
    for copy in held + reads:
        copy.start()
    writes = []
    for b in range(BUCKETS):
        if b < 4 or b == 11:
            rows = wide.at[b]
            place = gd.at[b * W : (b + 1) * W, :] if b < 4 else go
            parts = [(rows.at[q * W : (q + 1) * W], place.at[:, q * W : (q + 1) * W]) for q in range(2)]
        elif b < 8:
            parts = [(wide.at[b], gu.at[:, (b - 4) * W : (b - 3) * W])]
        else:
            parts = [(wide.at[b], gq.at[b - 8])]
        writes.append([pltpu.make_async_copy(src, dst, out_sem.at[b, q]) for q, (src, dst) in enumerate(parts)])
    own = ds(c * W, W)
    gqv[0:1, :] = sums[pl.ds(c, 1), own]
    gqv[1:2, :] = sums[pl.ds(1 + c, 1), own]
    for i in range(2):
        gub[:, i * D : (i + 1) * D] = sums[pl.ds(3 + 2 * c + i, 1), :]
        ga[i : i + 1, :] = sums[8 + i : 9 + i, own]
        gg[i : i + 1, :] = sums[10 + i : 11 + i, own]
        gs[i : i + 1, :] = sums[12 + i : 13 + i, own]
    for read, write in zip(held, passed):
        read.wait()
        write.start()
    for b in range(BUCKETS):
        reads[b].wait()
        wide[b] = low[b].astype(F32)
        for copy in writes[b]:
            copy.start()
    for copies in writes + [passed]:
        for copy in copies:
            copy.wait()


def unpack_call(gall, gsm, lo, ig, D, FF):
    W, F = D // 2, FF // 2
    sds = jax.ShapeDtypeStruct
    any_spec = pl.BlockSpec(memory_space=pl.ANY)
    vm_spec = pl.BlockSpec(memory_space=pltpu.VMEM)
    return pl.pallas_call(
        partial(unpack_kernel, D, FF),
        in_specs=[any_spec, vm_spec, any_spec, any_spec],
        out_specs=(any_spec, vm_spec, any_spec, any_spec, vm_spec, any_spec, vm_spec, vm_spec, vm_spec, any_spec, any_spec),
        out_shape=(
            sds((3, D, W), F32), sds((2, W), F32), sds((W, D), F32), sds((D, F), F32), sds((1, F), F32),
            sds((F, D), F32), sds((2, W), F32), sds((2, W), F32), sds((2, W), F32), sds(lo.shape, lo.dtype), sds(ig.shape, ig.dtype),
        ),
        scratch_shapes=[
            pltpu.VMEM((BUCKETS, D, W), BF16), pltpu.VMEM((BUCKETS, D, W), F32), pltpu.VMEM(lo.shape, lo.dtype), pltpu.VMEM(ig.shape, ig.dtype),
            pltpu.SemaphoreType.DMA((BUCKETS,)), pltpu.SemaphoreType.DMA((BUCKETS, 2)), pltpu.SemaphoreType.DMA((4,)),
        ],
        compiler_params=pltpu.CompilerParams(vmem_limit_bytes=60 * 2**20),
        name="unpack",
    )(gall, gsm, lo, ig)


def shards(tokens, segment_ids, out_cotangent, w_qkv, qv_bias, w_out, w_up, up_bias, w_down, add_bias, norm_gain, norm_bias):
    D = tokens.shape[1]
    FF = 2 * w_up.shape[2]
    S = segment_ids.shape[1]
    grid = lax.axis_size("dp") == 2 * LINE
    lo, ig, gall, gsm = main_call(
        grid, S, tokens, out_cotangent, segment_ids, w_qkv[0].transpose(1, 0, 2), qv_bias[0],
        w_out[0], w_up[0], up_bias, w_down[0], add_bias[0], norm_gain[0], norm_bias[0],
    )
    if not grid:
        gall, gsm = lax.psum(gall[: BUCKETS * D], "dp"), lax.psum(gsm, "dp")
    gq, gqv, go, gu, gub, gd, ga, gg, gs, lo, ig = unpack_call(gall, gsm, lo, ig, D, FF)
    return (
        lo[None], ig[None], gq.transpose(1, 0, 2)[None], gqv[None], go[None], gu[None], gub, gd[None],
        ga[None], gg[None], gs[None],
    )


def solution(mesh):
    return jax.shard_map(
        shards,
        mesh=mesh,
        in_specs=(
            P(("dp", "tensor"), None), P("dp", None), P(("dp", "tensor"), None),
            P("section", None, None, "tensor"), P("section", None, "tensor"), P("section", "tensor", None),
            P("section", None, "tensor"), P("section", "tensor"), P("section", "tensor", None),
            P("section", None, None), P("section", None, None), P("section", None, None),
        ),
        out_specs=(
            P("section", ("dp", "tensor"), None), P("section", ("dp", "tensor"), None),
            P("section", None, None, "tensor"), P("section", None, "tensor"), P("section", "tensor", None),
            P("section", None, "tensor"), P("section", "tensor"), P("section", "tensor", None),
            P("section", None, "tensor"), P("section", None, "tensor"), P("section", None, "tensor"),
        ),
        check_vma=False,
    )
```

```python
from functools import partial

import jax
import jax.numpy as jnp
from jax import lax
from jax.experimental import pallas as pl
from jax.experimental.pallas import tpu as pltpu
from jax.sharding import PartitionSpec as P

HEAD_DIM = 64
norm_eps = 1e-12
masked_score = -1e30
LINE = 4
BUCKETS = 12
LENT, GUEST, GUEST_TURN = 4, 12, 8
A_ROWS = (512,)
MOST_A, MOST_B = 512, 256
MESH = pl.DeviceIdType.MESH
F32 = jnp.float32
BF16 = jnp.bfloat16


def mm(a, b):
    return lax.dot_general(a, b, (((1,), (0,)), ((), ())), preferred_element_type=F32)


def mm_nt(a, b):
    return lax.dot_general(a, b, (((1,), (1,)), ((), ())), preferred_element_type=F32)


def mm_tn(a, b):
    return lax.dot_general(a, b, (((0,), (0,)), ((), ())), preferred_element_type=F32)


def ds(start, size, align=None):
    return pl.ds(pl.multiple_of(start, align or size), size)


def eights(v):
    return jnp.sum(v.reshape(v.shape[0] // 8, 8, v.shape[1]), axis=0)


def gelu_and_slope(g):
    size = jnp.abs(g)
    x = 1.0 + 0.2316419 * size
    t = pl.reciprocal(x, approx=True)
    t = t * (2.0 - x * t)
    density = 0.3989422804014327 * jnp.exp2(g * g * -0.7213475204444817)
    tail = ((((1.330274429 * t - 1.821255978) * t + 1.781477937) * t - 0.356563782) * t + 0.319381530) * t * density
    cdf = jnp.where(g > 0.0, 1.0 - tail, tail)
    return g * cdf, cdf + g * density


def row_mean(v):
    return jnp.sum(v, axis=-1, keepdims=True) * (1.0 / v.shape[-1])


class Line:
    def __init__(self, red, base, size, most, landing, sems):
        self.red, self.base, self.size, self.most, self.landing, self.sems = red, base, size, most, landing, sems

    def own(self, b, j):
        return ds(self.base(b) + j * self.size, self.size, 16)

    def slot(self, b, j):
        return ds(b * (LINE + 1) * self.most + j * self.size, self.size, 16)

    def sum_up(self, b, j):
        r = self.red
        return r.remote(r.G.at[self.own(b, j)], self.landing.at[self.slot(b, j)], b, self.sems + j, r.above)

    def sum_down(self, b, j):
        r = self.red
        place = jnp.where(j == r.z - 1, LINE, j)
        return r.remote(r.G.at[self.own(b, j)], self.landing.at[self.slot(b, place)], b, self.sems + LINE + j, r.below)

    def from_above(self, b, j):
        r = self.red
        place = jnp.where(j == r.z, LINE, j)
        return r.remote(r.G.at[self.own(b, j)], self.landing.at[self.slot(b, place)], b, self.sems + LINE + j, r.below)

    def out_up(self, b, j, own=False):
        r = self.red
        return r.remote(r.place(own).at[self.own(b, j)], r.out.at[self.own(b, j)], b, self.sems + 2 * LINE + j, r.above)

    def out_down(self, b, j, own=False):
        r = self.red
        return r.remote(r.place(own).at[self.own(b, j)], r.out.at[self.own(b, j)], b, self.sems + 3 * LINE + j, r.below)

    def add(self, b, j, *places):
        G = self.red.G
        rows = self.own(b, j)
        total = G[rows, :].astype(F32)
        for place in places:
            total = total + self.landing[self.slot(b, place), :].astype(F32)
        G[rows, :] = total.astype(BF16)

    def begin(self, b):
        z = self.red.z

        @pl.when(z == 0)
        def _():
            for i in range(LINE - 1):
                self.sum_up(b, LINE - 1 - i).start()

        @pl.when(z == LINE - 1)
        def _():
            for i in range(LINE - 1):
                self.sum_down(b, i).start()

    def pass_on(self, b, i):
        z = self.red.z
        end = LINE - 1 - z
        up, down = LINE - 2 - i + z, 1 + i - end

        @pl.when((up > z) & (up < LINE) & (z > 0))
        def _():
            self.sum_up(b, up).wait_recv()
            self.add(b, up, up)
            self.sum_up(b, up).start()

        @pl.when((down < z) & (down >= 0) & (end > 0))
        def _():
            self.from_above(b, down).wait_recv()
            self.add(b, down, down)
            self.sum_down(b, down).start()

    def finish_own(self, b):
        z = self.red.z

        @pl.when(z > 0)
        def _():
            self.sum_up(b, z).wait_recv()

        @pl.when(z < LINE - 1)
        def _():
            self.from_above(b, z).wait_recv()

        @pl.when(z == 0)
        def _():
            self.add(b, 0, LINE)

        @pl.when(z == LINE - 1)
        def _():
            self.add(b, LINE - 1, LINE - 1)

        @pl.when((z > 0) & (z < LINE - 1))
        def _():
            self.add(b, z, z, LINE)

    def spread(self, b):
        z = self.red.z

        @pl.when(z < LINE - 1)
        def _():
            self.out_up(b, z, True).start()

        @pl.when(z > 0)
        def _():
            self.out_down(b, z, True).start()

        self.keep(b).start()

    def keep(self, b):
        r = self.red
        rows = self.own(b, r.z)
        return pltpu.make_async_copy(r.G.at[rows], r.out.at[rows], r.csem.at[b, self.sems // (4 * LINE)])

    def spread_on(self, b, i):
        z = self.red.z

        @pl.when(z - i >= 0)
        def _():
            self.out_up(b, z - i).wait_recv()

            @pl.when(z < LINE - 1)
            def _():
                self.out_up(b, z - i).start()

        @pl.when(z + i < LINE)
        def _():
            self.out_down(b, z + i).wait_recv()

            @pl.when(z > 0)
            def _():
                self.out_down(b, z + i).start()

    def drain(self, b):
        z = self.red.z
        for j in range(LINE):
            @pl.when(j > z)
            def _():
                self.sum_up(b, j).wait_send()

            @pl.when(j < z)
            def _():
                self.sum_down(b, j).wait_send()

            @pl.when((j <= z) & (z < LINE - 1))
            def _():
                self.out_up(b, j).wait_send()

            @pl.when((j >= z) & (z > 0))
            def _():
                self.out_down(b, j).wait_send()


class Reduction:
    stages = 9

    def __init__(self, D, s, d, c, G, out, LA1, LA, LB, LS, SM, SML, asend, arecv, ssend, srecv, csem, xsend, xrecv):
        self.out, self.csem, self.xsend, self.xrecv = out, csem, xsend, xrecv
        self.G, self.LA1, self.LS, self.SM, self.SML = G, LA1, LS, SM, SML
        self.asend, self.arecv, self.ssend, self.srecv = asend, arecv, ssend, srecv
        self.z, self.y = d // 2, d % 2
        self.s, self.d, self.c = s, d, c
        self.above = (s, jnp.minimum(d + 2, 2 * LINE - 1), c)
        self.below = (s, jnp.maximum(d - 2, 0), c)
        self.beside = (s, d + 1 - 2 * self.y, c)
        self.D = D
        self.kinds = []
        for a_rows in A_ROWS:
            half = a_rows // 2
            base = partial(lambda half, b: b * D + self.y * half, half)
            a = Line(self, base, half // LINE, MOST_A // 2 // LINE, LA, 0)
            base = partial(lambda a_rows, b: b * D + a_rows, a_rows)
            self.kinds.append((half, a, Line(self, base, (D - a_rows) // LINE, MOST_B // LINE, LB, 4 * LINE)))
        z = self.z
        pair = z + 1 - 2 * (z % 2)
        far = (z + 2) % 4
        self.small_peers = [None, self.beside, (s, pair * 2 + self.y, c), (s, far * 2 + self.y, c)]

    def place(self, own):
        return self.G if own else self.out

    def remote(self, src, dst, b, sem, to):
        return pltpu.make_async_remote_copy(src, dst, self.asend.at[b, sem], self.arecv.at[b, sem], device_id=to, device_id_type=MESH)

    def greet(self, barrier):
        def hello(to):
            pl.semaphore_signal(barrier, inc=1, device_id=to, device_id_type=MESH)
        for to in self.small_peers[1:]:
            hello(to)
        @pl.when((self.z == 1))
        def _():
            hello(self.above)

        @pl.when((self.z == 2))
        def _():
            hello(self.below)

    def greetings(self):
        return 3 + ((self.z == 1) | (self.z == 2)).astype(jnp.int32)

    def small_copy(self, k):
        return pltpu.make_async_remote_copy(self.SM, self.SML.at[k], self.ssend.at[k], self.srecv.at[k], device_id=self.small_peers[k], device_id_type=MESH)

    def small_start(self, k):
        self.small_copy(k).start()

    def small_finish(self, k):
        self.small_copy(k).wait()
        self.SM[...] += self.SML[k]

    def give_side(self, b, half):
        rows = ds(b * self.D + (1 - self.y) * half, half, 16)
        return self.remote(self.G.at[rows], self.LA1.at[ds(b * (MOST_A // 2), half, 16)], b, 8 * LINE, self.beside)

    def share_side(self, b, half):
        rows = ds(b * self.D + self.y * half, half, 16)
        return self.remote(self.out.at[rows], self.out.at[rows], b, 8 * LINE + 1, self.beside)

    def swap(self, b, B):
        return self.remote(self.G.at[B.own(b, self.z)], self.LS.at[ds(b * B.most, B.size, 16)], b, 8 * LINE + 2, self.beside)

    def stage(self, k, b, kind):
        half, A, B = kind
        if k == 0:
            self.give_side(b, half).start()
            B.begin(b)
        elif k == 1:
            B.pass_on(b, 0)
            self.give_side(b, half).wait_recv()
            rows = ds(b * self.D + self.y * half, half, 16)
            land = ds(b * (MOST_A // 2), half, 16)
            self.G[rows, :] = (self.G[rows, :].astype(F32) + self.LA1[land, :].astype(F32)).astype(BF16)
            A.begin(b)
        elif k == 2:
            B.pass_on(b, 1)
            A.pass_on(b, 0)
        elif k == 3:
            B.finish_own(b)
            self.swap(b, B).start()
            A.pass_on(b, 1)
        elif k == 4:
            A.finish_own(b)
            A.spread(b)
            self.swap(b, B).wait()
            rows, land = B.own(b, self.z), ds(b * B.most, B.size, 16)
            self.G[rows, :] = (self.G[rows, :].astype(F32) + self.LS[land, :].astype(F32)).astype(BF16)
            B.spread(b)
        elif k <= 7:
            A.spread_on(b, k - 4)
            B.spread_on(b, k - 4)
            if k == 7:
                A.keep(b).wait()
                self.share_side(b, half).start()
        else:
            self.share_side(b, half).wait_recv()

    def turns(self):
        return jnp.where(self.s == 0, BUCKETS - 1, BUCKETS + 1)

    def bucket(self, turn):
        lender = turn + jnp.where(turn >= LENT, 1, 0)
        keeper = jnp.where(turn == GUEST_TURN, GUEST, turn - jnp.where(turn > GUEST_TURN, 1, 0))
        return jnp.where(self.s == 0, lender, keeper)

    def lend(self):
        src, dst = self.G.at[LENT * self.D : (LENT + 1) * self.D], self.G.at[GUEST * self.D : (GUEST + 1) * self.D]
        return pltpu.make_async_remote_copy(src, dst, self.xsend.at[0], self.xrecv.at[0], device_id=(1 - self.s, self.d, self.c), device_id_type=MESH)

    def give_back(self):
        src, dst = self.out.at[GUEST * self.D : (GUEST + 1) * self.D], self.out.at[LENT * self.D : (LENT + 1) * self.D]
        return pltpu.make_async_remote_copy(src, dst, self.xsend.at[1], self.xrecv.at[1], device_id=(1 - self.s, self.d, self.c), device_id_type=MESH)

    def slot(self, tau):
        for k in (7, 0, 6, 5, 4, 3, 2, 1, 8):
            turn = tau - k
            b = self.bucket(turn)
            if k == 0:
                @pl.when((self.s == 1) & (turn == GUEST_TURN))
                def _():
                    self.lend().wait_recv()

            @pl.when((turn >= 0) & (turn < self.turns()))
            def _():
                self.stage(k, b, self.kinds[0])

    def guest_done(self):
        @pl.when(self.s == 1)
        def _():
            self.kinds[0][2].keep(GUEST).wait()
            self.give_back().start()

    def drain(self):
        half, A, B = self.kinds[0]

        def one(turn, _):
            b = self.bucket(turn)
            A.drain(b)
            B.drain(b)
            self.give_side(b, half).wait_send()
            self.share_side(b, half).wait_send()

            @pl.when(b != GUEST)
            def _():
                B.keep(b).wait()

            return 0

        lax.fori_loop(0, self.turns(), one, 0)

        @pl.when(self.s == 0)
        def _():
            self.lend().wait_send()
            self.give_back().wait_recv()

        @pl.when(self.s == 1)
        def _():
            self.give_back().wait_send()


def main_kernel(
    D, FF, S, grid,
    tok, cot, seg, wq_in, qv_in, wo_in, wu_in, ub_in, wd_in, add_in, gain, shift,
    lo, ig, gall, gsm,
    wq, wo, wu, wd, bq, bu,
    X, QKV, O, N1, N2, Hr, U, GP, R, dB, dA, dOs, dQKV,
    r1s, r2s, Hf, Zf, bias, dY, YB, IGB, IGF,
    sq, su, sv, SM, SML, G, LA1, LA, LB, LS,
    lsem, wsend, wrecv, rsend, rrecv, gsend, grecv, osem, ssend, srecv, asend, arecv, csem, xsend, xrecv,
):
    s = lax.axis_index("section")
    d = lax.axis_index("dp")
    c = lax.axis_index("tensor")
    other = 1 - c
    core_peer = (s, d, other)
    x_peer = (1 - s, d, c)
    half_d, half_f, half_q = D // 2, FF // 2, 3 * D // 2
    pairs = D // 128
    lo_pairs = pairs // 2

    barrier = pltpu.get_barrier_semaphore()
    pl.semaphore_signal(barrier, inc=1, device_id=core_peer, device_id_type=MESH)
    pl.semaphore_signal(barrier, inc=1, device_id=x_peer, device_id_type=MESH)
    if grid:
        ring = Reduction(D, s, d, c, G, gall, LA1, LA, LB, LS, SM, SML, asend, arecv, ssend, srecv, csem, xsend, xrecv)
        ring.greet(barrier)

    weights = [(wq_in.at[j], wq.at[:, ds(c * half_q + j * half_d, half_d)]) for j in range(3)] + [
        (wo_in, wo.at[ds(c * half_d, half_d), :]),
        (wu_in, wu.at[:, ds(c * half_f, half_f, 128)]),
        (wd_in, wd.at[ds(c * half_f, half_f), :]),
    ]
    biases = [bq.at[:, ds(c * half_q, half_q, 128)], bu.at[:, ds(c * half_f, half_f, 128)]]
    local = [pltpu.make_async_copy(src, dst, lsem.at[i]) for i, (src, dst) in enumerate(weights)]
    remote = [
        pltpu.make_async_remote_copy(src, dst, wsend.at[i], wrecv.at[i], device_id=core_peer, device_id_type=MESH)
        for i, (src, dst) in enumerate(weights + [(b, b) for b in biases])
    ]
    tok_copy = pltpu.make_async_copy(tok, X, lsem.at[6])
    cot_copy = pltpu.make_async_copy(cot, dY, lsem.at[7])

    @pl.when(s == 0)
    def _():
        tok_copy.start()

    @pl.when(s == 1)
    def _():
        cot_copy.start()

    for copy in local:
        copy.start()
    bq[:, ds(c * half_q, half_d)] = jnp.broadcast_to(qv_in[0:1, :].astype(F32), (8, half_d))
    bq[:, ds(c * half_q + half_d, half_d)] = jnp.zeros((8, half_d), F32)
    bq[:, ds(c * half_q + 2 * half_d, half_d)] = jnp.broadcast_to(qv_in[1:2, :].astype(F32), (8, half_d))
    bu[:, ds(c * half_f, half_f)] = jnp.broadcast_to(ub_in[...].astype(F32), (8, half_f))
    pl.semaphore_wait(barrier, 2 + ring.greetings() if grid else 2)
    for i in (0, 1, 2, 6, 7):
        remote[i].start()

    for q in range(2):
        row = jnp.broadcast_to(seg[pl.ds(2 * c + q, 1), :].astype(F32), (S, S))
        bias[q] = jnp.where(row.T == row, 0.0, masked_score)
    sq[...] = jnp.zeros_like(sq)
    su[...] = jnp.zeros_like(su)
    sv[...] = jnp.zeros_like(sv)
    lane = lax.broadcasted_iota(jnp.int32, (1, 128), 1)
    first_scaled = jnp.where(lane < HEAD_DIM, 0.125, 0.0).astype(BF16)
    second_scaled = jnp.where(lane < HEAD_DIM, 0.0, 0.125).astype(BF16)
    first_half = jnp.where(lane < HEAD_DIM, 1.0, 0.0).astype(BF16)
    second_half = jnp.where(lane < HEAD_DIM, 0.0, 1.0).astype(BF16)

    def need(*which):
        for i in which:
            if i < 6:
                local[i].wait()
            remote[i].wait_recv()

    def relay(m, part):
        rows = ds(m * S + part * (S // 2), S // 2)
        sem = 2 * m + part
        return pltpu.make_async_remote_copy(YB.at[rows], X.at[rows], rsend.at[sem], rrecv.at[sem], device_id=x_peer, device_id_type=MESH)

    def relay_back(m):
        rows = ds(m * S, S)
        return pltpu.make_async_remote_copy(IGB.at[rows], dY.at[rows], rsend.at[2 * m], rrecv.at[2 * m], device_id=x_peer, device_id_type=MESH)

    def pair_columns(p):
        base = (p // lo_pairs) * half_q + (p % lo_pairs) * 128
        return ds(base, 128), ds(base + half_d, 128), ds(base + 2 * half_d, 128)

    def normed(m, which, N, rs, finish, sent=None):
        def norm_rows(j, _):
            near, rows = ds(j * 32, 32), ds(m * S + j * 32, 32)
            z = Zf[near, :]
            centered = z - row_mean(z)
            scaled = lax.rsqrt(row_mean(centered * centered) + norm_eps)
            n = centered * scaled
            N[rows, :] = n.astype(BF16)
            rs[rows, :] = jnp.broadcast_to(scaled, (32, 128))
            finish(near, rows, n * gain[which : which + 1, :] + shift[which : which + 1, :])
            return 0

        for part in range(2):
            lax.fori_loop(part * S // 64, (part + 1) * S // 64, norm_rows, 0, unroll=True)
            if sent is not None:
                sent(part)

    def forward(t, m):
        rows = ds(m * S, S)

        @pl.when(t == 0)
        def _():
            @pl.when(s == 0)
            def _():
                tok_copy.wait()
            need(0, 1, 2, 6, 7)
            remote[3].start()
            remote[4].start()

        @pl.when(s == 1)
        def _():
            relay(m, 0).wait_recv()
            relay(m, 1).wait_recv()

        def qkv_tile(i, _):
            cols = ds(i * 256, 256)
            QKV[rows, cols] = (mm(X[rows, :], wq[:, cols]) + bq[0:1, cols]).astype(BF16)
            return 0

        lax.fori_loop(0, 3 * D // 256, qkv_tile, 0, unroll=True)

        def attend(p, _):
            qc, kc, vc = pair_columns(p)
            q2, k2, v2 = QKV[rows, qc], QKV[rows, kc], QKV[rows, vc]
            weights = ds((m * pairs + p) * S, S)
            outs = []
            for h, (mask, half) in enumerate(((first_scaled, first_half), (second_scaled, second_half))):
                kh = k2 * mask
                shares = []
                for part in range(0, S, 128):
                    st = mm_nt(kh, q2[part : part + 128, :]) + bias[m, :, part : part + 128]
                    e = jnp.exp(st - jnp.max(st, axis=0, keepdims=True))
                    share = (e * (1.0 / jnp.sum(e, axis=0, keepdims=True))).astype(BF16)
                    R[weights, h * S + part : h * S + part + 128] = share
                    shares.append(share)
                outs.append(mm_tn(jnp.concatenate(shares, axis=1), v2 * half))
            O[rows, ds(p * 128, 128)] = (outs[0] + outs[1]).astype(BF16)
            return 0

        lax.fori_loop(0, pairs, attend, 0, unroll=True)

        @pl.when(t == 0)
        def _():
            need(3)
            remote[5].start()

        def out_tile(i, _):
            cols = ds(i * 256, 256)
            Zf[:, cols] = mm(O[rows, :], wo[:, cols]) + X[rows, cols].astype(F32) + add_in[0:1, cols]
            return 0

        lax.fori_loop(0, D // 256, out_tile, 0, unroll=3)

        def first_done(near, rows, h):
            Hf[near, :] = h
            Hr[rows, :] = h.astype(BF16)

        normed(m, 0, N1, r1s, first_done)

        @pl.when(t == 0)
        def _():
            need(4)

        def up_tile(i, _):
            cols = ds(i * 256, 256)
            g = mm(Hr[rows, :], wu[:, cols])
            for j in range(0, S, 32):
                u, slope = gelu_and_slope(g[j : j + 32] + bu[0:1, cols])
                U[ds(m * S + j, 32), cols] = u.astype(BF16)
                GP[ds(m * S + j, 32), cols] = slope.astype(BF16)
            return 0

        lax.fori_loop(0, FF // 256, up_tile, 0, unroll=True)

        @pl.when(t == 0)
        def _():
            need(5)

        def down_tile(i, _):
            cols = ds(i * 256, 256)
            Zf[:, cols] = mm(U[rows, :], wd[:, cols]) + Hf[:, cols] + add_in[1:2, cols]
            return 0

        lax.fori_loop(0, D // 256, down_tile, 0, unroll=3)

        def second_done(near, rows, y):
            YB[rows, :] = y.astype(BF16)

        def send(part):
            @pl.when(s == 0)
            def _():
                relay(m, part).start()

        normed(m, 1, N2, r2s, second_done, send)
        pltpu.make_async_copy(YB.at[rows], lo.at[rows], osem.at[m]).start()

    def norm_back(m, which, get, N, rs, low):
        def back_rows(j, sums):
            near, rows = ds(j * 32, 32), ds(m * S + j * 32, 32)
            dy, n = get(near, rows), N[rows, :].astype(F32)
            e = dy * gain[which : which + 1, :]
            dz = rs[rows, 0:1] * (e - row_mean(e) - n * row_mean(e * n))
            Zf[near, :] = dz
            low[rows, :] = dz.astype(BF16)
            return sums[0] + eights(dz), sums[1] + eights(dy * n), sums[2] + eights(dy)

        sums = lax.fori_loop(0, S // 32, back_rows, (jnp.zeros((8, D), F32),) * 3, unroll=4)
        for i in range(3):
            sv[2 * i + which] += sums[i]

    def backward(t, m, last):
        rows = ds(m * S, S)

        @pl.when(s == 0)
        def _():
            relay_back(m).wait_recv()

        @pl.when((s == 1) & (m == 0))
        def _():
            cot_copy.wait()

        norm_back(m, 1, lambda near, rows: dY[rows, :].astype(F32), N2, r2s, dB)

        def down_back(i, _):
            cols = ds(i * 256, 256)
            dg = mm_nt(dB[rows, :], wd[cols, :]) * GP[rows, cols].astype(F32)
            su[:, cols] += eights(dg)
            GP[rows, cols] = dg.astype(BF16)
            return 0

        lax.fori_loop(0, FF // 256, down_back, 0, unroll=True)
        last(0)

        def up_back(i, _):
            cols = ds(i * 256, 256)
            Hf[:, cols] = mm_nt(GP[rows, :], wu[cols, :]) + Zf[:, cols]
            return 0

        lax.fori_loop(0, D // 256, up_back, 0, unroll=3)
        norm_back(m, 0, lambda near, rows: Hf[near, :], N1, r1s, dA)
        last(1)

        def out_back(i, _):
            cols = ds(i * 256, 256)
            dOs[:, cols] = mm_nt(dA[rows, :], wo[cols, :]).astype(BF16)
            return 0

        lax.fori_loop(0, D // 256, out_back, 0, unroll=3)
        last(2)

        def attend_back(p, _):
            qc, kc, vc = pair_columns(p)
            q2, k2, v2 = QKV[rows, qc], QKV[rows, kc], QKV[rows, vc]
            do2 = dOs[:, ds(p * 128, 128)]
            kt = k2.T
            weights = ds((m * pairs + p) * S, S)
            parts = []
            for h, half in enumerate((first_half, second_half)):
                vh = v2 * half
                for part in range(0, S, 128):
                    cols = slice(h * S + part, h * S + part + 128)
                    drt = mm_nt(vh, do2[part : part + 128, :])
                    rf = R[weights, cols].astype(F32)
                    parts.append((rf * (drt - jnp.sum(rf * drt, axis=0, keepdims=True))).astype(BF16))
            dst = jnp.concatenate(parts, axis=1)
            dk = mm(dst, jnp.concatenate([q2 * first_scaled, q2 * second_scaled], axis=0))
            dv = mm(R[weights, :], jnp.concatenate([do2 * first_half, do2 * second_half], axis=0))
            dqt = [mm(kt[h * HEAD_DIM : (h + 1) * HEAD_DIM], dst[:, h * S : (h + 1) * S]) for h in range(2)]
            dq = (jnp.concatenate(dqt, axis=0) * 0.125).T.astype(BF16)
            dvb = dv.astype(BF16)
            dQKV[rows, qc] = dq
            dQKV[rows, kc] = dk.astype(BF16)
            dQKV[rows, vc] = dvb
            sq[:, qc] += eights(dq.astype(F32))
            sq[:, vc] += eights(dvb.astype(F32))
            return 0

        lax.fori_loop(0, pairs, attend_back, 0, unroll=True)
        last(3)

        def in_back(i, _):
            cols = ds(i * 256, 256)
            dx = mm_nt(dQKV[rows, :], wq[cols, :]) + Zf[:, cols]
            IGF[rows, cols] = dx
            IGB[rows, cols] = dx.astype(BF16)
            return 0

        lax.fori_loop(0, D // 256, in_back, 0, unroll=3)
        pltpu.make_async_copy(IGF.at[rows], ig.at[rows], osem.at[2 + m]).start()

        @pl.when(s == 1)
        def _():
            relay_back(m).start()

    W = D // 2

    def across(i, start, size, right):
        return mm(R[ds(i * D + start, size, 128), :], right)

    def grad_tiles(k, kind, i):
        if kind == "down":
            left = U[:, ds(k * half_f + i * W, W, 128)]
            whole = mm_tn(left, dB[...])
            return [whole[:, q * W : (q + 1) * W] for q in range(2)]
        if kind == "out":
            return [across(1, k * half_d, W, dA[:, q * W : (q + 1) * W]) for q in range(2)]
        cols = ds(k * (half_f if kind == "up" else half_q) + i * W, W, 128)
        which, right = (0, GP) if kind == "up" else (2, dQKV)
        return [across(which, q * W, W, right[:, cols]) for q in range(2)]

    first = {"down": 0, "up": 4, "qkv": 8, "out": 11}

    def halves(k, kind, i):
        if kind == "down":
            return [wd.at[ds(k * half_f + i * W, W), q * W : (q + 1) * W] for q in range(2)]
        if kind == "out":
            return [wo.at[ds(k * half_d, W), q * W : (q + 1) * W] for q in range(2)]
        cols = ds(k * (half_f if kind == "up" else half_q) + i * W, W, 128)
        ref = wu if kind == "up" else wq
        return [ref.at[q * W : (q + 1) * W, cols] for q in range(2)]

    def exchange(kind, i):
        b = first[kind] + i
        return [
            pltpu.make_async_remote_copy(part, G.at[ds(b * D + q * W, W)], gsend.at[b, q], grecv.at[b, q], device_id=core_peer, device_id_type=MESH)
            for q, part in enumerate(halves(other, kind, i))
        ]

    def give(kind, i):
        tiles = grad_tiles(other, kind, i)
        for q, copy in enumerate(exchange(kind, i)):
            halves(other, kind, i)[q][...] = tiles[q].astype(BF16)
            copy.start()

    def keep(kind, i):
        tiles = grad_tiles(c, kind, i)
        b = first[kind] + i
        for q, copy in enumerate(exchange(kind, i)):
            copy.wait_recv()
            rows = ds(b * D + q * W, W)
            G[rows, :] = (tiles[q] + G[rows, :].astype(F32)).astype(BF16)

    def slot(tau):
        if grid:
            ring.slot(tau)

    def give_all_down():
        def give_down(i, _):
            give("down", i)
            return 0

        lax.fori_loop(0, 4, give_down, 0)

    def step(t, _):
        back = jnp.where(s == 0, t // 2, t % 2)
        m = jnp.where(s == 0, t % 2, t // 2)

        def last(i):
            @pl.when((s == 0) & (m == 1))
            def _():
                if i == 0:
                    give_all_down()
                keep("down", i)
                slot(i)

        @pl.when(back == 0)
        def _():
            forward(t, m)

        @pl.when(back == 1)
        def _():
            backward(t, m, last)

        return 0

    lax.fori_loop(0, 4, step, 0)

    @pl.when(s == 1)
    def _():
        give_all_down()

        def keep_down(i, _):
            keep("down", i)
            slot(i)
            return 0

        lax.fori_loop(0, 4, keep_down, 0)

    for i, whole in enumerate((Hr, O, X)):
        R[i * D : (i + 1) * D, :] = whole[...].T

    def give_up(i, _):
        give("up", i)
        return 0

    lax.fori_loop(0, 4, give_up, 0)

    def total(v):
        return jnp.sum(v, axis=0, keepdims=True)

    for i in range(3):
        SM[i : i + 1, :] = total(sq[:, i * D : (i + 1) * D])
    for i in range(4):
        SM[3 + i : 4 + i, :] = total(su[:, i * D : (i + 1) * D])
    SM[7:8, :] = jnp.zeros((1, D), F32)
    for i in range(6):
        SM[8 + i : 9 + i, :] = total(sv[i])
    SM[14:16, :] = jnp.zeros((2, D), F32)
    small_core = pltpu.make_async_remote_copy(SM, SML.at[0], ssend.at[0], srecv.at[0], device_id=core_peer, device_id_type=MESH)
    small_core.start()

    def keep_rest(i, _):
        @pl.when(i < 2)
        def _():
            keep("up", 2 * i)
            keep("up", 2 * i + 1)

        if grid:
            @pl.when((i == 0) & (s == 0))
            def _():
                ring.lend().start()

        @pl.when(i == 0)
        def _():
            give("qkv", 0)
            give("qkv", 1)

        @pl.when(i == 1)
        def _():
            give("qkv", 2)
            give("out", 0)

        @pl.when(i == 2)
        def _():
            keep("qkv", 0)
            keep("qkv", 1)

        @pl.when(i == 3)
        def _():
            keep("qkv", 2)
            keep("out", 0)

        slot(4 + i)
        return 0

    lax.fori_loop(0, 4, keep_rest, 0)
    small_core.wait()
    SM[...] += SML[0]
    if grid:
        ring.small_start(1)

    if grid:
        def last_slot(tau, _):
            slot(tau)
            return 0

        ring.small_finish(1)
        ring.small_start(2)
        lax.fori_loop(8, 10, last_slot, 0)
        ring.small_finish(2)
        ring.small_start(3)
        lax.fori_loop(10, GUEST_TURN + ring.stages, last_slot, 0)
        ring.guest_done()
        lax.fori_loop(GUEST_TURN + ring.stages, ring.turns() + ring.stages - 1, last_slot, 0)
        ring.small_finish(3)
        ring.drain()
    else:
        result = pltpu.make_async_copy(G.at[0 : BUCKETS * D], gall.at[0 : BUCKETS * D], osem.at[4])
        result.start()
        result.wait()
    small_result = pltpu.make_async_copy(SM, gsm, osem.at[5])
    small_result.start()
    for kind, n in (("down", 4), ("up", 4), ("qkv", 3), ("out", 1)):
        for i in range(n):
            for copy in exchange(kind, i):
                copy.wait_send()
    small_result.wait()
    for copy in remote:
        copy.wait_send()
    for m in range(2):
        rows = ds(m * S, S)
        pltpu.make_async_copy(YB.at[rows], lo.at[rows], osem.at[m]).wait()
        pltpu.make_async_copy(IGF.at[rows], ig.at[rows], osem.at[2 + m]).wait()

    @pl.when(s == 0)
    def _():
        for m in range(2):
            relay(m, 0).wait_send()
            relay(m, 1).wait_send()

    @pl.when(s == 1)
    def _():
        for m in range(2):
            relay_back(m).wait_send()


def main_call(grid, S, tok, cot, seg, wq, qv, wo, wu, ub, wd, add, gain, shift):
    rows, D = tok.shape
    FF = 2 * wu.shape[1]
    hd, hq = D // 2, 3 * D // 2
    any_spec = pl.BlockSpec(memory_space=pl.ANY)
    vm_spec = pl.BlockSpec(memory_space=pltpu.VMEM)
    sds = jax.ShapeDtypeStruct
    V, DMA = pltpu.VMEM, pltpu.SemaphoreType.DMA
    slots = BUCKETS + 1
    line_a, line_b = MOST_A // 2 // LINE, MOST_B // LINE
    scratch = [
        V((D, 2 * hq), BF16), V((D, D), BF16), V((D, FF), BF16), V((FF, D), BF16), V((8, 2 * hq), F32), V((8, FF), F32),
        V((rows, D), BF16), V((rows, 3 * D), BF16), V((rows, D), BF16), V((rows, D), BF16), V((rows, D), BF16), V((rows, D), BF16),
        V((rows, FF), BF16), V((rows, FF), BF16), V((2 * (D // 128) * S, 2 * S), BF16),
        V((rows, D), BF16), V((rows, D), BF16), V((S, D), BF16), V((rows, 3 * D), BF16),
        V((rows, 128), F32), V((rows, 128), F32), V((S, D), F32), V((S, D), F32), V((2, S, S), F32),
        V((rows, D), BF16), V((rows, D), BF16), V((rows, D), BF16), V((rows, D), F32),
        V((8, 2 * hq), F32), V((8, FF), F32), V((6, 8, D), F32), V((16, D), F32), V((4, 16, D), F32),
        V((slots * D, hd), BF16), V((slots * MOST_A // 2, hd), BF16), V((slots * line_a * (LINE + 1), hd), BF16),
        V((slots * line_b * (LINE + 1), hd), BF16), V((slots * line_b, hd), BF16),
        DMA((8,)), DMA((8,)), DMA((8,)), DMA((4,)), DMA((4,)),
        DMA((BUCKETS, 2)), DMA((BUCKETS, 2)), DMA((6,)), DMA((4,)), DMA((4,)),
        DMA((slots, 8 * LINE + 3)), DMA((slots, 8 * LINE + 3)), DMA((slots, 2)), DMA((2,)), DMA((2,)),
    ]
    return pl.pallas_call(
        partial(main_kernel, D, FF, S, grid),
        out_shape=(sds((rows, D), BF16), sds((rows, D), F32), sds(((BUCKETS + 1) * D, hd), BF16), sds((16, D), F32)),
        in_specs=[any_spec, any_spec, vm_spec, any_spec, vm_spec, any_spec, any_spec, vm_spec, any_spec, vm_spec, vm_spec, vm_spec],
        out_specs=(any_spec,) * 4,
        scratch_shapes=scratch,
        compiler_params=pltpu.CompilerParams(collective_id=0, has_side_effects=True, vmem_limit_bytes=60 * 2**20),
        name="layer_pass",
    )(tok, cot, seg, wq, qv, wo, wu, ub, wd, add, gain, shift)


def unpack_kernel(D, FF, gall, sums, lo, ig, gq, gqv, go, gu, gub, gd, ga, gg, gs, lo_out, ig_out, low, wide, lo_held, ig_held, in_sem, out_sem, pass_sem):
    c = lax.axis_index("tensor")
    W = D // 2
    reads = [pltpu.make_async_copy(gall.at[b * D : (b + 1) * D], low.at[b], in_sem.at[b]) for b in range(BUCKETS)]
    held = [pltpu.make_async_copy(src, dst, pass_sem.at[i]) for i, (src, dst) in enumerate(((lo, lo_held), (ig, ig_held)))]
    passed = [pltpu.make_async_copy(src, dst, pass_sem.at[2 + i]) for i, (src, dst) in enumerate(((lo_held, lo_out), (ig_held, ig_out)))]
    for copy in held + reads:
        copy.start()
    writes = []
    for b in range(BUCKETS):
        if b < 4 or b == 11:
            rows = wide.at[b]
            place = gd.at[b * W : (b + 1) * W, :] if b < 4 else go
            parts = [(rows.at[q * W : (q + 1) * W], place.at[:, q * W : (q + 1) * W]) for q in range(2)]
        elif b < 8:
            parts = [(wide.at[b], gu.at[:, (b - 4) * W : (b - 3) * W])]
        else:
            parts = [(wide.at[b], gq.at[b - 8])]
        writes.append([pltpu.make_async_copy(src, dst, out_sem.at[b, q]) for q, (src, dst) in enumerate(parts)])
    own = ds(c * W, W)
    gqv[0:1, :] = sums[pl.ds(c, 1), own]
    gqv[1:2, :] = sums[pl.ds(1 + c, 1), own]
    for i in range(2):
        gub[:, i * D : (i + 1) * D] = sums[pl.ds(3 + 2 * c + i, 1), :]
        ga[i : i + 1, :] = sums[8 + i : 9 + i, own]
        gg[i : i + 1, :] = sums[10 + i : 11 + i, own]
        gs[i : i + 1, :] = sums[12 + i : 13 + i, own]
    for read, write in zip(held, passed):
        read.wait()
        write.start()
    for b in range(BUCKETS):
        reads[b].wait()
        wide[b] = low[b].astype(F32)
        for copy in writes[b]:
            copy.start()
    for copies in writes + [passed]:
        for copy in copies:
            copy.wait()


def unpack_call(gall, gsm, lo, ig, D, FF):
    W, F = D // 2, FF // 2
    sds = jax.ShapeDtypeStruct
    any_spec = pl.BlockSpec(memory_space=pl.ANY)
    vm_spec = pl.BlockSpec(memory_space=pltpu.VMEM)
    return pl.pallas_call(
        partial(unpack_kernel, D, FF),
        in_specs=[any_spec, vm_spec, any_spec, any_spec],
        out_specs=(any_spec, vm_spec, any_spec, any_spec, vm_spec, any_spec, vm_spec, vm_spec, vm_spec, any_spec, any_spec),
        out_shape=(
            sds((3, D, W), F32), sds((2, W), F32), sds((W, D), F32), sds((D, F), F32), sds((1, F), F32),
            sds((F, D), F32), sds((2, W), F32), sds((2, W), F32), sds((2, W), F32), sds(lo.shape, lo.dtype), sds(ig.shape, ig.dtype),
        ),
        scratch_shapes=[
            pltpu.VMEM((BUCKETS, D, W), BF16), pltpu.VMEM((BUCKETS, D, W), F32), pltpu.VMEM(lo.shape, lo.dtype), pltpu.VMEM(ig.shape, ig.dtype),
            pltpu.SemaphoreType.DMA((BUCKETS,)), pltpu.SemaphoreType.DMA((BUCKETS, 2)), pltpu.SemaphoreType.DMA((4,)),
        ],
        compiler_params=pltpu.CompilerParams(vmem_limit_bytes=60 * 2**20),
        name="unpack",
    )(gall, gsm, lo, ig)


def shards(tokens, segment_ids, out_cotangent, w_qkv, qv_bias, w_out, w_up, up_bias, w_down, add_bias, norm_gain, norm_bias):
    D = tokens.shape[1]
    FF = 2 * w_up.shape[2]
    S = segment_ids.shape[1]
    grid = lax.axis_size("dp") == 2 * LINE
    lo, ig, gall, gsm = main_call(
        grid, S, tokens, out_cotangent, segment_ids, w_qkv[0].transpose(1, 0, 2), qv_bias[0],
        w_out[0], w_up[0], up_bias, w_down[0], add_bias[0], norm_gain[0], norm_bias[0],
    )
    if not grid:
        gall, gsm = lax.psum(gall[: BUCKETS * D], "dp"), lax.psum(gsm, "dp")
    gq, gqv, go, gu, gub, gd, ga, gg, gs, lo, ig = unpack_call(gall, gsm, lo, ig, D, FF)
    return (
        lo[None], ig[None], gq.transpose(1, 0, 2)[None], gqv[None], go[None], gu[None], gub, gd[None],
        ga[None], gg[None], gs[None],
    )


def solution(mesh):
    return jax.shard_map(
        shards,
        mesh=mesh,
        in_specs=(
            P(("dp", "tensor"), None), P("dp", None), P(("dp", "tensor"), None),
            P("section", None, None, "tensor"), P("section", None, "tensor"), P("section", "tensor", None),
            P("section", None, "tensor"), P("section", "tensor"), P("section", "tensor", None),
            P("section", None, None), P("section", None, None), P("section", None, None),
        ),
        out_specs=(
            P("section", ("dp", "tensor"), None), P("section", ("dp", "tensor"), None),
            P("section", None, None, "tensor"), P("section", None, "tensor"), P("section", "tensor", None),
            P("section", None, "tensor"), P("section", "tensor"), P("section", "tensor", None),
            P("section", None, "tensor"), P("section", None, "tensor"), P("section", None, "tensor"),
        ),
        check_vma=False,
    )
```
